32 devices in a mesh: req: 8 (over y, x, core), head: 4 (over z).
Axes of the slice: x: 2, y: 2, z: 4, core: 2. Of those that a mesh axis runs over, the one named last changes fastest.
Arguments:
- streams: bfloat16 [6144, 4, 2048], P('req', None, 'head'), may hold values from -6 to 6
- hc_in: float32 [2, 4], replicated, may hold values from 0.2 to 1
- hc_mix: float32 [2, 4, 4], replicated, may hold values from -0.4 to 0.4
- hc_out: float32 [2, 4], replicated, may hold values from 0.5 to 1.5
- qkv_weight: bfloat16 [2048, 3, 2048], P(None, None, 'head'), may hold values from -0.125 to 0.125
- out_weight: bfloat16 [2048, 2048], P('head'), may hold values from -0.125 to 0.125
- up_gate: bfloat16 [2048, 2, 8192], P(None, None, 'head'), may hold values from -0.125 to 0.125
- down_weight: bfloat16 [8192, 2048], P('head'), may hold values from -0.0625 to 0.0625
- draft_weight: bfloat16 [2, 2048, 2048], P(None, None, 'head'), may hold values from -0.125 to 0.125
- lm_head: bfloat16 [2048, 50304], P(None, ('req', 'head')), may hold values from -0.125 to 0.125
- k_pages: bfloat16 [384, 128, 16, 128], P('req', None, 'head'), may hold values from -45 to 45
- v_pages: bfloat16 [384, 128, 16, 128], P('req', None, 'head'), may hold values from -6 to 6
- page_owner: int32 [384], P('req'), may hold values from -1 to 127, as said below
- page_fill: int32 [384], P('req'), may hold values from 0 to 128, as said below
- cache_len: int32 [128], P('req'), may hold values from 1 to 16384, as said below
- tree_parent: int32 [128, 48], P('req'), may hold values from 0 to 46, as said below
- accepted_index: int32 [128], P('req'), may hold values from 0 to 47
Outputs:
- new_streams: bfloat16 [6144, 4, 2048], P('req', None, 'head')
- logits: float32 [128, 2, 50304], P(('req', 'head'))
The draws below stay inside these ranges and needn't reach their ends.
Inputs may be any that keep to these rules, and one draw needn't show every extreme that they name: `page_owner`: each page slot holds one page of the request it names, or -1 where it is empty. Every request owns at least one page and one request owns 128 pages; the live pages of a device's slots vary widely from device to device. `page_fill`: 0 for an empty slot; every page of a request is full except at most one. `cache_len`: equals the valid entries of the pages the request owns; one request has exactly 16384. `tree_parent`: entry i names a smaller position, the parent of position i; position 0 is the root and names itself.
All inputs are finite; a program needn't handle non-finite values.
Results may differ from the reference program's by a relative error of at most 0.027.
Values may be sent and summed in bfloat16 or wider, within the bound.
No kernel may reach another device: no remote copies, remote signals or barrier semaphores. Data moves between devices by JAX's collectives and lax.ppermute only.
A program may use at most 512 MiB of HBM per device.

```python
import math
import jax
import jax.numpy as jnp
from jax import lax

D = 2048
HEADS = 16
HD = 128
FF = 8192
VOCAB = 50304
NS = 4
TREE = 48
PAGE = 128
LONG_PAGES = 128
NDRAFT = 2
LEAVES_EACH_PART = 48
REQUESTS = 128
TOKENS = 6144
LEAF_PLACES_SUM = 384


def page_layout(key):
    sampler_seeds = jax.random.split(jax.random.fold_in(key, 5), 6)
    order_req = jnp.arange(REQUESTS, dtype=jnp.int32)
    power = jax.random.randint(sampler_seeds[0], (REQUESTS,), 0, 6)
    extra = jax.random.randint(sampler_seeds[1], (REQUESTS,), 0, jnp.left_shift(1, power))
    extra = jnp.minimum(extra, LONG_PAGES - 2)
    longest = jax.random.randint(sampler_seeds[2], (), 0, REQUESTS)
    is_long = order_req == longest
    extra = jnp.where(is_long, 0, extra)
    before = jnp.cumsum(extra) - extra
    room = 2 * LEAF_PLACES_SUM // 3 - REQUESTS - (LONG_PAGES - 1)
    extra = jnp.clip(room - before, 0, extra)
    extra = jnp.where(is_long, LONG_PAGES - 1, extra)
    count = 1 + extra
    last_fill = jax.random.randint(sampler_seeds[3], (REQUESTS,), 1, PAGE + 1)
    last_fill = jnp.where(is_long, PAGE, last_fill)
    lengths = (count - 1) * PAGE + last_fill
    starts = jnp.cumsum(count) - count
    total = jnp.sum(count)
    current_position = jnp.arange(LEAF_PLACES_SUM, dtype=jnp.int32)
    owner_of = jnp.sum((starts[None, :] <= current_position[:, None]).astype(jnp.int32), axis=1) - 1
    within = current_position - starts[owner_of]
    fill_of = jnp.where(within == count[owner_of] - 1, last_fill[owner_of], PAGE)
    is_live = current_position < total
    owner_of = jnp.where(is_live, owner_of, -1)
    fill_of = jnp.where(is_live, fill_of, 0)
    partition_number = LEAF_PLACES_SUM // LEAVES_EACH_PART
    appended_symbol = jnp.left_shift(1, jax.random.randint(sampler_seeds[4], (partition_number,), 0, 12))
    extreme_perturbation = jax.random.randint(sampler_seeds[5], (LEAF_PLACES_SUM,), 0, 1024)
    proposal_rating = (appended_symbol[current_position // LEAVES_EACH_PART] + extreme_perturbation) * LEAF_PLACES_SUM + current_position
    slot_of = jnp.argsort(-proposal_rating, stable=True)
    owner = jnp.zeros((LEAF_PLACES_SUM,), jnp.int32).at[slot_of].set(owner_of.astype(jnp.int32))
    fill = jnp.zeros((LEAF_PLACES_SUM,), jnp.int32).at[slot_of].set(fill_of.astype(jnp.int32))
    return (owner, fill, lengths.astype(jnp.int32))


def draw_page_owner(key, part):
    return page_layout(key)[0]


def draw_page_fill(key, part):
    return page_layout(key)[1]


def draw_cache_len(key, part):
    return page_layout(key)[2]


def draw_tree_parent(key, part):
    places = jnp.arange(TREE, dtype=jnp.int32)
    raw = jax.random.randint(jax.random.fold_in(key, 3), (REQUESTS, TREE), 0, jnp.maximum(places, 1)[None, :])
    return jnp.where(places[None, :] == 0, 0, raw).astype(jnp.int32)


def draw_k_pages(key, part):
    shape = (LEAF_PLACES_SUM, PAGE, HEADS, HD)
    base = jnp.clip(jax.random.normal(key, shape, jnp.float32), -6.0, 6.0)
    return base.astype(jnp.bfloat16)


def plant(result, own_key, least, largest):
    longest = result.shape.index(max(result.shape))
    spots = []
    for shift in (0, 1):
        where = [jax.random.randint(jax.random.fold_in(own_key, axis), (), 0, length) for axis, length in enumerate(result.shape)]
        where[longest] = (where[longest] + shift) % result.shape[longest]
        spots.append(tuple(where))
    return result.at[spots[0]].set(least).at[spots[1]].set(largest)


def level_of(rng, extent, cuts, low, high):
    def one(position, shards_of):
        draws = jax.random.uniform(jax.random.fold_in(jax.random.fold_in(rng, 6), position), (shards_of,), jnp.float32, low / len(cuts), high / len(cuts))
        return jnp.repeat(jnp.exp(draws), extent[position] // shards_of).reshape((-1,) + (1,) * (len(extent) - position - 1))

    gain = one(*cuts[0])
    for cut in cuts[1:]:
        gain = gain * one(*cut)
    return gain


def scatter_about(stream_key, shape, scale, limit, pieces=(), kind=jnp.bfloat16):
    result = jax.random.normal(stream_key, shape, jnp.float32) * scale
    if len(pieces) > 0:
        result = level_of(stream_key, shape, pieces, -0.22, 0.18) * result
    return jnp.clip(result, min=-limit, max=limit).astype(kind)


def setup_inputs(seed: int = 0) -> dict:
    keys = jax.random.split(jax.random.key(seed), 18)
    streams = scatter_about(keys[0], (TOKENS, NS, D), 1.0, 6.0, ((0, 8), (2, 4)))
    hc_in = jnp.clip(jax.random.uniform(keys[1], (2, NS), jnp.float32, 0.2, 1.0), 0.2, 1.0)
    hc_mix = jnp.clip(jax.random.uniform(keys[2], (2, NS, NS), jnp.float32, -0.4, 0.4), -0.4, 0.4)
    hc_out = jnp.clip(jax.random.uniform(keys[3], (2, NS), jnp.float32, 0.5, 1.5), 0.5, 1.5)
    qkv_weight = scatter_about(keys[4], (D, 3, HEADS * HD), D ** -0.5, 0.125, ((2, 4),))
    out_weight = scatter_about(keys[5], (HEADS * HD, D), (HEADS * HD) ** -0.5, 0.125, ((0, 4),))
    up_gate = scatter_about(keys[6], (D, 2, FF), D ** -0.5, 0.125, ((2, 4),))
    down_weight = scatter_about(keys[7], (FF, D), FF ** -0.5, 0.0625, ((0, 4),))
    draft_weight = scatter_about(keys[8], (NDRAFT, D, D), D ** -0.5, 0.125, ((2, 4),))
    lm_head = scatter_about(keys[9], (D, VOCAB), D ** -0.5, 0.125, ((1, 32),))
    k_pages = draw_k_pages(jax.random.fold_in(keys[17], 71), 0)
    v_pages = scatter_about(keys[11], (LEAF_PLACES_SUM, PAGE, HEADS, HD), 1.0, 6.0, ((0, 8), (2, 4)))
    page_owner = draw_page_owner(jax.random.fold_in(keys[17], 71), 0)
    page_fill = draw_page_fill(jax.random.fold_in(keys[17], 71), 0)
    cache_len = draw_cache_len(jax.random.fold_in(keys[17], 71), 0)
    tree_parent = draw_tree_parent(jax.random.fold_in(keys[17], 71), 0)
    accepted_index = plant(jax.random.randint(keys[16], (REQUESTS,), 0, TREE), jax.random.fold_in(keys[16], 1), 0, TREE - 1).astype(jnp.int32)
    return dict(streams=streams, hc_in=hc_in, hc_mix=hc_mix, hc_out=hc_out, qkv_weight=qkv_weight, out_weight=out_weight, up_gate=up_gate, down_weight=down_weight, draft_weight=draft_weight, lm_head=lm_head, k_pages=k_pages, v_pages=v_pages, page_owner=page_owner, page_fill=page_fill, cache_len=cache_len, tree_parent=tree_parent, accepted_index=accepted_index)


NEG_FILL = -1e+30
PRECISE = lax.Precision.HIGHEST

def layer_norm(values):
    center = lax.optimization_barrier(jnp.mean(values, axis=-1, keepdims=True))
    square = lax.optimization_barrier(jnp.mean(values * values, axis=-1, keepdims=True))
    return (values - center) * lax.rsqrt(square - center * center + 1e-05)

def ancestors(parents):
    length = parents.shape[1]
    places = jnp.arange(length, dtype=jnp.int32)
    linked = (parents[:, :, None] == places[None, None, :]) | (places[:, None] == places[None, :])[None]
    reach = linked.astype(jnp.float32)
    for repeat in range(max(1, (length - 1).bit_length())):
        reach = jnp.minimum(jnp.einsum('jik,jkl->jil', reach, reach, precision=PRECISE), 1.0)
    return reach

def rotate(values, positions):
    half = values.shape[-1] // 2
    freqs = jnp.exp(jnp.arange(half, dtype=jnp.float32) * (-2.0 * math.log(10000.0) / values.shape[-1]))
    angles = positions.astype(jnp.float32)[:, None] * freqs[None, :]
    cosine = jnp.cos(angles)[:, None, :]
    sine = jnp.sin(angles)[:, None, :]
    first = values[..., :half]
    second = values[..., half:]
    return jnp.concatenate([first * cosine - second * sine, second * cosine + first * sine], axis=-1)

def blend(stream_vals, weights):
    total = weights[0] * stream_vals[:, 0]
    for index in range(1, stream_vals.shape[1]):
        total = total + weights[index] * stream_vals[:, index]
    return total

def remix(stream_vals, mixing, out_scale, delta):
    count = stream_vals.shape[1]
    matrix = jnp.eye(count, dtype=jnp.float32) + mixing
    rows = [blend(stream_vals, matrix[:, target]) + out_scale[target] * delta for target in range(count)]
    return jnp.stack(rows, axis=1)

def stream_total(stream_vals):
    total = stream_vals[:, 0]
    for index in range(1, stream_vals.shape[1]):
        total = total + stream_vals[:, index]
    return total

def rounded(values):
    return lax.optimization_barrier(values.astype(jnp.bfloat16)).astype(jnp.float32)

def reference(streams, hc_in, hc_mix, hc_out, qkv_weight, out_weight, up_gate, down_weight, draft_weight, lm_head, k_pages, v_pages, page_owner, page_fill, cache_len, tree_parent, accepted_index):
    reach = ancestors(tree_parent)
    depth = (lax.optimization_barrier(jnp.sum(reach, axis=2)) - 1.0).astype(jnp.int32)
    positions = (cache_len[:, None] + depth).reshape(TOKENS)
    stream_vals = streams.astype(jnp.float32)
    normed = layer_norm(blend(stream_vals, hc_in[0])).astype(jnp.bfloat16)
    projected = jnp.dot(normed, qkv_weight.reshape(D, 3 * HEADS * HD), preferred_element_type=jnp.float32)
    projected = projected.reshape(TOKENS, 3, HEADS, HD)
    queries = (rotate(projected[:, 0], positions) * HD ** (-0.5)).astype(jnp.bfloat16)
    keys_new = rotate(projected[:, 1], positions).astype(jnp.bfloat16)
    values_new = projected[:, 2].astype(jnp.bfloat16)
    query_all = queries.reshape(REQUESTS, TREE, HEADS, HD)
    key_all = keys_new.reshape(REQUESTS, TREE, HEADS, HD)
    value_all = values_new.reshape(REQUESTS, TREE, HEADS, HD)
    safe_owner = jnp.maximum(page_owner, 0)
    live = (page_owner >= 0)[:, None] & (jnp.arange(PAGE, dtype=jnp.int32)[None, :] < page_fill[:, None])
    owned = (page_owner[:, None] == jnp.arange(REQUESTS, dtype=jnp.int32)[None, :]).astype(jnp.float32)

    def one_head(head):
        query = lax.dynamic_index_in_dim(query_all, head, 2, keepdims=False).astype(jnp.float32)
        key_new = lax.dynamic_index_in_dim(key_all, head, 2, keepdims=False).astype(jnp.float32)
        value_new = lax.dynamic_index_in_dim(value_all, head, 2, keepdims=False).astype(jnp.float32)
        key_old = lax.dynamic_index_in_dim(k_pages, head, 2, keepdims=False).astype(jnp.float32)
        value_old = lax.dynamic_index_in_dim(v_pages, head, 2, keepdims=False).astype(jnp.float32)
        cache_scores = jnp.einsum('sqd,spd->sqp', query[safe_owner], key_old, precision=PRECISE)
        cache_scores = jnp.where(live[:, None, :], cache_scores, NEG_FILL)
        tree_scores = jnp.einsum('jqd,jkd->jqk', query, key_new, precision=PRECISE)
        tree_scores = jnp.where(reach > 0, tree_scores, NEG_FILL)
        page_top = lax.optimization_barrier(jnp.max(cache_scores, axis=2))
        owned_top = lax.optimization_barrier(jnp.max(jnp.where(owned[:, :, None] > 0, page_top[:, None, :], NEG_FILL), axis=0))
        top = jnp.maximum(owned_top, lax.optimization_barrier(jnp.max(tree_scores, axis=2)))
        cache_weights = jnp.where(live[:, None, :], jnp.exp(cache_scores - top[safe_owner][:, :, None]), 0.0)
        tree_weights = jnp.where(reach > 0, jnp.exp(tree_scores - top[:, :, None]), 0.0)
        total = jnp.dot(owned.T, lax.optimization_barrier(jnp.sum(cache_weights, axis=2)), precision=PRECISE) + lax.optimization_barrier(jnp.sum(tree_weights, axis=2))
        page_sums = jnp.einsum('sqp,spd->sqd', rounded(cache_weights), value_old, precision=PRECISE)
        summed = jnp.dot(owned.T, page_sums.reshape(LEAF_PLACES_SUM, TREE * HD), precision=PRECISE).reshape(REQUESTS, TREE, HD)
        summed = summed + jnp.einsum('jqk,jkd->jqd', rounded(tree_weights), value_new, precision=PRECISE)
        return summed / total[:, :, None]
    per_head = lax.map(one_head, jnp.arange(HEADS, dtype=jnp.int32))
    attended = jnp.transpose(per_head, (1, 2, 0, 3)).reshape(TOKENS, HEADS * HD).astype(jnp.bfloat16)
    attn_delta = jnp.dot(attended, out_weight, preferred_element_type=jnp.float32)
    first_streams = remix(stream_vals, hc_mix[0], hc_out[0], attn_delta)
    normed_mid = layer_norm(blend(first_streams, hc_in[1])).astype(jnp.bfloat16)
    gate_up = jnp.dot(normed_mid, up_gate.reshape(D, 2 * FF), preferred_element_type=jnp.float32)
    hidden = (jax.nn.silu(gate_up[:, :FF]) * gate_up[:, FF:]).astype(jnp.bfloat16)
    mlp_delta = jnp.dot(hidden, down_weight, preferred_element_type=jnp.float32)
    second_streams = remix(first_streams, hc_mix[1], hc_out[1], mlp_delta)
    new_streams = second_streams.astype(jnp.bfloat16)
    rows_taken = jnp.arange(REQUESTS, dtype=jnp.int32) * TREE + accepted_index
    final_norm = layer_norm(stream_total(second_streams[rows_taken]))
    branch = jnp.einsum('jd,kde->jke', rounded(final_norm), draft_weight.astype(jnp.float32), precision=PRECISE)
    drafts = (final_norm[:, None, :] + jax.nn.silu(branch)).astype(jnp.bfloat16)
    logits = jnp.dot(drafts.reshape(REQUESTS * NDRAFT, D), lm_head, preferred_element_type=jnp.float32)
    return (new_streams, logits.reshape(REQUESTS, NDRAFT, VOCAB))
```

```python
import functools
import math

import jax
import jax.numpy as jnp
from jax import lax
from jax.experimental import pallas as pl
from jax.experimental.pallas import tpu as pltpu
from jax.sharding import PartitionSpec as P

NEG_FILL = -1e30
EMPTY = -1e29
PRECISE = lax.Precision.HIGHEST
CHUNKS = 2
LANES = 128
VMEM_BYTES = 40 * 1024 * 1024


def params(count=1):
    return pltpu.CompilerParams(
        dimension_semantics=("arbitrary",) * count, vmem_limit_bytes=VMEM_BYTES
    )


def ancestors(parents):
    length = parents.shape[1]
    places = jnp.arange(length, dtype=jnp.int32)
    linked = (parents[:, :, None] == places[None, None, :]) | (places[:, None] == places[None, :])[
        None
    ]
    reach = linked.astype(jnp.float32)
    for repeat in range(max(1, (length - 1).bit_length())):
        reach = jnp.minimum(jnp.einsum("jik,jkl->jil", reach, reach, precision=PRECISE), 1.0)
    return reach


def layer_norm(values):
    center = jnp.mean(values, axis=-1, keepdims=True)
    square = jnp.mean(values * values, axis=-1, keepdims=True)
    return (values - center) * lax.rsqrt(square - center * center + 1e-05)


def blend(stream_vals, weights):
    total = weights[0] * stream_vals[:, 0]
    for index in range(1, stream_vals.shape[1]):
        total = total + weights[index] * stream_vals[:, index]
    return total


def chain_gather(block):
    count = lax.axis_size("head")
    right, left = [block], [block]
    for step in range(1, count):
        right.append(
            lax.ppermute(right[-1], "head", [(z, z + 1) for z in range(step - 1, count - 1)])
        )
        left.append(
            lax.ppermute(left[-1], "head", [(z, z - 1) for z in range(1, count - step + 1)])
        )
    return right, left


def in_order(right, left):
    count = lax.axis_size("head")
    rank = lax.axis_index("head")
    blocks = []
    for source in range(count):
        value = right[0]
        for step in range(1, count):
            if source + step < count:
                value = jnp.where(rank == source + step, right[step], value)
            if source - step >= 0:
                value = jnp.where(rank == source - step, left[step], value)
        blocks.append(value)
    return blocks


def chain_scatter(share):
    count = lax.axis_size("head")
    shares = {}
    for step in range(1, count):
        for key in (step, count - step):
            if key not in shares:
                shares[key] = share(key).astype(jnp.bfloat16)
    from_left = from_right = None
    for step in range(1, count):
        to_right, to_left = shares[step], shares[count - step]
        if step > 1:
            to_right = (to_right.astype(jnp.float32) + from_left.astype(jnp.float32)).astype(
                jnp.bfloat16
            )
            to_left = (to_left.astype(jnp.float32) + from_right.astype(jnp.float32)).astype(
                jnp.bfloat16
            )
        from_left = lax.ppermute(to_right, "head", [(z, z + 1) for z in range(step)])
        from_right = lax.ppermute(
            to_left, "head", [(z, z - 1) for z in range(count - step, count)]
        )
    return share(0) + from_left.astype(jnp.float32) + from_right.astype(jnp.float32)


def shift_gather(small):
    count = lax.axis_size("head")
    rank = lax.axis_index("head")
    parts = [small] + [
        lax.ppermute(small, "head", [(z, (z + step) % count) for z in range(count)])
        for step in range(1, count)
    ]
    stacked = jnp.stack(parts)
    return jnp.stack(
        [
            lax.dynamic_index_in_dim(stacked, (rank - source) % count, 0, keepdims=False)
            for source in range(count)
        ]
    )


def gathered_norm(values, width):
    local = values.shape[1]
    sums = jnp.sum(values, axis=1)
    squares = jnp.sum(values * values, axis=1)
    center = sums / local
    sent = (values - center[:, None]).astype(jnp.bfloat16)
    stats = shift_gather(jnp.stack([sums, squares]))
    right, left = chain_gather(sent)
    mean = jnp.sum(stats[:, 0], axis=0) / width
    variance = jnp.sum(stats[:, 1], axis=0) / width - mean * mean
    scale = lax.rsqrt(variance + 1e-05)
    blocks = in_order(right, left)
    normed = [
        (
            (block.astype(jnp.float32) + (stats[rank, 0] / local - mean)[:, None])
            * scale[:, None]
        ).astype(jnp.bfloat16)
        for rank, block in enumerate(blocks)
    ]
    return jnp.concatenate(normed, axis=1), right[-1]


def columns_for(weight, step):
    count = lax.axis_size("head")
    width = weight.shape[1] // count
    owner = (lax.axis_index("head") - step) % count
    return lax.dynamic_slice_in_dim(weight, owner * width, width, 1)


def swapped(values, bit):
    count = lax.axis_size("req")
    return lax.ppermute(values, "req", [(r, r ^ bit) for r in range(count)])


def bit_orders():
    bits = [1 << index for index in range((lax.axis_size("req") - 1).bit_length())]
    return bits[0], (bits[1:], bits[1:][::-1])


def gather_requests(values):
    half = values.shape[0] // 2
    near, orders = bit_orders()
    parts = []
    for part, order in enumerate(orders):
        blocks = {0: values[part * half : (part + 1) * half]}
        for bit in list(order) + [near]:
            for index in list(blocks):
                blocks[index ^ bit] = swapped(blocks[index], bit)
        parts.append(blocks)
    return [
        jnp.concatenate([blocks[index] for blocks in parts])
        for index in range(lax.axis_size("req"))
    ]


def scatter_requests(sums, logs, merge):
    near, orders = bit_orders()
    count = lax.axis_size("req")
    far = count // 2
    state = []
    mine = [sums[:far], logs[:far]]
    theirs = [swapped(sums[far:], near), swapped(logs[far:], near)]
    merged = merge(mine, theirs)
    half = sums.shape[1] // 2
    done = []
    for part, order in enumerate(orders):
        kept = [value[:, part * half : (part + 1) * half] for value in merged]
        places = list(range(far))
        for place, bit in enumerate(order):
            stay = [at for at, index in enumerate(places) if not index & (bit >> 1)]
            leave = [at for at, index in enumerate(places) if index & (bit >> 1)]
            pick = lambda value, which: jnp.concatenate([value[at : at + 1] for at in which])
            ours = [pick(value, stay) for value in kept]
            got = [swapped(pick(value, leave), bit) for value in kept]
            places = [places[at] for at in stay]
            kept = merge(ours, got) if place < len(order) - 1 else (ours, got)
        done.append(kept)
    return done


def rotate_kernel(heads, size, scale, x_ref, cos_ref, sin_ref, q_ref, k_ref, v_ref):
    width = heads * size
    cosine, sine = cos_ref[...], sin_ref[...]
    for head in range(heads):
        at = head * size
        for base, out_ref, factor in ((0, q_ref, scale), (width, k_ref, 1.0)):
            values = x_ref[:, base + at : base + at + size]
            turned = values * cosine + pltpu.roll(values, size // 2, 1) * sine
            out_ref[:, at : at + size] = (turned * factor).astype(out_ref.dtype)
    v_ref[...] = x_ref[:, 2 * width :].astype(v_ref.dtype)


def rotate_all(projected, cosine, sine, heads, size, rows):
    tokens = projected.shape[0]
    out = jax.ShapeDtypeStruct((tokens, heads * size), jnp.bfloat16)
    block = lambda width: pl.BlockSpec((rows, width), lambda i: (i, 0))
    return pl.pallas_call(
        functools.partial(rotate_kernel, heads, size, size ** (-0.5)),
        grid=(tokens // rows,),
        in_specs=[block(3 * heads * size), block(size), block(size)],
        out_specs=[block(heads * size)] * 3,
        out_shape=[out] * 3,
        compiler_params=params(),
        name="rotate",
    )(projected, cosine, sine)


def lay_logs(columns, rows):
    lane = lax.broadcasted_iota(jnp.int32, (LANES, LANES), 1)
    table = jnp.full((LANES, LANES), NEG_FILL, jnp.float32)
    for head, column in enumerate(columns):
        tall = jnp.concatenate(
            [column, jnp.full((LANES - rows, 1), NEG_FILL, jnp.float32)], axis=0
        )
        table = jnp.where(lane == head, tall, table)
    return jnp.transpose(table)[:8]


def tree_kernel(heads, size, q_ref, k_ref, v_ref, reach_ref, out_ref, log_ref):
    seen = reach_ref[0] > 0
    logs = []
    for head in range(heads):
        at = slice(head * size, (head + 1) * size)
        scores = lax.dot_general(
            q_ref[0, :, at],
            k_ref[0, :, at],
            (((1,), (1,)), ((), ())),
            preferred_element_type=jnp.float32,
        )
        scores = jnp.where(seen, scores, NEG_FILL)
        top = jnp.max(scores, axis=1, keepdims=True)
        weights = jnp.where(seen, jnp.exp(scores - top), 0.0)
        total = jnp.sum(weights, axis=1, keepdims=True)
        summed = jnp.dot(
            weights.astype(jnp.bfloat16), v_ref[0, :, at], preferred_element_type=jnp.float32
        )
        out_ref[0, :, at] = summed / total
        logs.append(top + jnp.log(total))
    log_ref[0] = lay_logs(logs, q_ref.shape[1])


def tree_attention(queries, keys, values, reach, heads, size):
    requests, tree, width = queries.shape
    block = pl.BlockSpec((1, tree, width), lambda j: (j, 0, 0))
    return pl.pallas_call(
        functools.partial(tree_kernel, heads, size),
        grid=(requests,),
        in_specs=[block] * 3 + [pl.BlockSpec((1, tree, tree), lambda j: (j, 0, 0))],
        out_specs=[block, pl.BlockSpec((1, 8, LANES), lambda j: (j, 0, 0))],
        out_shape=[
            jax.ShapeDtypeStruct((requests, tree, width), jnp.float32),
            jax.ShapeDtypeStruct((requests, 8, LANES), jnp.float32),
        ],
        compiler_params=params(),
        name="tree_attention",
    )(queries, keys, values, reach)


def page_kernel(
    heads,
    size,
    page_ref,
    place_ref,
    fill_ref,
    first_ref,
    last_ref,
    live_ref,
    q_ref,
    k_ref,
    v_ref,
    out_ref,
    log_ref,
    acc_ref,
    top_ref,
    total_ref,
):
    step = pl.program_id(0)
    tree = q_ref.shape[1]

    @pl.when(step == 0)
    def _():
        log_ref[...] = jnp.full(log_ref.shape, NEG_FILL, jnp.float32)

    @pl.when(step < live_ref[0])
    def _():
        @pl.when(first_ref[step] == 1)
        def _():
            acc_ref[...] = jnp.zeros(acc_ref.shape, jnp.float32)
            top_ref[...] = jnp.full(top_ref.shape, NEG_FILL, jnp.float32)
            total_ref[...] = jnp.zeros(total_ref.shape, jnp.float32)

        entries = k_ref.shape[2]
        valid = lax.broadcasted_iota(jnp.int32, (tree, entries), 1) < fill_ref[step]
        for head in range(heads):
            at = slice(head * size, (head + 1) * size)
            scores = lax.dot_general(
                q_ref[0, :, at],
                k_ref[0, head],
                (((1,), (1,)), ((), ())),
                preferred_element_type=jnp.float32,
            )
            scores = jnp.where(valid, scores, NEG_FILL)
            before = top_ref[head]
            top = jnp.maximum(before, jnp.max(scores, axis=1, keepdims=True))
            weights = jnp.where(valid, jnp.exp(scores - top), 0.0)
            decay = jnp.exp(before - top)
            top_ref[head] = top
            total_ref[head] = total_ref[head] * decay + jnp.sum(weights, axis=1, keepdims=True)
            acc_ref[:, at] = acc_ref[:, at] * decay + jnp.dot(
                weights.astype(jnp.bfloat16), v_ref[0, head], preferred_element_type=jnp.float32
            )

        @pl.when(last_ref[step] == 1)
        def _():
            logs = []
            for head in range(heads):
                at = slice(head * size, (head + 1) * size)
                total = total_ref[head]
                some = total > 0
                safe = jnp.where(some, total, 1.0)
                out_ref[0, :, at] = (acc_ref[:, at] / safe).astype(out_ref.dtype)
                logs.append(jnp.where(some, top_ref[head] + jnp.log(safe), NEG_FILL)[:, :1])
            log_ref[place_ref[step]] = lay_logs(logs, tree)


def page_attention(queries, k_pages, v_pages, plan, heads, size):
    requests, tree, width = queries.shape
    entries = k_pages.shape[2]
    row = pl.BlockSpec((1, tree, width), lambda p, page, place, *rest: (place[p], 0, 0))
    leaf = pl.BlockSpec(
        (1, heads, entries, size), lambda p, page, place, *rest: (page[p], 0, 0, 0)
    )
    grid_spec = pltpu.PrefetchScalarGridSpec(
        num_scalar_prefetch=6,
        grid=(k_pages.shape[0],),
        in_specs=[row, leaf, leaf],
        out_specs=[
            row,
            pl.BlockSpec((requests, 8, LANES), lambda p, *rest: (0, 0, 0)),
        ],
        scratch_shapes=[
            pltpu.VMEM((tree, width), jnp.float32),
            pltpu.VMEM((heads, tree, size), jnp.float32),
            pltpu.VMEM((heads, tree, size), jnp.float32),
        ],
    )
    return pl.pallas_call(
        functools.partial(page_kernel, heads, size),
        grid_spec=grid_spec,
        out_shape=[
            jax.ShapeDtypeStruct((requests, tree, width), jnp.bfloat16),
            jax.ShapeDtypeStruct((requests, 8, LANES), jnp.float32),
        ],
        compiler_params=params(),
        name="page_attention",
    )(*plan, queries, k_pages, v_pages)


def merge_kernel(heads, size, count, *refs):
    sums, logs, out_ref = refs[:count], refs[count : 2 * count], refs[2 * count]
    log_ref = refs[2 * count + 1] if len(refs) > 2 * count + 1 else None
    tree = out_ref.shape[1]
    for request in range(out_ref.shape[0]):
        tables = [ref[request] for ref in logs]
        top = functools.reduce(jnp.maximum, tables)
        total = functools.reduce(lambda a, b: a + b, [jnp.exp(table - top) for table in tables])
        merged = top + jnp.log(total)
        if log_ref is not None:
            log_ref[request] = merged
        shares = [
            jnp.transpose(jnp.where(table > EMPTY, jnp.exp(table - merged), 0.0))
            for table in tables
        ]
        for head in range(heads):
            at = slice(head * size, (head + 1) * size)
            value = jnp.zeros((tree, size), jnp.float32)
            for ref, share in zip(sums, shares):
                factor = share[:tree, head : head + 1]
                term = ref[request, :, at].astype(jnp.float32)
                value = value + jnp.where(factor > 0, term * factor, 0.0)
            out_ref[request, :, at] = value.astype(out_ref.dtype)


def merge_partials(pairs, heads, size, with_logs=True):
    requests, tree, width = pairs[0][0].shape
    group = max(size for size in (1, 2, 4, 8) if requests % size == 0)
    big = pl.BlockSpec((group, tree, width), lambda j: (j, 0, 0))
    small = pl.BlockSpec((group, 8, LANES), lambda j: (j, 0, 0))
    out_specs = [big, small] if with_logs else [big]
    out_shape = [
        jax.ShapeDtypeStruct((requests, tree, width), jnp.bfloat16),
        jax.ShapeDtypeStruct((requests, 8, LANES), jnp.float32),
    ][: len(out_specs)]
    return pl.pallas_call(
        functools.partial(merge_kernel, heads, size, len(pairs)),
        grid=(requests // group,),
        in_specs=[big] * len(pairs) + [small] * len(pairs),
        out_specs=out_specs,
        out_shape=out_shape,
        compiler_params=params(),
        name="merge_partials",
    )(*[pair[0] for pair in pairs], *[pair[1] for pair in pairs])


def page_plan(owner, fill, first_request, requests, all_local, count):
    slots = owner.shape[0]
    me = lax.axis_index("req")
    source = owner // all_local
    local = owner % all_local - first_request
    mine = (owner >= 0) & (local >= 0) & (local < requests)
    index = source ^ me
    index = (index & 1) * (count // 2) + (index >> 1)
    place = jnp.where(mine, index * requests + local, count * requests)
    spot = jnp.arange(slots, dtype=jnp.int32)
    ahead = (place[None, :] < place[:, None]) | (
        (place[None, :] == place[:, None]) & (spot[None, :] < spot[:, None])
    )
    rank = jnp.sum(ahead.astype(jnp.int32), axis=1)
    live = jnp.sum(mine.astype(jnp.int32))
    wanted = jnp.minimum(spot, jnp.maximum(live - 1, 0))
    chosen = rank[None, :] == wanted[:, None]
    take = lambda values: jnp.sum(jnp.where(chosen, values[None, :], 0), axis=1)
    pages, places, fills = take(spot), take(jnp.where(mine, place, 0)), take(fill)
    changed = (places[1:] != places[:-1]).astype(jnp.int32)
    one = jnp.ones((1,), jnp.int32)
    first = jnp.concatenate([one, changed])
    last = jnp.concatenate([changed, one])
    last = jnp.where(spot == live - 1, 1, last)
    return (pages, places, fills, first, last, live[None])


def on_device(
    streams,
    hc_in,
    hc_mix,
    hc_out,
    qkv_weight,
    out_weight,
    up_gate,
    down_weight,
    draft_weight,
    lm_head,
    k_pages,
    v_pages,
    page_owner,
    page_fill,
    cache_len,
    tree_parent,
    accepted_index,
):
    tokens_local = streams.shape[0]
    stream_count = streams.shape[1]
    feature_local = streams.shape[2]
    width = qkv_weight.shape[0]
    req_local = cache_len.shape[0]
    tree_size = tree_parent.shape[1]
    heads = k_pages.shape[2]
    size = k_pages.shape[3]
    draft_count = draft_weight.shape[0]
    parts = lax.axis_size("req")
    all_requests = req_local * parts

    identity = jnp.eye(stream_count, dtype=jnp.float32)
    first_mix, second_mix = identity + hc_mix[0], identity + hc_mix[1]
    mid_in = jnp.sum(first_mix * hc_in[1][None, :], axis=1)
    mid_out = jnp.sum(hc_out[0] * hc_in[1])
    both_mix = jnp.sum(first_mix[:, :, None] * second_mix[None, :, :], axis=1)
    both_out = jnp.sum(hc_out[0][:, None] * second_mix, axis=0)

    reach = ancestors(tree_parent)
    depth = (jnp.sum(reach, axis=2) - 1.0).astype(jnp.int32)
    positions = (cache_len[:, None] + depth).reshape(tokens_local)
    half = size // 2
    freqs = jnp.exp(jnp.arange(half, dtype=jnp.float32) * (-2.0 * math.log(10000.0) / size))
    angles = positions.astype(jnp.float32)[:, None] * freqs[None, :]
    cosine, sine = jnp.cos(angles), jnp.sin(angles)
    cosine = jnp.concatenate([cosine, cosine], axis=1)
    sine = jnp.concatenate([-sine, sine], axis=1)

    k_heads = jnp.transpose(k_pages, (0, 2, 1, 3))
    v_heads = jnp.transpose(v_pages, (0, 2, 1, 3))
    hidden_local = up_gate.shape[2]
    gate_weight, up_weight = up_gate[:, 0], up_gate[:, 1]

    step_requests = req_local // CHUNKS
    step_tokens = step_requests * tree_size
    merge = lambda ours, got: merge_flat(ours, got, heads, size)

    token = None
    attended_in = []
    for chunk in range(CHUNKS):
        rows = slice(chunk * step_tokens, (chunk + 1) * step_tokens)
        stream_vals = streams[rows].astype(jnp.float32)
        mixed_in = blend(stream_vals, hc_in[0])
        if token is not None:
            mixed_in, token = lax.optimization_barrier((mixed_in, token))
        normed, token = gathered_norm(mixed_in, width)
        attended_in.append(normed)

    attn_parts, mlp_parts = [], []
    for chunk in range(CHUNKS):
        rows = slice(chunk * step_tokens, (chunk + 1) * step_tokens)
        asked = slice(chunk * step_requests, (chunk + 1) * step_requests)
        normed = attended_in[chunk]
        projected = jnp.concatenate(
            [
                jnp.dot(normed, qkv_weight[:, third], preferred_element_type=jnp.float32)
                for third in range(3)
            ],
            axis=1,
        )
        queries, keys, values = rotate_all(
            projected, cosine[rows], sine[rows], heads, size, 2 * tree_size
        )
        shape = (step_requests, tree_size, heads * size)
        queries, keys, values = (item.reshape(shape) for item in (queries, keys, values))
        blocks = gather_requests(queries)
        near_last = [index for low in (0, 1) for index in range(parts) if index & 1 == low]
        query_all = jnp.concatenate([blocks[index] for index in near_last])
        plan = page_plan(
            page_owner, page_fill, chunk * step_requests, step_requests, req_local, parts
        )
        sums, logs = page_attention(query_all, k_heads, v_heads, plan, heads, size)
        tree_pair = tree_attention(queries, keys, values, reach[asked], heads, size)
        done = scatter_requests(
            sums.reshape(parts, step_requests, tree_size, heads * size),
            logs.reshape(parts, step_requests, 8, LANES),
            merge,
        )
        part_requests = step_requests // 2
        attended = []
        for part, (ours, got) in enumerate(done):
            own = slice(part * part_requests, (part + 1) * part_requests)
            pairs = [
                tuple(value.reshape((-1,) + value.shape[2:]) for value in pair)
                for pair in (ours, got)
            ] + [(tree_pair[0][own], tree_pair[1][own])]
            attended.append(merge_partials(pairs, heads, size, with_logs=False)[0])
        attended = jnp.concatenate(attended).reshape(step_tokens, heads * size)
        attn_delta = chain_scatter(
            lambda step: jnp.dot(
                attended, columns_for(out_weight, step), preferred_element_type=jnp.float32
            )
        )
        attn_parts.append(attn_delta)

        stream_vals = streams[rows].astype(jnp.float32)
        mixed_mid = blend(stream_vals, mid_in) + mid_out * attn_delta
        normed_mid, token = gathered_norm(mixed_mid, width)
        gate = jnp.dot(normed_mid, gate_weight, preferred_element_type=jnp.float32)
        up = jnp.dot(normed_mid, up_weight, preferred_element_type=jnp.float32)
        hidden = (jax.nn.silu(gate) * up).astype(jnp.bfloat16)
        mlp_parts.append(
            chain_scatter(
                lambda step: jnp.dot(
                    hidden, columns_for(down_weight, step), preferred_element_type=jnp.float32
                )
            )
        )

    attn_delta = jnp.concatenate(attn_parts)
    mlp_delta = jnp.concatenate(mlp_parts)
    stream_vals = streams.astype(jnp.float32)
    new_streams = both_out[None, :, None] * attn_delta[:, None] + (
        hc_out[1][None, :, None] * mlp_delta[:, None]
    )
    for index in range(stream_count):
        new_streams = (
            new_streams + both_mix[index][None, :, None] * stream_vals[:, index : index + 1]
        )
    new_streams = new_streams.astype(jnp.bfloat16)

    rows_taken = jnp.arange(req_local, dtype=jnp.int32) * tree_size + accepted_index
    final_local = (
        jnp.sum(both_out) * attn_delta[rows_taken] + jnp.sum(hc_out[1]) * mlp_delta[rows_taken]
    ) + blend(stream_vals[rows_taken], jnp.sum(both_mix, axis=1))
    final_full = lax.all_gather(final_local, "head", axis=1, tiled=True)
    final_norm = layer_norm(final_full)
    own_columns = lax.dynamic_slice_in_dim(
        final_norm, lax.axis_index("head") * feature_local, feature_local, 1
    )
    branch = jnp.einsum(
        "jd,kde->jke",
        final_norm.astype(jnp.bfloat16),
        draft_weight,
        preferred_element_type=jnp.float32,
    )
    drafted = (own_columns[:, None, :] + jax.nn.silu(branch)).astype(jnp.bfloat16)
    draft_full = lax.all_gather(drafted, "head", axis=2, tiled=True)
    draft_all = lax.all_gather(draft_full, "req", axis=0, tiled=True)
    logits_local = jnp.dot(
        draft_all.reshape(-1, width), lm_head, preferred_element_type=jnp.float32
    )
    logits_local = logits_local.reshape(all_requests, draft_count, -1)
    logits = lax.all_to_all(
        logits_local.astype(jnp.bfloat16), ("req", "head"), split_axis=0, concat_axis=2, tiled=True
    ).astype(logits_local.dtype)
    return (new_streams, logits)


def merge_flat(ours, got, heads, size):
    lead = ours[0].shape[:2]
    pairs = [
        tuple(value.reshape((-1,) + value.shape[2:]) for value in pair) for pair in (ours, got)
    ]
    merged = merge_partials(pairs, heads, size)
    return [value.reshape(lead + value.shape[1:]) for value in merged]


def solution(mesh):
    in_specs = (
        P("req", None, "head"),
        P(),
        P(),
        P(),
        P(None, None, "head"),
        P("head", None),
        P(None, None, "head"),
        P("head", None),
        P(None, None, "head"),
        P(None, ("req", "head")),
        P("req", None, "head", None),
        P("req", None, "head", None),
        P("req"),
        P("req"),
        P("req"),
        P("req", None),
        P("req"),
    )
    out_specs = (P("req", None, "head"), P(("req", "head"), None, None))
    return jax.shard_map(
        on_device, mesh=mesh, in_specs=in_specs, out_specs=out_specs, check_vma=False
    )
```

```python
import functools
import math

import jax
import jax.numpy as jnp
from jax import lax
from jax.experimental import pallas as pl
from jax.experimental.pallas import tpu as pltpu
from jax.sharding import PartitionSpec as P

NEG_FILL = -1e30
EMPTY = -1e29
PRECISE = lax.Precision.HIGHEST
CHUNKS = 2
LANES = 128
VMEM_BYTES = 40 * 1024 * 1024


def params(count=1):
    return pltpu.CompilerParams(
        dimension_semantics=("arbitrary",) * count, vmem_limit_bytes=VMEM_BYTES
    )


def ancestors(parents):
    length = parents.shape[1]
    places = jnp.arange(length, dtype=jnp.int32)
    linked = (parents[:, :, None] == places[None, None, :]) | (places[:, None] == places[None, :])[
        None
    ]
    reach = linked.astype(jnp.float32)
    for repeat in range(max(1, (length - 1).bit_length())):
        reach = jnp.minimum(jnp.einsum("jik,jkl->jil", reach, reach, precision=PRECISE), 1.0)
    return reach


def layer_norm(values):
    center = jnp.mean(values, axis=-1, keepdims=True)
    square = jnp.mean(values * values, axis=-1, keepdims=True)
    return (values - center) * lax.rsqrt(square - center * center + 1e-05)


def blend(stream_vals, weights):
    total = weights[0] * stream_vals[:, 0]
    for index in range(1, stream_vals.shape[1]):
        total = total + weights[index] * stream_vals[:, index]
    return total


def chain_gather(block):
    count = lax.axis_size("head")
    right, left = [block], [block]
    for step in range(1, count):
        right.append(
            lax.ppermute(right[-1], "head", [(z, z + 1) for z in range(step - 1, count - 1)])
        )
        left.append(
            lax.ppermute(left[-1], "head", [(z, z - 1) for z in range(1, count - step + 1)])
        )
    return right, left


def in_order(right, left):
    count = lax.axis_size("head")
    rank = lax.axis_index("head")
    blocks = []
    for source in range(count):
        value = right[0]
        for step in range(1, count):
            if source + step < count:
                value = jnp.where(rank == source + step, right[step], value)
            if source - step >= 0:
                value = jnp.where(rank == source - step, left[step], value)
        blocks.append(value)
    return blocks


def chain_scatter(shares):
    count = lax.axis_size("head")
    from_left = from_right = None
    for step in range(1, count):
        to_right, to_left = shares[step], shares[count - step]
        if step > 1:
            to_right = (to_right.astype(jnp.float32) + from_left.astype(jnp.float32)).astype(
                jnp.bfloat16
            )
            to_left = (to_left.astype(jnp.float32) + from_right.astype(jnp.float32)).astype(
                jnp.bfloat16
            )
        from_left = lax.ppermute(to_right, "head", [(z, z + 1) for z in range(step)])
        from_right = lax.ppermute(
            to_left, "head", [(z, z - 1) for z in range(count - step, count)]
        )
    own = shares[0].astype(jnp.float32)
    return own + from_left.astype(jnp.float32) + from_right.astype(jnp.float32)


def shift_gather(small):
    count = lax.axis_size("head")
    rank = lax.axis_index("head")
    parts = [small] + [
        lax.ppermute(small, "head", [(z, (z + step) % count) for z in range(count)])
        for step in range(1, count)
    ]
    stacked = jnp.stack(parts)
    return jnp.stack(
        [
            lax.dynamic_index_in_dim(stacked, (rank - source) % count, 0, keepdims=False)
            for source in range(count)
        ]
    )


def gathered_norm(values, width):
    local = values.shape[1]
    sums = jnp.sum(values, axis=1)
    squares = jnp.sum(values * values, axis=1)
    center = sums / local
    sent = (values - center[:, None]).astype(jnp.bfloat16)
    stats = shift_gather(jnp.stack([sums, squares]))
    right, left = chain_gather(sent)
    mean = jnp.sum(stats[:, 0], axis=0) / width
    variance = jnp.sum(stats[:, 1], axis=0) / width - mean * mean
    scale = lax.rsqrt(variance + 1e-05)
    blocks = in_order(right, left)
    normed = [
        (
            (block.astype(jnp.float32) + (stats[rank, 0] / local - mean)[:, None])
            * scale[:, None]
        ).astype(jnp.bfloat16)
        for rank, block in enumerate(blocks)
    ]
    return jnp.concatenate(normed, axis=1), right[-1]


def swapped(values, bit):
    count = lax.axis_size("req")
    return lax.ppermute(values, "req", [(r, r ^ bit) for r in range(count)])


def bit_orders():
    bits = [1 << index for index in range((lax.axis_size("req") - 1).bit_length())]
    return bits[0], (bits[1:], bits[1:][::-1])


def gather_requests(values):
    half = values.shape[0] // 2
    near, orders = bit_orders()
    parts = []
    for part, order in enumerate(orders):
        blocks = {0: values[part * half : (part + 1) * half]}
        for bit in order:
            for index in list(blocks):
                blocks[index ^ bit] = swapped(blocks[index], bit)
        parts.append(blocks)
    even = jnp.concatenate([blocks[index] for index in sorted(parts[0]) for blocks in parts])
    return even, swapped(even, near)


def scatter_requests(sums, logs, merge):
    near, orders = bit_orders()
    count = lax.axis_size("req")
    far = count // 2
    state = []
    mine = [sums[:far], logs[:far]]
    theirs = [swapped(sums[far:], near), swapped(logs[far:], near)]
    merged = first_merged = merge(mine, theirs)
    half = sums.shape[1] // 2
    done = []
    for part, order in enumerate(orders):
        kept = [value[:, part * half : (part + 1) * half] for value in merged]
        places = list(range(far))
        for place, bit in enumerate(order):
            stay = [at for at, index in enumerate(places) if not index & (bit >> 1)]
            leave = [at for at, index in enumerate(places) if index & (bit >> 1)]
            pick = lambda value, which: jnp.concatenate([value[at : at + 1] for at in which])
            ours = [pick(value, stay) for value in kept]
            got = [swapped(pick(value, leave), bit) for value in kept]
            places = [places[at] for at in stay]
            kept = merge(ours, got) if place < len(order) - 1 else (ours, got)
        done.append(kept)
    return done, first_merged[1]


def rotate_kernel(heads, size, scale, x_ref, cos_ref, sin_ref, q_ref, k_ref, v_ref):
    width = heads * size
    cosine, sine = cos_ref[...], sin_ref[...]
    for head in range(heads):
        at = head * size
        for base, out_ref, factor in ((0, q_ref, scale), (width, k_ref, 1.0)):
            values = x_ref[:, base + at : base + at + size]
            turned = values * cosine + pltpu.roll(values, size // 2, 1) * sine
            out_ref[:, at : at + size] = (turned * factor).astype(out_ref.dtype)
    v_ref[...] = x_ref[:, 2 * width :].astype(v_ref.dtype)


def rotate_all(projected, cosine, sine, heads, size, rows):
    tokens = projected.shape[0]
    out = jax.ShapeDtypeStruct((tokens, heads * size), jnp.bfloat16)
    block = lambda width: pl.BlockSpec((rows, width), lambda i: (i, 0))
    return pl.pallas_call(
        functools.partial(rotate_kernel, heads, size, size ** (-0.5)),
        grid=(tokens // rows,),
        in_specs=[block(3 * heads * size), block(size), block(size)],
        out_specs=[block(heads * size)] * 3,
        out_shape=[out] * 3,
        compiler_params=params(),
        name="rotate",
    )(projected, cosine, sine)


def lay_logs(columns, rows):
    lane = lax.broadcasted_iota(jnp.int32, (LANES, LANES), 1)
    table = jnp.full((LANES, LANES), NEG_FILL, jnp.float32)
    for head, column in enumerate(columns):
        tall = jnp.concatenate(
            [column, jnp.full((LANES - rows, 1), NEG_FILL, jnp.float32)], axis=0
        )
        table = jnp.where(lane == head, tall, table)
    return jnp.transpose(table)[:8]


def tree_kernel(heads, size, q_ref, k_ref, v_ref, reach_ref, out_ref, log_ref):
    seen = reach_ref[0] > 0
    logs = []
    for head in range(heads):
        at = slice(head * size, (head + 1) * size)
        scores = lax.dot_general(
            q_ref[0, :, at],
            k_ref[0, :, at],
            (((1,), (1,)), ((), ())),
            preferred_element_type=jnp.float32,
        )
        scores = jnp.where(seen, scores, NEG_FILL)
        top = jnp.max(scores, axis=1, keepdims=True)
        weights = jnp.where(seen, jnp.exp(scores - top), 0.0)
        total = jnp.sum(weights, axis=1, keepdims=True)
        summed = jnp.dot(
            weights.astype(jnp.bfloat16), v_ref[0, :, at], preferred_element_type=jnp.float32
        )
        out_ref[0, :, at] = summed / total
        logs.append(top + jnp.log(total))
    log_ref[0] = lay_logs(logs, q_ref.shape[1])


def tree_attention(queries, keys, values, reach, heads, size):
    requests, tree, width = queries.shape
    block = pl.BlockSpec((1, tree, width), lambda j: (j, 0, 0))
    return pl.pallas_call(
        functools.partial(tree_kernel, heads, size),
        grid=(requests,),
        in_specs=[block] * 3 + [pl.BlockSpec((1, tree, tree), lambda j: (j, 0, 0))],
        out_specs=[block, pl.BlockSpec((1, 8, LANES), lambda j: (j, 0, 0))],
        out_shape=[
            jax.ShapeDtypeStruct((requests, tree, width), jnp.float32),
            jax.ShapeDtypeStruct((requests, 8, LANES), jnp.float32),
        ],
        compiler_params=params(),
        name="tree_attention",
    )(queries, keys, values, reach)


def page_kernel(
    heads,
    size,
    page_ref,
    place_ref,
    fill_ref,
    first_ref,
    last_ref,
    live_ref,
    even_ref,
    odd_ref,
    k_ref,
    v_ref,
    out_ref,
    log_ref,
    acc_ref,
    top_ref,
    total_ref,
):
    step = pl.program_id(0)
    tree = even_ref.shape[1]
    spans = [slice(head * size, (head + 1) * size) for head in range(heads)]

    @pl.when(step == 0)
    def _():
        log_ref[...] = jnp.full(log_ref.shape, NEG_FILL, jnp.float32)

    @pl.when(step < live_ref[0])
    def _():
        @pl.when(first_ref[step] == 1)
        def _():
            acc_ref[...] = jnp.zeros(acc_ref.shape, jnp.float32)
            top_ref[...] = jnp.full(top_ref.shape, NEG_FILL, jnp.float32)
            total_ref[...] = jnp.zeros(total_ref.shape, jnp.float32)

        entries = k_ref.shape[2]
        is_even = place_ref[step] < log_ref.shape[0] // 2
        asked = jnp.where(is_even, even_ref[0], odd_ref[0])
        valid = lax.broadcasted_iota(jnp.int32, (tree, entries), 1) < fill_ref[step]
        scores = [
            lax.dot_general(
                asked[:, span],
                k_ref[0, head],
                (((1,), (1,)), ((), ())),
                preferred_element_type=jnp.float32,
            )
            for head, span in enumerate(spans)
        ]
        scores = [jnp.where(valid, score, NEG_FILL) for score in scores]
        before = [top_ref[head] for head in range(heads)]
        tops = [
            jnp.maximum(old, jnp.max(score, axis=1, keepdims=True))
            for old, score in zip(before, scores)
        ]
        weights = [
            jnp.where(valid, jnp.exp(score - top), 0.0) for score, top in zip(scores, tops)
        ]
        decays = [jnp.exp(old - top) for old, top in zip(before, tops)]
        sums = [
            jnp.dot(
                weight.astype(jnp.bfloat16), v_ref[0, head], preferred_element_type=jnp.float32
            )
            for head, weight in enumerate(weights)
        ]
        totals = [
            total_ref[head] * decays[head] + jnp.sum(weights[head], axis=1, keepdims=True)
            for head in range(heads)
        ]
        news = [acc_ref[:, span] * decays[head] + sums[head] for head, span in enumerate(spans)]
        for head, span in enumerate(spans):
            top_ref[head] = tops[head]
            total_ref[head] = totals[head]
            acc_ref[:, span] = news[head]

        @pl.when(last_ref[step] == 1)
        def _():
            logs = []
            for head, span in enumerate(spans):
                total = total_ref[head]
                some = total > 0
                safe = jnp.where(some, total, 1.0)
                out_ref[0, :, span] = (acc_ref[:, span] / safe).astype(out_ref.dtype)
                logs.append(jnp.where(some, top_ref[head] + jnp.log(safe), NEG_FILL)[:, :1])
            log_ref[place_ref[step]] = lay_logs(logs, tree)


def page_attention(even, odd, k_pages, v_pages, plan, heads, size):
    half, tree, width = even.shape
    requests = 2 * half
    entries = k_pages.shape[2]
    low = lambda p, page, place, *rest: (jnp.minimum(place[p], half - 1), 0, 0)
    high = lambda p, page, place, *rest: (jnp.maximum(place[p] - half, 0), 0, 0)
    row = lambda at: pl.BlockSpec((1, tree, width), at)
    leaf = pl.BlockSpec(
        (1, heads, entries, size), lambda p, page, place, *rest: (page[p], 0, 0, 0)
    )
    grid_spec = pltpu.PrefetchScalarGridSpec(
        num_scalar_prefetch=6,
        grid=(k_pages.shape[0],),
        in_specs=[row(low), row(high), leaf, leaf],
        out_specs=[
            row(lambda p, page, place, *rest: (place[p], 0, 0)),
            pl.BlockSpec((requests, 8, LANES), lambda p, *rest: (0, 0, 0)),
        ],
        scratch_shapes=[
            pltpu.VMEM((tree, width), jnp.float32),
            pltpu.VMEM((heads, tree, size), jnp.float32),
            pltpu.VMEM((heads, tree, size), jnp.float32),
        ],
    )
    return pl.pallas_call(
        functools.partial(page_kernel, heads, size),
        grid_spec=grid_spec,
        out_shape=[
            jax.ShapeDtypeStruct((requests, tree, width), jnp.bfloat16),
            jax.ShapeDtypeStruct((requests, 8, LANES), jnp.float32),
        ],
        compiler_params=params(),
        name="page_attention",
    )(*plan, even, odd, k_pages, v_pages)


def owned_tile(index, rank, per, count):
    owner = lax.rem(rank - lax.div(index, per) + count, count)
    return owner * per + lax.rem(index, per)


def project_kernel(rank_ref, x_ref, w_ref, out_ref):
    out_ref[0] = jnp.dot(x_ref[...], w_ref[...], preferred_element_type=jnp.float32).astype(
        out_ref.dtype
    )


def project(values, weight, rank):
    count = lax.axis_size("head")
    rows, depth = values.shape
    columns = weight.shape[1] // count
    tile = min(columns, 256)
    per = columns // tile
    grid_spec = pltpu.PrefetchScalarGridSpec(
        num_scalar_prefetch=1,
        grid=(count * per,),
        in_specs=[
            pl.BlockSpec((rows, depth), lambda i, z: (0, 0)),
            pl.BlockSpec(
                (depth, tile), lambda i, z: (0, owned_tile(i, z[0], per, count))
            ),
        ],
        out_specs=pl.BlockSpec((1, rows, tile), lambda i, z: (lax.div(i, per), 0, lax.rem(i, per))),
    )
    return pl.pallas_call(
        project_kernel,
        grid_spec=grid_spec,
        out_shape=jax.ShapeDtypeStruct((count, rows, columns), jnp.bfloat16),
        compiler_params=params(),
        name="project",
    )(rank, values, weight)


def mlp_kernel(steps, tile, rank_ref, x_ref, gate_ref, up_ref, down_ref, out_ref, hidden_ref):
    step = pl.program_id(0)

    @pl.when(step < steps)
    def _():
        gate = jnp.dot(x_ref[...], gate_ref[...], preferred_element_type=jnp.float32)
        up = jnp.dot(x_ref[...], up_ref[...], preferred_element_type=jnp.float32)
        at = pl.ds(pl.multiple_of(step * tile, tile), tile)
        hidden_ref[:, at] = (jax.nn.silu(gate) * up).astype(hidden_ref.dtype)

    @pl.when(step >= steps)
    def _():
        out_ref[0] = jnp.dot(
            hidden_ref[...], down_ref[...], preferred_element_type=jnp.float32
        ).astype(out_ref.dtype)


def mlp(values, gate_up, down, rank):
    count = lax.axis_size("head")
    rows, width = values.shape
    hidden = down.shape[0]
    tile = min(hidden, 256)
    steps = hidden // tile
    columns = down.shape[1] // count
    out_tile = min(columns, 256)
    per = columns // out_tile
    late = lambda i: jnp.maximum(i - steps, 0)
    early = lambda i: jnp.minimum(i, steps - 1)
    grid_spec = pltpu.PrefetchScalarGridSpec(
        num_scalar_prefetch=1,
        grid=(steps + count * per,),
        in_specs=[
            pl.BlockSpec((rows, width), lambda i, z: (0, 0)),
            pl.BlockSpec((width, tile), lambda i, z: (0, early(i))),
            pl.BlockSpec((width, tile), lambda i, z: (0, steps + early(i))),
            pl.BlockSpec(
                (hidden, out_tile),
                lambda i, z: (0, owned_tile(late(i), z[0], per, count)),
            ),
        ],
        out_specs=pl.BlockSpec(
            (1, rows, out_tile), lambda i, z: (lax.div(late(i), per), 0, lax.rem(late(i), per))
        ),
        scratch_shapes=[pltpu.VMEM((rows, hidden), jnp.bfloat16)],
    )
    return pl.pallas_call(
        functools.partial(mlp_kernel, steps, tile),
        grid_spec=grid_spec,
        out_shape=jax.ShapeDtypeStruct((count, rows, columns), jnp.bfloat16),
        compiler_params=params(),
        name="mlp",
    )(rank, values, gate_up, gate_up, down)


def merge_kernel(heads, size, count, *refs):
    sums, logs, out_ref = refs[:count], refs[count : 2 * count], refs[2 * count]
    log_ref = refs[2 * count + 1] if len(refs) > 2 * count + 1 else None
    tree = out_ref.shape[1]
    for request in range(out_ref.shape[0]):
        tables = [ref[request] for ref in logs]
        top = functools.reduce(jnp.maximum, tables)
        total = functools.reduce(lambda a, b: a + b, [jnp.exp(table - top) for table in tables])
        merged = top + jnp.log(total)
        if log_ref is not None:
            log_ref[request] = merged
        shares = [
            jnp.transpose(jnp.where(table > EMPTY, jnp.exp(table - merged), 0.0))
            for table in tables
        ]
        for head in range(heads):
            at = slice(head * size, (head + 1) * size)
            value = jnp.zeros((tree, size), jnp.float32)
            for ref, share in zip(sums, shares):
                factor = share[:tree, head : head + 1]
                term = ref[request, :, at].astype(jnp.float32)
                value = value + jnp.where(factor > 0, term * factor, 0.0)
            out_ref[request, :, at] = value.astype(out_ref.dtype)


def merge_partials(pairs, heads, size, with_logs=True):
    requests, tree, width = pairs[0][0].shape
    group = max(size for size in (1, 2, 4, 8) if requests % size == 0)
    big = pl.BlockSpec((group, tree, width), lambda j: (j, 0, 0))
    small = pl.BlockSpec((group, 8, LANES), lambda j: (j, 0, 0))
    out_specs = [big, small] if with_logs else [big]
    out_shape = [
        jax.ShapeDtypeStruct((requests, tree, width), jnp.bfloat16),
        jax.ShapeDtypeStruct((requests, 8, LANES), jnp.float32),
    ][: len(out_specs)]
    return pl.pallas_call(
        functools.partial(merge_kernel, heads, size, len(pairs)),
        grid=(requests // group,),
        in_specs=[big] * len(pairs) + [small] * len(pairs),
        out_specs=out_specs,
        out_shape=out_shape,
        compiler_params=params(),
        name="merge_partials",
    )(*[pair[0] for pair in pairs], *[pair[1] for pair in pairs])


def page_plan(owner, fill, first_request, requests, all_local, count):
    slots = owner.shape[0]
    me = lax.axis_index("req")
    source = owner // all_local
    local = owner % all_local - first_request
    mine = (owner >= 0) & (local >= 0) & (local < requests)
    index = source ^ me
    index = (index & 1) * (count // 2) + (index >> 1)
    place = jnp.where(mine, index * requests + local, count * requests)
    spot = jnp.arange(slots, dtype=jnp.int32)
    ahead = (place[None, :] < place[:, None]) | (
        (place[None, :] == place[:, None]) & (spot[None, :] < spot[:, None])
    )
    rank = jnp.sum(ahead.astype(jnp.int32), axis=1)
    live = jnp.sum(mine.astype(jnp.int32))
    wanted = jnp.minimum(spot, jnp.maximum(live - 1, 0))
    chosen = rank[None, :] == wanted[:, None]
    take = lambda values: jnp.sum(jnp.where(chosen, values[None, :], 0), axis=1)
    pages, places, fills = take(spot), take(jnp.where(mine, place, 0)), take(fill)
    changed = (places[1:] != places[:-1]).astype(jnp.int32)
    one = jnp.ones((1,), jnp.int32)
    first = jnp.concatenate([one, changed])
    last = jnp.concatenate([changed, one])
    last = jnp.where(spot == live - 1, 1, last)
    return (pages, places, fills, first, last, live[None])


def on_device(
    streams,
    hc_in,
    hc_mix,
    hc_out,
    qkv_weight,
    out_weight,
    up_gate,
    down_weight,
    draft_weight,
    lm_head,
    k_pages,
    v_pages,
    page_owner,
    page_fill,
    cache_len,
    tree_parent,
    accepted_index,
):
    tokens_local = streams.shape[0]
    stream_count = streams.shape[1]
    feature_local = streams.shape[2]
    width = qkv_weight.shape[0]
    req_local = cache_len.shape[0]
    tree_size = tree_parent.shape[1]
    heads = k_pages.shape[2]
    size = k_pages.shape[3]
    draft_count = draft_weight.shape[0]
    parts = lax.axis_size("req")
    all_requests = req_local * parts

    identity = jnp.eye(stream_count, dtype=jnp.float32)
    first_mix, second_mix = identity + hc_mix[0], identity + hc_mix[1]
    mid_in = jnp.sum(first_mix * hc_in[1][None, :], axis=1)
    mid_out = jnp.sum(hc_out[0] * hc_in[1])
    both_mix = jnp.sum(first_mix[:, :, None] * second_mix[None, :, :], axis=1)
    both_out = jnp.sum(hc_out[0][:, None] * second_mix, axis=0)

    reach = ancestors(tree_parent)
    depth = (jnp.sum(reach, axis=2) - 1.0).astype(jnp.int32)
    positions = (cache_len[:, None] + depth).reshape(tokens_local)
    half = size // 2
    freqs = jnp.exp(jnp.arange(half, dtype=jnp.float32) * (-2.0 * math.log(10000.0) / size))
    angles = positions.astype(jnp.float32)[:, None] * freqs[None, :]
    cosine, sine = jnp.cos(angles), jnp.sin(angles)
    cosine = jnp.concatenate([cosine, cosine], axis=1)
    sine = jnp.concatenate([-sine, sine], axis=1)

    k_heads = jnp.transpose(k_pages, (0, 2, 1, 3))
    v_heads = jnp.transpose(v_pages, (0, 2, 1, 3))
    rank = lax.axis_index("head").astype(jnp.int32)[None]

    step_requests = req_local // CHUNKS
    step_tokens = step_requests * tree_size
    merge = lambda ours, got: merge_flat(ours, got, heads, size)

    token = None
    attended_in = []
    for chunk in range(CHUNKS):
        rows = slice(chunk * step_tokens, (chunk + 1) * step_tokens)
        stream_vals = streams[rows].astype(jnp.float32)
        mixed_in = blend(stream_vals, hc_in[0])
        if token is not None:
            mixed_in, token = lax.optimization_barrier((mixed_in, token))
        normed, token = gathered_norm(mixed_in, width)
        attended_in.append(normed)

    all_shape = (step_requests, tree_size, heads * size)
    gate_up = None
    before_pages = None
    attn_parts, mlp_parts = [], []
    for chunk in range(CHUNKS):
        rows = slice(chunk * step_tokens, (chunk + 1) * step_tokens)
        asked = slice(chunk * step_requests, (chunk + 1) * step_requests)
        normed = attended_in[chunk]
        projected = jnp.concatenate(
            [
                jnp.dot(normed, qkv_weight[:, third], preferred_element_type=jnp.float32)
                for third in range(3)
            ],
            axis=1,
        )
        if gate_up is None:
            projected, gate_up = lax.optimization_barrier((projected, up_gate))
            gate_up = gate_up.reshape(width, -1)
        queries, keys, values = rotate_all(
            projected, cosine[rows], sine[rows], heads, size, 2 * tree_size
        )
        queries, keys, values = (item.reshape(all_shape) for item in (queries, keys, values))
        even, odd = gather_requests(queries)
        plan = page_plan(
            page_owner, page_fill, chunk * step_requests, step_requests, req_local, parts
        )
        if before_pages is not None:
            even, odd, before_pages = lax.optimization_barrier((even, odd, before_pages))
        sums, logs = page_attention(even, odd, k_heads, v_heads, plan, heads, size)
        tree_pair = tree_attention(queries, keys, values, reach[asked], heads, size)
        done, before_pages = scatter_requests(
            sums.reshape((parts,) + all_shape),
            logs.reshape(parts, step_requests, 8, LANES),
            merge,
        )
        part_requests = step_requests // 2
        attended = []
        for part, (ours, got) in enumerate(done):
            own = slice(part * part_requests, (part + 1) * part_requests)
            pairs = [
                tuple(value.reshape((-1,) + value.shape[2:]) for value in pair)
                for pair in (ours, got)
            ] + [(tree_pair[0][own], tree_pair[1][own])]
            attended.append(merge_partials(pairs, heads, size, with_logs=False)[0])
        attended = jnp.concatenate(attended).reshape(step_tokens, heads * size)
        attn_delta = chain_scatter(project(attended, out_weight, rank))
        attn_parts.append(attn_delta)

        stream_vals = streams[rows].astype(jnp.float32)
        mixed_mid = blend(stream_vals, mid_in) + mid_out * attn_delta
        normed_mid, token = gathered_norm(mixed_mid, width)
        mlp_parts.append(chain_scatter(mlp(normed_mid, gate_up, down_weight, rank)))

    attn_delta = jnp.concatenate(attn_parts)
    mlp_delta = jnp.concatenate(mlp_parts)
    stream_vals = streams.astype(jnp.float32)
    new_streams = both_out[None, :, None] * attn_delta[:, None] + (
        hc_out[1][None, :, None] * mlp_delta[:, None]
    )
    for index in range(stream_count):
        new_streams = (
            new_streams + both_mix[index][None, :, None] * stream_vals[:, index : index + 1]
        )
    new_streams = new_streams.astype(jnp.bfloat16)

    rows_taken = jnp.arange(req_local, dtype=jnp.int32) * tree_size + accepted_index
    final_local = (
        jnp.sum(both_out) * attn_delta[rows_taken] + jnp.sum(hc_out[1]) * mlp_delta[rows_taken]
    ) + blend(stream_vals[rows_taken], jnp.sum(both_mix, axis=1))
    final_full = jnp.concatenate(list(shift_gather(final_local)), axis=1)
    final_norm = layer_norm(final_full)
    own_columns = lax.dynamic_slice_in_dim(
        final_norm, lax.axis_index("head") * feature_local, feature_local, 1
    )
    branch = jnp.einsum(
        "jd,kde->jke",
        final_norm.astype(jnp.bfloat16),
        draft_weight,
        preferred_element_type=jnp.float32,
    )
    drafted = (own_columns[:, None, :] + jax.nn.silu(branch)).astype(jnp.bfloat16)
    draft_all = lax.all_gather(drafted, ("req", "head"), axis=0, tiled=False)
    draft_all = draft_all.reshape((parts, -1) + drafted.shape).transpose(0, 2, 3, 1, 4)
    logits_local = jnp.dot(
        draft_all.reshape(-1, width), lm_head, preferred_element_type=jnp.float32
    )
    logits_local = logits_local.reshape(all_requests, draft_count, -1)
    logits = lax.all_to_all(
        logits_local.astype(jnp.bfloat16), ("req", "head"), split_axis=0, concat_axis=2, tiled=True
    ).astype(logits_local.dtype)
    return (new_streams, logits)


def merge_flat(ours, got, heads, size):
    lead = ours[0].shape[:2]
    pairs = [
        tuple(value.reshape((-1,) + value.shape[2:]) for value in pair) for pair in (ours, got)
    ]
    merged = merge_partials(pairs, heads, size)
    return [value.reshape(lead + value.shape[1:]) for value in merged]


def solution(mesh):
    in_specs = (
        P("req", None, "head"),
        P(),
        P(),
        P(),
        P(None, None, "head"),
        P("head", None),
        P(None, None, "head"),
        P("head", None),
        P(None, None, "head"),
        P(None, ("req", "head")),
        P("req", None, "head", None),
        P("req", None, "head", None),
        P("req"),
        P("req"),
        P("req"),
        P("req", None),
        P("req"),
    )
    out_specs = (P("req", None, "head"), P(("req", "head"), None, None))
    return jax.shard_map(
        on_device, mesh=mesh, in_specs=in_specs, out_specs=out_specs, check_vma=False
    )
```

```python
import functools
import math

import jax
import jax.numpy as jnp
from jax import lax
from jax.experimental import pallas as pl
from jax.experimental.pallas import tpu as pltpu
from jax.sharding import PartitionSpec as P

NEG_FILL = -1e30
EMPTY = -1e29
PRECISE = lax.Precision.HIGHEST
CHUNKS = 2
LANES = 128
VMEM_BYTES = 40 * 1024 * 1024


def params(count=1):
    return pltpu.CompilerParams(
        dimension_semantics=("arbitrary",) * count, vmem_limit_bytes=VMEM_BYTES
    )


def ancestors(parents):
    length = parents.shape[1]
    places = jnp.arange(length, dtype=jnp.int32)
    linked = (parents[:, :, None] == places[None, None, :]) | (places[:, None] == places[None, :])[
        None
    ]
    reach = linked.astype(jnp.float32)
    for repeat in range(max(1, (length - 1).bit_length())):
        reach = jnp.minimum(jnp.einsum("jik,jkl->jil", reach, reach, precision=PRECISE), 1.0)
    return reach


def layer_norm(values):
    center = jnp.mean(values, axis=-1, keepdims=True)
    square = jnp.mean(values * values, axis=-1, keepdims=True)
    return (values - center) * lax.rsqrt(square - center * center + 1e-05)


def blend(stream_vals, weights):
    total = weights[0] * stream_vals[:, 0]
    for index in range(1, stream_vals.shape[1]):
        total = total + weights[index] * stream_vals[:, index]
    return total


def shift_gather(small):
    count = lax.axis_size("head")
    rank = lax.axis_index("head")
    parts = [small] + [
        lax.ppermute(small, "head", [(z, (z + step) % count) for z in range(count)])
        for step in range(1, count)
    ]
    stacked = jnp.stack(parts)
    return jnp.stack(
        [
            lax.dynamic_index_in_dim(stacked, (rank - source) % count, 0, keepdims=False)
            for source in range(count)
        ]
    )


def gathered_norm(values, width, after=None):
    local = values.shape[1]
    sums = jnp.sum(values, axis=1)
    squares = jnp.sum(values * values, axis=1)
    center = sums / local
    sent = (values - center[:, None]).astype(jnp.bfloat16)
    stats = shift_gather(jnp.stack([sums, squares]))
    if after is not None:
        sent, after = lax.optimization_barrier((sent, after))
    gathered = lax.all_gather(sent, "head", axis=1, tiled=True)
    mean = jnp.sum(stats[:, 0], axis=0) / width
    variance = jnp.sum(stats[:, 1], axis=0) / width - mean * mean
    scale = lax.rsqrt(variance + 1e-05)
    normed = [
        (
            (
                gathered[:, rank * local : (rank + 1) * local].astype(jnp.float32)
                + (stats[rank, 0] / local - mean)[:, None]
            )
            * scale[:, None]
        ).astype(jnp.bfloat16)
        for rank in range(lax.axis_size("head"))
    ]
    return jnp.concatenate(normed, axis=1), gathered


def scatter_columns(shares):
    return lax.psum_scatter(shares, "head", scatter_dimension=1, tiled=True).astype(jnp.float32)


def swapped(values, bit):
    count = lax.axis_size("req")
    return lax.ppermute(values, "req", [(r, r ^ bit) for r in range(count)])


def bit_orders():
    bits = [1 << index for index in range((lax.axis_size("req") - 1).bit_length())]
    return bits[0], (bits[1:], bits[1:][::-1])


def gather_requests(values):
    half = values.shape[0] // 2
    near, orders = bit_orders()
    parts = []
    for part, order in enumerate(orders):
        blocks = {0: values[part * half : (part + 1) * half]}
        for bit in order:
            for index in list(blocks):
                blocks[index ^ bit] = swapped(blocks[index], bit)
        parts.append(blocks)
    even = jnp.concatenate([blocks[index] for index in sorted(parts[0]) for blocks in parts])
    return even, swapped(even, near)


def scatter_requests(sums, logs, merge):
    near, orders = bit_orders()
    count = lax.axis_size("req")
    far = count // 2
    state = []
    mine = [sums[:far], logs[:far]]
    theirs = [swapped(sums[far:], near), swapped(logs[far:], near)]
    merged = first_merged = merge(mine, theirs)
    half = sums.shape[1] // 2
    done = []
    for part, order in enumerate(orders):
        kept = [value[:, part * half : (part + 1) * half] for value in merged]
        places = list(range(far))
        for place, bit in enumerate(order):
            stay = [at for at, index in enumerate(places) if not index & (bit >> 1)]
            leave = [at for at, index in enumerate(places) if index & (bit >> 1)]
            pick = lambda value, which: jnp.concatenate([value[at : at + 1] for at in which])
            ours = [pick(value, stay) for value in kept]
            got = [swapped(pick(value, leave), bit) for value in kept]
            places = [places[at] for at in stay]
            kept = merge(ours, got) if place < len(order) - 1 else (ours, got)
        done.append(kept)
    return done, first_merged[1]


def rotate_kernel(heads, size, scale, x_ref, cos_ref, sin_ref, q_ref, k_ref, v_ref):
    width = heads * size
    cosine, sine = cos_ref[...], sin_ref[...]
    for head in range(heads):
        at = head * size
        for base, out_ref, factor in ((0, q_ref, scale), (width, k_ref, 1.0)):
            values = x_ref[:, base + at : base + at + size]
            turned = values * cosine + pltpu.roll(values, size // 2, 1) * sine
            out_ref[:, at : at + size] = (turned * factor).astype(out_ref.dtype)
    v_ref[...] = x_ref[:, 2 * width :].astype(v_ref.dtype)


def rotate_all(projected, cosine, sine, heads, size, rows):
    tokens = projected.shape[0]
    out = jax.ShapeDtypeStruct((tokens, heads * size), jnp.bfloat16)
    block = lambda width: pl.BlockSpec((rows, width), lambda i: (i, 0))
    return pl.pallas_call(
        functools.partial(rotate_kernel, heads, size, size ** (-0.5)),
        grid=(tokens // rows,),
        in_specs=[block(3 * heads * size), block(size), block(size)],
        out_specs=[block(heads * size)] * 3,
        out_shape=[out] * 3,
        compiler_params=params(),
        name="rotate",
    )(projected, cosine, sine)


def lay_logs(columns, rows):
    lane = lax.broadcasted_iota(jnp.int32, (LANES, LANES), 1)
    table = jnp.full((LANES, LANES), NEG_FILL, jnp.float32)
    for head, column in enumerate(columns):
        tall = jnp.concatenate(
            [column, jnp.full((LANES - rows, 1), NEG_FILL, jnp.float32)], axis=0
        )
        table = jnp.where(lane == head, tall, table)
    return jnp.transpose(table)[:8]


def tree_kernel(heads, size, q_ref, k_ref, v_ref, reach_ref, out_ref, log_ref):
    seen = reach_ref[0] > 0
    logs = []
    for head in range(heads):
        at = slice(head * size, (head + 1) * size)
        scores = lax.dot_general(
            q_ref[0, :, at],
            k_ref[0, :, at],
            (((1,), (1,)), ((), ())),
            preferred_element_type=jnp.float32,
        )
        scores = jnp.where(seen, scores, NEG_FILL)
        top = jnp.max(scores, axis=1, keepdims=True)
        weights = jnp.where(seen, jnp.exp(scores - top), 0.0)
        total = jnp.sum(weights, axis=1, keepdims=True)
        summed = jnp.dot(
            weights.astype(jnp.bfloat16), v_ref[0, :, at], preferred_element_type=jnp.float32
        )
        out_ref[0, :, at] = summed / total
        logs.append(top + jnp.log(total))
    log_ref[0] = lay_logs(logs, q_ref.shape[1])


def tree_attention(queries, keys, values, reach, heads, size):
    requests, tree, width = queries.shape
    block = pl.BlockSpec((1, tree, width), lambda j: (j, 0, 0))
    return pl.pallas_call(
        functools.partial(tree_kernel, heads, size),
        grid=(requests,),
        in_specs=[block] * 3 + [pl.BlockSpec((1, tree, tree), lambda j: (j, 0, 0))],
        out_specs=[block, pl.BlockSpec((1, 8, LANES), lambda j: (j, 0, 0))],
        out_shape=[
            jax.ShapeDtypeStruct((requests, tree, width), jnp.float32),
            jax.ShapeDtypeStruct((requests, 8, LANES), jnp.float32),
        ],
        compiler_params=params(),
        name="tree_attention",
    )(queries, keys, values, reach)


def page_kernel(
    heads,
    size,
    page_ref,
    place_ref,
    fill_ref,
    first_ref,
    last_ref,
    live_ref,
    even_ref,
    odd_ref,
    k_ref,
    v_ref,
    out_ref,
    log_ref,
    acc_ref,
    top_ref,
    total_ref,
):
    step = pl.program_id(0)
    tree = even_ref.shape[1]
    spans = [slice(head * size, (head + 1) * size) for head in range(heads)]

    @pl.when(step == 0)
    def _():
        log_ref[...] = jnp.full(log_ref.shape, NEG_FILL, jnp.float32)

    @pl.when(step < live_ref[0])
    def _():
        @pl.when(first_ref[step] == 1)
        def _():
            acc_ref[...] = jnp.zeros(acc_ref.shape, jnp.float32)
            top_ref[...] = jnp.full(top_ref.shape, NEG_FILL, jnp.float32)
            total_ref[...] = jnp.zeros(total_ref.shape, jnp.float32)

        entries = k_ref.shape[2]
        is_even = place_ref[step] < log_ref.shape[0] // 2
        asked = jnp.where(is_even, even_ref[0], odd_ref[0])
        valid = lax.broadcasted_iota(jnp.int32, (tree, entries), 1) < fill_ref[step]
        scores = [
            lax.dot_general(
                asked[:, span],
                k_ref[0, head],
                (((1,), (1,)), ((), ())),
                preferred_element_type=jnp.float32,
            )
            for head, span in enumerate(spans)
        ]
        scores = [jnp.where(valid, score, NEG_FILL) for score in scores]
        before = [top_ref[head] for head in range(heads)]
        tops = [
            jnp.maximum(old, jnp.max(score, axis=1, keepdims=True))
            for old, score in zip(before, scores)
        ]
        weights = [
            jnp.where(valid, jnp.exp(score - top), 0.0) for score, top in zip(scores, tops)
        ]
        decays = [jnp.exp(old - top) for old, top in zip(before, tops)]
        sums = [
            jnp.dot(
                weight.astype(jnp.bfloat16), v_ref[0, head], preferred_element_type=jnp.float32
            )
            for head, weight in enumerate(weights)
        ]
        totals = [
            total_ref[head] * decays[head] + jnp.sum(weights[head], axis=1, keepdims=True)
            for head in range(heads)
        ]
        news = [acc_ref[:, span] * decays[head] + sums[head] for head, span in enumerate(spans)]
        for head, span in enumerate(spans):
            top_ref[head] = tops[head]
            total_ref[head] = totals[head]
            acc_ref[:, span] = news[head]

        @pl.when(last_ref[step] == 1)
        def _():
            logs = []
            for head, span in enumerate(spans):
                total = total_ref[head]
                some = total > 0
                safe = jnp.where(some, total, 1.0)
                out_ref[0, :, span] = (acc_ref[:, span] / safe).astype(out_ref.dtype)
                logs.append(jnp.where(some, top_ref[head] + jnp.log(safe), NEG_FILL)[:, :1])
            log_ref[place_ref[step]] = lay_logs(logs, tree)


def page_attention(even, odd, k_pages, v_pages, plan, heads, size):
    half, tree, width = even.shape
    requests = 2 * half
    entries = k_pages.shape[2]
    low = lambda p, page, place, *rest: (jnp.minimum(place[p], half - 1), 0, 0)
    high = lambda p, page, place, *rest: (jnp.maximum(place[p] - half, 0), 0, 0)
    row = lambda at: pl.BlockSpec((1, tree, width), at)
    leaf = pl.BlockSpec(
        (1, heads, entries, size), lambda p, page, place, *rest: (page[p], 0, 0, 0)
    )
    grid_spec = pltpu.PrefetchScalarGridSpec(
        num_scalar_prefetch=6,
        grid=(k_pages.shape[0],),
        in_specs=[row(low), row(high), leaf, leaf],
        out_specs=[
            row(lambda p, page, place, *rest: (place[p], 0, 0)),
            pl.BlockSpec((requests, 8, LANES), lambda p, *rest: (0, 0, 0)),
        ],
        scratch_shapes=[
            pltpu.VMEM((tree, width), jnp.float32),
            pltpu.VMEM((heads, tree, size), jnp.float32),
            pltpu.VMEM((heads, tree, size), jnp.float32),
        ],
    )
    return pl.pallas_call(
        functools.partial(page_kernel, heads, size),
        grid_spec=grid_spec,
        out_shape=[
            jax.ShapeDtypeStruct((requests, tree, width), jnp.bfloat16),
            jax.ShapeDtypeStruct((requests, 8, LANES), jnp.float32),
        ],
        compiler_params=params(),
        name="page_attention",
    )(*plan, even, odd, k_pages, v_pages)


def project_kernel(x_ref, w_ref, out_ref):
    out_ref[...] = jnp.dot(x_ref[...], w_ref[...], preferred_element_type=jnp.float32).astype(
        out_ref.dtype
    )


def project(values, weight):
    rows, depth = values.shape
    columns = weight.shape[1]
    tile = min(columns, 512)
    return pl.pallas_call(
        project_kernel,
        grid=(columns // tile,),
        in_specs=[
            pl.BlockSpec((rows, depth), lambda i: (0, 0)),
            pl.BlockSpec((depth, tile), lambda i: (0, i)),
        ],
        out_specs=pl.BlockSpec((rows, tile), lambda i: (0, i)),
        out_shape=jax.ShapeDtypeStruct((rows, columns), jnp.bfloat16),
        compiler_params=params(),
        name="project",
    )(values, weight)


def mlp_kernel(steps, tile, x_ref, gate_ref, up_ref, down_ref, out_ref, hidden_ref):
    step = pl.program_id(0)

    @pl.when(step < steps)
    def _():
        gate = jnp.dot(x_ref[...], gate_ref[...], preferred_element_type=jnp.float32)
        up = jnp.dot(x_ref[...], up_ref[...], preferred_element_type=jnp.float32)
        at = pl.ds(pl.multiple_of(step * tile, tile), tile)
        hidden_ref[:, at] = (jax.nn.silu(gate) * up).astype(hidden_ref.dtype)

    @pl.when(step >= steps)
    def _():
        out_ref[...] = jnp.dot(
            hidden_ref[...], down_ref[...], preferred_element_type=jnp.float32
        ).astype(out_ref.dtype)


def mlp(values, gate_up, down):
    rows, width = values.shape
    hidden, columns = down.shape
    tile = min(hidden, 256)
    steps = hidden // tile
    out_tile = min(columns, 256)
    late = lambda i: jnp.maximum(i - steps, 0)
    early = lambda i: jnp.minimum(i, steps - 1)
    return pl.pallas_call(
        functools.partial(mlp_kernel, steps, tile),
        grid=(steps + columns // out_tile,),
        in_specs=[
            pl.BlockSpec((rows, width), lambda i: (0, 0)),
            pl.BlockSpec((width, tile), lambda i: (0, early(i))),
            pl.BlockSpec((width, tile), lambda i: (0, steps + early(i))),
            pl.BlockSpec((hidden, out_tile), lambda i: (0, late(i))),
        ],
        out_specs=pl.BlockSpec((rows, out_tile), lambda i: (0, late(i))),
        out_shape=jax.ShapeDtypeStruct((rows, columns), jnp.bfloat16),
        scratch_shapes=[pltpu.VMEM((rows, hidden), jnp.bfloat16)],
        compiler_params=params(),
        name="mlp",
    )(values, gate_up, gate_up, down)


def merge_kernel(heads, size, count, *refs):
    sums, logs, out_ref = refs[:count], refs[count : 2 * count], refs[2 * count]
    log_ref = refs[2 * count + 1] if len(refs) > 2 * count + 1 else None
    tree = out_ref.shape[1]
    for request in range(out_ref.shape[0]):
        tables = [ref[request] for ref in logs]
        top = functools.reduce(jnp.maximum, tables)
        total = functools.reduce(lambda a, b: a + b, [jnp.exp(table - top) for table in tables])
        merged = top + jnp.log(total)
        if log_ref is not None:
            log_ref[request] = merged
        shares = [
            jnp.transpose(jnp.where(table > EMPTY, jnp.exp(table - merged), 0.0))
            for table in tables
        ]
        for head in range(heads):
            at = slice(head * size, (head + 1) * size)
            value = jnp.zeros((tree, size), jnp.float32)
            for ref, share in zip(sums, shares):
                factor = share[:tree, head : head + 1]
                term = ref[request, :, at].astype(jnp.float32)
                value = value + jnp.where(factor > 0, term * factor, 0.0)
            out_ref[request, :, at] = value.astype(out_ref.dtype)


def merge_partials(pairs, heads, size, with_logs=True):
    requests, tree, width = pairs[0][0].shape
    group = max(size for size in (1, 2, 4, 8) if requests % size == 0)
    big = pl.BlockSpec((group, tree, width), lambda j: (j, 0, 0))
    small = pl.BlockSpec((group, 8, LANES), lambda j: (j, 0, 0))
    out_specs = [big, small] if with_logs else [big]
    out_shape = [
        jax.ShapeDtypeStruct((requests, tree, width), jnp.bfloat16),
        jax.ShapeDtypeStruct((requests, 8, LANES), jnp.float32),
    ][: len(out_specs)]
    return pl.pallas_call(
        functools.partial(merge_kernel, heads, size, len(pairs)),
        grid=(requests // group,),
        in_specs=[big] * len(pairs) + [small] * len(pairs),
        out_specs=out_specs,
        out_shape=out_shape,
        compiler_params=params(),
        name="merge_partials",
    )(*[pair[0] for pair in pairs], *[pair[1] for pair in pairs])


def page_plan(owner, fill, first_request, requests, all_local, count):
    slots = owner.shape[0]
    me = lax.axis_index("req")
    source = owner // all_local
    local = owner % all_local - first_request
    mine = (owner >= 0) & (local >= 0) & (local < requests)
    index = source ^ me
    index = (index & 1) * (count // 2) + (index >> 1)
    place = jnp.where(mine, index * requests + local, count * requests)
    spot = jnp.arange(slots, dtype=jnp.int32)
    ahead = (place[None, :] < place[:, None]) | (
        (place[None, :] == place[:, None]) & (spot[None, :] < spot[:, None])
    )
    rank = jnp.sum(ahead.astype(jnp.int32), axis=1)
    live = jnp.sum(mine.astype(jnp.int32))
    wanted = jnp.minimum(spot, jnp.maximum(live - 1, 0))
    chosen = rank[None, :] == wanted[:, None]
    take = lambda values: jnp.sum(jnp.where(chosen, values[None, :], 0), axis=1)
    pages, places, fills = take(spot), take(jnp.where(mine, place, 0)), take(fill)
    changed = (places[1:] != places[:-1]).astype(jnp.int32)
    one = jnp.ones((1,), jnp.int32)
    first = jnp.concatenate([one, changed])
    last = jnp.concatenate([changed, one])
    last = jnp.where(spot == live - 1, 1, last)
    return (pages, places, fills, first, last, live[None])


def on_device(
    streams,
    hc_in,
    hc_mix,
    hc_out,
    qkv_weight,
    out_weight,
    up_gate,
    down_weight,
    draft_weight,
    lm_head,
    k_pages,
    v_pages,
    page_owner,
    page_fill,
    cache_len,
    tree_parent,
    accepted_index,
):
    tokens_local = streams.shape[0]
    stream_count = streams.shape[1]
    feature_local = streams.shape[2]
    width = qkv_weight.shape[0]
    req_local = cache_len.shape[0]
    tree_size = tree_parent.shape[1]
    heads = k_pages.shape[2]
    size = k_pages.shape[3]
    draft_count = draft_weight.shape[0]
    parts = lax.axis_size("req")
    all_requests = req_local * parts

    identity = jnp.eye(stream_count, dtype=jnp.float32)
    first_mix, second_mix = identity + hc_mix[0], identity + hc_mix[1]
    mid_in = jnp.sum(first_mix * hc_in[1][None, :], axis=1)
    mid_out = jnp.sum(hc_out[0] * hc_in[1])
    both_mix = jnp.sum(first_mix[:, :, None] * second_mix[None, :, :], axis=1)
    both_out = jnp.sum(hc_out[0][:, None] * second_mix, axis=0)

    reach = ancestors(tree_parent)
    depth = (jnp.sum(reach, axis=2) - 1.0).astype(jnp.int32)
    positions = (cache_len[:, None] + depth).reshape(tokens_local)
    half = size // 2
    freqs = jnp.exp(jnp.arange(half, dtype=jnp.float32) * (-2.0 * math.log(10000.0) / size))
    angles = positions.astype(jnp.float32)[:, None] * freqs[None, :]
    cosine, sine = jnp.cos(angles), jnp.sin(angles)
    cosine = jnp.concatenate([cosine, cosine], axis=1)
    sine = jnp.concatenate([-sine, sine], axis=1)

    k_heads = jnp.transpose(k_pages, (0, 2, 1, 3))
    v_heads = jnp.transpose(v_pages, (0, 2, 1, 3))

    step_requests = req_local // CHUNKS
    step_tokens = step_requests * tree_size
    merge = lambda ours, got: merge_flat(ours, got, heads, size)

    token = None
    attended_in = []
    for chunk in range(CHUNKS):
        rows = slice(chunk * step_tokens, (chunk + 1) * step_tokens)
        stream_vals = streams[rows].astype(jnp.float32)
        mixed_in = blend(stream_vals, hc_in[0])
        normed, token = gathered_norm(mixed_in, width, token)
        attended_in.append(normed)

    all_shape = (step_requests, tree_size, heads * size)
    gate_up = None
    before_pages = None
    attn_parts, mlp_parts = [], []
    for chunk in range(CHUNKS):
        rows = slice(chunk * step_tokens, (chunk + 1) * step_tokens)
        asked = slice(chunk * step_requests, (chunk + 1) * step_requests)
        normed = attended_in[chunk]
        projected = jnp.concatenate(
            [
                jnp.dot(normed, qkv_weight[:, third], preferred_element_type=jnp.float32)
                for third in range(3)
            ],
            axis=1,
        )
        if gate_up is None:
            projected, gate_up = lax.optimization_barrier((projected, up_gate))
            gate_up = gate_up.reshape(width, -1)
        queries, keys, values = rotate_all(
            projected, cosine[rows], sine[rows], heads, size, 2 * tree_size
        )
        queries, keys, values = (item.reshape(all_shape) for item in (queries, keys, values))
        even, odd = gather_requests(queries)
        plan = page_plan(
            page_owner, page_fill, chunk * step_requests, step_requests, req_local, parts
        )
        if before_pages is not None:
            even, odd, before_pages = lax.optimization_barrier((even, odd, before_pages))
        sums, logs = page_attention(even, odd, k_heads, v_heads, plan, heads, size)
        tree_pair = tree_attention(queries, keys, values, reach[asked], heads, size)
        done, before_pages = scatter_requests(
            sums.reshape((parts,) + all_shape),
            logs.reshape(parts, step_requests, 8, LANES),
            merge,
        )
        part_requests = step_requests // 2
        attended = []
        for part, (ours, got) in enumerate(done):
            own = slice(part * part_requests, (part + 1) * part_requests)
            pairs = [
                tuple(value.reshape((-1,) + value.shape[2:]) for value in pair)
                for pair in (ours, got)
            ] + [(tree_pair[0][own], tree_pair[1][own])]
            attended.append(merge_partials(pairs, heads, size, with_logs=False)[0])
        attended = jnp.concatenate(attended).reshape(step_tokens, heads * size)
        attn_delta = scatter_columns(project(attended, out_weight))
        attn_parts.append(attn_delta)

        stream_vals = streams[rows].astype(jnp.float32)
        mixed_mid = blend(stream_vals, mid_in) + mid_out * attn_delta
        normed_mid = gathered_norm(mixed_mid, width)[0]
        mlp_parts.append(scatter_columns(mlp(normed_mid, gate_up, down_weight)))

    attn_delta = jnp.concatenate(attn_parts)
    mlp_delta = jnp.concatenate(mlp_parts)
    stream_vals = streams.astype(jnp.float32)
    new_streams = both_out[None, :, None] * attn_delta[:, None] + (
        hc_out[1][None, :, None] * mlp_delta[:, None]
    )
    for index in range(stream_count):
        new_streams = (
            new_streams + both_mix[index][None, :, None] * stream_vals[:, index : index + 1]
        )
    new_streams = new_streams.astype(jnp.bfloat16)

    rows_taken = jnp.arange(req_local, dtype=jnp.int32) * tree_size + accepted_index
    final_local = (
        jnp.sum(both_out) * attn_delta[rows_taken] + jnp.sum(hc_out[1]) * mlp_delta[rows_taken]
    ) + blend(stream_vals[rows_taken], jnp.sum(both_mix, axis=1))
    final_full = jnp.concatenate(list(shift_gather(final_local)), axis=1)
    final_norm = layer_norm(final_full)
    own_columns = lax.dynamic_slice_in_dim(
        final_norm, lax.axis_index("head") * feature_local, feature_local, 1
    )
    branch = jnp.einsum(
        "jd,kde->jke",
        final_norm.astype(jnp.bfloat16),
        draft_weight,
        preferred_element_type=jnp.float32,
    )
    drafted = (own_columns[:, None, :] + jax.nn.silu(branch)).astype(jnp.bfloat16)
    draft_full = jnp.concatenate(list(shift_gather(drafted)), axis=2)
    draft_all = lax.all_gather(draft_full, "req", axis=0, tiled=True)
    logits_local = jnp.dot(
        draft_all.reshape(-1, width), lm_head, preferred_element_type=jnp.float32
    )
    logits_local = logits_local.reshape(all_requests, draft_count, -1)
    logits = lax.all_to_all(
        logits_local.astype(jnp.bfloat16), ("req", "head"), split_axis=0, concat_axis=2, tiled=True
    ).astype(logits_local.dtype)
    return (new_streams, logits)


def merge_flat(ours, got, heads, size):
    lead = ours[0].shape[:2]
    pairs = [
        tuple(value.reshape((-1,) + value.shape[2:]) for value in pair) for pair in (ours, got)
    ]
    merged = merge_partials(pairs, heads, size)
    return [value.reshape(lead + value.shape[1:]) for value in merged]


def solution(mesh):
    in_specs = (
        P("req", None, "head"),
        P(),
        P(),
        P(),
        P(None, None, "head"),
        P("head", None),
        P(None, None, "head"),
        P("head", None),
        P(None, None, "head"),
        P(None, ("req", "head")),
        P("req", None, "head", None),
        P("req", None, "head", None),
        P("req"),
        P("req"),
        P("req"),
        P("req", None),
        P("req"),
    )
    out_specs = (P("req", None, "head"), P(("req", "head"), None, None))
    return jax.shard_map(
        on_device, mesh=mesh, in_specs=in_specs, out_specs=out_specs, check_vma=False
    )
```

```python
import functools
import math

import jax
import jax.numpy as jnp
from jax import lax
from jax.experimental import pallas as pl
from jax.experimental.pallas import tpu as pltpu
from jax.sharding import PartitionSpec as P

NEG_FILL = -1e30
EMPTY = -1e29
PRECISE = lax.Precision.HIGHEST
CHUNKS = 2
LANES = 128
PAGES_A_STEP = 2
VMEM_BYTES = 40 * 1024 * 1024


def params(count=1):
    return pltpu.CompilerParams(
        dimension_semantics=("arbitrary",) * count, vmem_limit_bytes=VMEM_BYTES
    )


def ancestors(parents):
    length = parents.shape[1]
    places = jnp.arange(length, dtype=jnp.int32)
    linked = (parents[:, :, None] == places[None, None, :]) | (places[:, None] == places[None, :])[
        None
    ]
    reach = linked.astype(jnp.float32)
    for repeat in range(max(1, (length - 1).bit_length())):
        reach = jnp.minimum(jnp.einsum("jik,jkl->jil", reach, reach, precision=PRECISE), 1.0)
    return reach


def layer_norm(values):
    center = jnp.mean(values, axis=-1, keepdims=True)
    square = jnp.mean(values * values, axis=-1, keepdims=True)
    return (values - center) * lax.rsqrt(square - center * center + 1e-05)


def blend(stream_vals, weights):
    total = weights[0] * stream_vals[:, 0]
    for index in range(1, stream_vals.shape[1]):
        total = total + weights[index] * stream_vals[:, index]
    return total


def shift_gather(small):
    count = lax.axis_size("head")
    rank = lax.axis_index("head")
    parts = [small] + [
        lax.ppermute(small, "head", [(z, (z + step) % count) for z in range(count)])
        for step in range(1, count)
    ]
    stacked = jnp.stack(parts)
    return jnp.stack(
        [
            lax.dynamic_index_in_dim(stacked, (rank - source) % count, 0, keepdims=False)
            for source in range(count)
        ]
    )


def shift_scatter(shares):
    count = lax.axis_size("head")
    rank = lax.axis_index("head")
    width = shares.shape[1] // count
    total = None
    for step in range(count):
        block = lax.dynamic_slice_in_dim(shares, (rank + step) % count * width, width, 1)
        if step:
            block = lax.ppermute(block, "head", [(z, (z + step) % count) for z in range(count)])
        block = block.astype(jnp.float32)
        total = block if total is None else total + block
    return total


def gathered_norm(values, width, after=None):
    local = values.shape[1]
    sums = jnp.sum(values, axis=1)
    squares = jnp.sum(values * values, axis=1)
    center = sums / local
    sent = (values - center[:, None]).astype(jnp.bfloat16)
    stats = shift_gather(jnp.stack([sums, squares]))
    if after is not None:
        sent, after = lax.optimization_barrier((sent, after))
    gathered = lax.all_gather(sent, "head", axis=1, tiled=True)
    mean = jnp.sum(stats[:, 0], axis=0) / width
    variance = jnp.sum(stats[:, 1], axis=0) / width - mean * mean
    scale = lax.rsqrt(variance + 1e-05)
    normed = [
        (
            (
                gathered[:, rank * local : (rank + 1) * local].astype(jnp.float32)
                + (stats[rank, 0] / local - mean)[:, None]
            )
            * scale[:, None]
        ).astype(jnp.bfloat16)
        for rank in range(lax.axis_size("head"))
    ]
    return jnp.concatenate(normed, axis=1), gathered, sent


def scatter_columns(shares):
    return lax.psum_scatter(shares, "head", scatter_dimension=1, tiled=True).astype(jnp.float32)


def swapped(values, bit):
    count = lax.axis_size("req")
    return lax.ppermute(values, "req", [(r, r ^ bit) for r in range(count)])


def bit_orders():
    bits = [1 << index for index in range((lax.axis_size("req") - 1).bit_length())]
    return bits[0], (bits[1:], bits[1:][::-1])


def gather_requests(values):
    half = values.shape[0] // 2
    near, orders = bit_orders()
    parts = []
    for part, order in enumerate(orders):
        blocks = {0: values[part * half : (part + 1) * half]}
        for bit in order:
            for index in list(blocks):
                blocks[index ^ bit] = swapped(blocks[index], bit)
        parts.append(blocks)
    even = jnp.concatenate([blocks[index] for index in sorted(parts[0]) for blocks in parts])
    return even, swapped(even, near)


def gather_small(values):
    count = lax.axis_size("req")
    near, orders = bit_orders()
    stacked = values[None]
    bits = []
    for bit in list(orders[0]) + [near]:
        stacked = jnp.concatenate([stacked, swapped(stacked, bit)])
        bits.append(bit)
    index = lax.axis_index("req") ^ jnp.arange(count, dtype=jnp.int32)
    place = jnp.zeros_like(index)
    for spot, bit in enumerate(bits):
        place = place + jnp.where((index & bit) != 0, 1 << spot, 0)
    return stacked[place]


def scatter_requests(sums, logs, merge):
    near, orders = bit_orders()
    count = lax.axis_size("req")
    far = count // 2
    state = []
    mine = [sums[:far], logs[:far]]
    theirs = [swapped(sums[far:], near), swapped(logs[far:], near)]
    merged = merge(mine, theirs)
    half = sums.shape[1] // 2
    done = []
    for part, order in enumerate(orders):
        kept = [value[:, part * half : (part + 1) * half] for value in merged]
        places = list(range(far))
        for place, bit in enumerate(order):
            stay = [at for at, index in enumerate(places) if not index & (bit >> 1)]
            leave = [at for at, index in enumerate(places) if index & (bit >> 1)]
            pick = lambda value, which: jnp.concatenate([value[at : at + 1] for at in which])
            ours = [pick(value, stay) for value in kept]
            got = [swapped(pick(value, leave), bit) for value in kept]
            places = [places[at] for at in stay]
            kept = merge(ours, got) if place < len(order) - 1 else (ours, got)
        done.append(kept)
    return done


def rotate_kernel(heads, size, scale, x_ref, cos_ref, sin_ref, q_ref, k_ref, v_ref):
    width = heads * size
    cosine, sine = cos_ref[...], sin_ref[...]
    for head in range(heads):
        at = head * size
        for base, out_ref, factor in ((0, q_ref, scale), (width, k_ref, 1.0)):
            values = x_ref[:, base + at : base + at + size]
            turned = values * cosine + pltpu.roll(values, size // 2, 1) * sine
            out_ref[:, at : at + size] = (turned * factor).astype(out_ref.dtype)
    v_ref[...] = x_ref[:, 2 * width :].astype(v_ref.dtype)


def rotate_all(projected, cosine, sine, heads, size, rows):
    tokens = projected.shape[0]
    out = jax.ShapeDtypeStruct((tokens, heads * size), jnp.bfloat16)
    block = lambda width: pl.BlockSpec((rows, width), lambda i: (i, 0))
    return pl.pallas_call(
        functools.partial(rotate_kernel, heads, size, size ** (-0.5)),
        grid=(tokens // rows,),
        in_specs=[block(3 * heads * size), block(size), block(size)],
        out_specs=[block(heads * size)] * 3,
        out_shape=[out] * 3,
        compiler_params=params(),
        name="rotate",
    )(projected, cosine, sine)


def lay_logs(columns, rows):
    lane = lax.broadcasted_iota(jnp.int32, (LANES, LANES), 1)
    table = jnp.full((LANES, LANES), NEG_FILL, jnp.float32)
    for head, column in enumerate(columns):
        tall = jnp.concatenate(
            [column, jnp.full((LANES - rows, 1), NEG_FILL, jnp.float32)], axis=0
        )
        table = jnp.where(lane == head, tall, table)
    return jnp.transpose(table)[:8]


def tree_kernel(heads, size, q_ref, k_ref, v_ref, reach_ref, out_ref, log_ref):
    seen = reach_ref[0] > 0
    logs = []
    for head in range(heads):
        at = slice(head * size, (head + 1) * size)
        scores = lax.dot_general(
            q_ref[0, :, at],
            k_ref[0, :, at],
            (((1,), (1,)), ((), ())),
            preferred_element_type=jnp.float32,
        )
        scores = jnp.where(seen, scores, NEG_FILL)
        top = jnp.max(scores, axis=1, keepdims=True)
        weights = jnp.where(seen, jnp.exp(scores - top), 0.0)
        total = jnp.sum(weights, axis=1, keepdims=True)
        summed = jnp.dot(
            weights.astype(jnp.bfloat16), v_ref[0, :, at], preferred_element_type=jnp.float32
        )
        out_ref[0, :, at] = summed / total
        logs.append(top + jnp.log(total))
    log_ref[0] = lay_logs(logs, q_ref.shape[1])


def tree_attention(queries, keys, values, reach, heads, size):
    requests, tree, width = queries.shape
    block = pl.BlockSpec((1, tree, width), lambda j: (j, 0, 0))
    return pl.pallas_call(
        functools.partial(tree_kernel, heads, size),
        grid=(requests,),
        in_specs=[block] * 3 + [pl.BlockSpec((1, tree, tree), lambda j: (j, 0, 0))],
        out_specs=[block, pl.BlockSpec((1, 8, LANES), lambda j: (j, 0, 0))],
        out_shape=[
            jax.ShapeDtypeStruct((requests, tree, width), jnp.float32),
            jax.ShapeDtypeStruct((requests, 8, LANES), jnp.float32),
        ],
        compiler_params=params(),
        name="tree_attention",
    )(queries, keys, values, reach)


def page_kernel(
    heads,
    size,
    page_ref,
    place_ref,
    fill_ref,
    first_ref,
    last_ref,
    live_ref,
    even_ref,
    odd_ref,
    *refs,
):
    leaves = refs[: 2 * PAGES_A_STEP]
    out_ref, log_ref, acc_ref, top_ref, total_ref = refs[2 * PAGES_A_STEP :]
    step = pl.program_id(0)
    half, tree = even_ref.shape[:2]
    spans = [slice(head * size, (head + 1) * size) for head in range(heads)]
    entries = leaves[0].shape[2]

    @pl.when(step == 0)
    def _():
        log_ref[...] = jnp.full(log_ref.shape, NEG_FILL, jnp.float32)

    @pl.when(step * PAGES_A_STEP < live_ref[0])
    def _():
        column = lax.broadcasted_iota(jnp.int32, (tree, entries), 1)
        units = [(part, head) for part in range(PAGES_A_STEP) for head in range(heads)]
        asked, valid = [], []
        for part in range(PAGES_A_STEP):
            visit = step * PAGES_A_STEP + part
            place = place_ref[visit]
            asked.append(
                jnp.where(
                    place < half,
                    even_ref[jnp.minimum(place, half - 1)],
                    odd_ref[jnp.maximum(place - half, 0)],
                )
            )
            valid.append(column < fill_ref[visit])
        scores = [
            lax.dot_general(
                asked[part][:, spans[head]],
                leaves[2 * part][0, head],
                (((1,), (1,)), ((), ())),
                preferred_element_type=jnp.float32,
            )
            for part, head in units
        ]
        scores = [
            jnp.where(valid[part], score, NEG_FILL) for (part, head), score in zip(units, scores)
        ]
        tops = [jnp.max(score, axis=1, keepdims=True) for score in scores]
        weights = [
            jnp.where(valid[part], jnp.exp(score - top), 0.0)
            for (part, head), score, top in zip(units, scores, tops)
        ]
        totals = [jnp.sum(weight, axis=1, keepdims=True) for weight in weights]
        sums = [
            jnp.dot(
                weight.astype(jnp.bfloat16),
                leaves[2 * part + 1][0, head],
                preferred_element_type=jnp.float32,
            )
            for (part, head), weight in zip(units, weights)
        ]
        for part in range(PAGES_A_STEP):
            visit = step * PAGES_A_STEP + part
            merge_page(
                visit,
                spans,
                tops[part * heads : (part + 1) * heads],
                totals[part * heads : (part + 1) * heads],
                sums[part * heads : (part + 1) * heads],
                place_ref,
                first_ref,
                last_ref,
                live_ref,
                out_ref,
                log_ref,
                acc_ref,
                top_ref,
                total_ref,
            )


def merge_page(
    visit,
    spans,
    tops,
    totals,
    sums,
    place_ref,
    first_ref,
    last_ref,
    live_ref,
    out_ref,
    log_ref,
    acc_ref,
    top_ref,
    total_ref,
):
    tree = acc_ref.shape[0]
    live = visit < live_ref[0]
    alone = (first_ref[visit] == 1) & (last_ref[visit] == 1)

    def write(tops, totals, sums):
        logs = []
        for span, top, total, value in zip(spans, tops, totals, sums):
            some = total > 0
            safe = jnp.where(some, total, 1.0)
            out_ref[place_ref[visit], :, span] = (value / safe).astype(out_ref.dtype)
            logs.append(jnp.where(some, top + jnp.log(safe), NEG_FILL)[:, :1])
        log_ref[place_ref[visit]] = lay_logs(logs, tree)

    @pl.when(live & alone)
    def _():
        write(tops, totals, sums)

    @pl.when(live & jnp.logical_not(alone))
    def _():
        @pl.when(first_ref[visit] == 1)
        def _():
            acc_ref[...] = jnp.zeros(acc_ref.shape, jnp.float32)
            top_ref[...] = jnp.full(top_ref.shape, NEG_FILL, jnp.float32)
            total_ref[...] = jnp.zeros(total_ref.shape, jnp.float32)

        for head, span in enumerate(spans):
            before = top_ref[head]
            top = jnp.maximum(before, tops[head])
            decay, gain = jnp.exp(before - top), jnp.exp(tops[head] - top)
            top_ref[head] = top
            total_ref[head] = total_ref[head] * decay + totals[head] * gain
            acc_ref[:, span] = acc_ref[:, span] * decay + sums[head] * gain

        @pl.when(last_ref[visit] == 1)
        def _():
            heads = range(len(spans))
            write(
                [top_ref[head] for head in heads],
                [total_ref[head] for head in heads],
                [acc_ref[:, span] for span in spans],
            )


def page_attention(even, odd, k_pages, v_pages, plan, heads, size):
    half, tree, width = even.shape
    requests = 2 * half
    slots, entries = k_pages.shape[0], k_pages.shape[2]
    whole = lambda shape: pl.BlockSpec(shape, lambda p, *rest: (0, 0, 0))

    def leaf(part):
        return pl.BlockSpec(
            (1, heads, entries, size),
            lambda p, page, *rest: (page[p * PAGES_A_STEP + part], 0, 0, 0),
        )

    grid_spec = pltpu.PrefetchScalarGridSpec(
        num_scalar_prefetch=6,
        grid=(slots // PAGES_A_STEP,),
        in_specs=[whole(even.shape), whole(odd.shape)]
        + [leaf(part) for part in range(PAGES_A_STEP) for _ in range(2)],
        out_specs=[whole((requests, tree, width)), whole((requests, 8, LANES))],
        scratch_shapes=[
            pltpu.VMEM((tree, width), jnp.float32),
            pltpu.VMEM((heads, tree, size), jnp.float32),
            pltpu.VMEM((heads, tree, size), jnp.float32),
        ],
    )
    return pl.pallas_call(
        functools.partial(page_kernel, heads, size),
        grid_spec=grid_spec,
        out_shape=[
            jax.ShapeDtypeStruct((requests, tree, width), jnp.bfloat16),
            jax.ShapeDtypeStruct((requests, 8, LANES), jnp.float32),
        ],
        compiler_params=params(),
        name="page_attention",
    )(*plan, even, odd, *([k_pages, v_pages] * PAGES_A_STEP))


def project_kernel(x_ref, w_ref, out_ref):
    out_ref[...] = jnp.dot(x_ref[...], w_ref[...], preferred_element_type=jnp.float32).astype(
        out_ref.dtype
    )


def project(values, weight):
    rows, depth = values.shape
    columns = weight.shape[1]
    tile = min(columns, 512)
    return pl.pallas_call(
        project_kernel,
        grid=(columns // tile,),
        in_specs=[
            pl.BlockSpec((rows, depth), lambda i: (0, 0)),
            pl.BlockSpec((depth, tile), lambda i: (0, i)),
        ],
        out_specs=pl.BlockSpec((rows, tile), lambda i: (0, i)),
        out_shape=jax.ShapeDtypeStruct((rows, columns), jnp.bfloat16),
        compiler_params=params(),
        name="project",
    )(values, weight)


def mlp_kernel(steps, tile, x_ref, gate_ref, up_ref, down_ref, out_ref, hidden_ref):
    step = pl.program_id(0)

    @pl.when(step < steps)
    def _():
        gate = jnp.dot(x_ref[...], gate_ref[...], preferred_element_type=jnp.float32)
        up = jnp.dot(x_ref[...], up_ref[...], preferred_element_type=jnp.float32)
        at = pl.ds(pl.multiple_of(step * tile, tile), tile)
        hidden_ref[:, at] = (jax.nn.silu(gate) * up).astype(hidden_ref.dtype)

    @pl.when(step >= steps)
    def _():
        out_ref[...] = jnp.dot(
            hidden_ref[...], down_ref[...], preferred_element_type=jnp.float32
        ).astype(out_ref.dtype)


def mlp(values, gate_up, down):
    rows, width = values.shape
    hidden, columns = down.shape
    tile = min(hidden, 256)
    steps = hidden // tile
    out_tile = min(columns, 256)
    late = lambda i: jnp.maximum(i - steps, 0)
    early = lambda i: jnp.minimum(i, steps - 1)
    return pl.pallas_call(
        functools.partial(mlp_kernel, steps, tile),
        grid=(steps + columns // out_tile,),
        in_specs=[
            pl.BlockSpec((rows, width), lambda i: (0, 0)),
            pl.BlockSpec((width, tile), lambda i: (0, early(i))),
            pl.BlockSpec((width, tile), lambda i: (0, steps + early(i))),
            pl.BlockSpec((hidden, out_tile), lambda i: (0, late(i))),
        ],
        out_specs=pl.BlockSpec((rows, out_tile), lambda i: (0, late(i))),
        out_shape=jax.ShapeDtypeStruct((rows, columns), jnp.bfloat16),
        scratch_shapes=[pltpu.VMEM((rows, hidden), jnp.bfloat16)],
        compiler_params=params(),
        name="mlp",
    )(values, gate_up, gate_up, down)


def merge_kernel(heads, size, count, *refs):
    sums, logs, out_ref = refs[:count], refs[count : 2 * count], refs[2 * count]
    log_ref = refs[2 * count + 1] if len(refs) > 2 * count + 1 else None
    tree = out_ref.shape[1]
    for request in range(out_ref.shape[0]):
        tables = [ref[request] for ref in logs]
        top = functools.reduce(jnp.maximum, tables)
        total = functools.reduce(lambda a, b: a + b, [jnp.exp(table - top) for table in tables])
        merged = top + jnp.log(total)
        if log_ref is not None:
            log_ref[request] = merged
        shares = [
            jnp.transpose(jnp.where(table > EMPTY, jnp.exp(table - merged), 0.0))
            for table in tables
        ]
        for head in range(heads):
            at = slice(head * size, (head + 1) * size)
            value = jnp.zeros((tree, size), jnp.float32)
            for ref, share in zip(sums, shares):
                factor = share[:tree, head : head + 1]
                term = ref[request, :, at].astype(jnp.float32)
                value = value + jnp.where(factor > 0, term * factor, 0.0)
            out_ref[request, :, at] = value.astype(out_ref.dtype)


def merge_partials(pairs, heads, size, with_logs=True):
    requests, tree, width = pairs[0][0].shape
    group = max(size for size in (1, 2, 4, 8) if requests % size == 0)
    big = pl.BlockSpec((group, tree, width), lambda j: (j, 0, 0))
    small = pl.BlockSpec((group, 8, LANES), lambda j: (j, 0, 0))
    out_specs = [big, small] if with_logs else [big]
    out_shape = [
        jax.ShapeDtypeStruct((requests, tree, width), jnp.bfloat16),
        jax.ShapeDtypeStruct((requests, 8, LANES), jnp.float32),
    ][: len(out_specs)]
    return pl.pallas_call(
        functools.partial(merge_kernel, heads, size, len(pairs)),
        grid=(requests // group,),
        in_specs=[big] * len(pairs) + [small] * len(pairs),
        out_specs=out_specs,
        out_shape=out_shape,
        compiler_params=params(),
        name="merge_partials",
    )(*[pair[0] for pair in pairs], *[pair[1] for pair in pairs])


def page_plan(owner, fill, first_request, requests, all_local, count):
    slots = owner.shape[0]
    me = lax.axis_index("req")
    source = owner // all_local
    local = owner % all_local - first_request
    mine = (owner >= 0) & (local >= 0) & (local < requests)
    index = source ^ me
    index = (index & 1) * (count // 2) + (index >> 1)
    place = jnp.where(mine, index * requests + local, count * requests)
    spot = jnp.arange(slots, dtype=jnp.int32)
    ahead = (place[None, :] < place[:, None]) | (
        (place[None, :] == place[:, None]) & (spot[None, :] < spot[:, None])
    )
    rank = jnp.sum(ahead.astype(jnp.int32), axis=1)
    live = jnp.sum(mine.astype(jnp.int32))
    wanted = jnp.minimum(spot, jnp.maximum(live - 1, 0))
    chosen = rank[None, :] == wanted[:, None]
    take = lambda values: jnp.sum(jnp.where(chosen, values[None, :], 0), axis=1)
    pages, places, fills = take(spot), take(jnp.where(mine, place, 0)), take(fill)
    changed = (places[1:] != places[:-1]).astype(jnp.int32)
    one = jnp.ones((1,), jnp.int32)
    first = jnp.concatenate([one, changed])
    last = jnp.concatenate([changed, one])
    last = jnp.where(spot == live - 1, 1, last)
    return (pages, places, fills, first, last, live[None])


def on_device(
    streams,
    hc_in,
    hc_mix,
    hc_out,
    qkv_weight,
    out_weight,
    up_gate,
    down_weight,
    draft_weight,
    lm_head,
    k_pages,
    v_pages,
    page_owner,
    page_fill,
    cache_len,
    tree_parent,
    accepted_index,
):
    tokens_local = streams.shape[0]
    stream_count = streams.shape[1]
    feature_local = streams.shape[2]
    width = qkv_weight.shape[0]
    req_local = cache_len.shape[0]
    tree_size = tree_parent.shape[1]
    heads = k_pages.shape[2]
    size = k_pages.shape[3]
    draft_count = draft_weight.shape[0]
    parts = lax.axis_size("req")
    all_requests = req_local * parts

    identity = jnp.eye(stream_count, dtype=jnp.float32)
    first_mix, second_mix = identity + hc_mix[0], identity + hc_mix[1]
    mid_in = jnp.sum(first_mix * hc_in[1][None, :], axis=1)
    mid_out = jnp.sum(hc_out[0] * hc_in[1])
    both_mix = jnp.sum(first_mix[:, :, None] * second_mix[None, :, :], axis=1)
    both_out = jnp.sum(hc_out[0][:, None] * second_mix, axis=0)

    reach = ancestors(tree_parent)
    depth = (jnp.sum(reach, axis=2) - 1.0).astype(jnp.int32)
    positions = (cache_len[:, None] + depth).reshape(tokens_local)
    half = size // 2
    freqs = jnp.exp(jnp.arange(half, dtype=jnp.float32) * (-2.0 * math.log(10000.0) / size))
    angles = positions.astype(jnp.float32)[:, None] * freqs[None, :]
    cosine, sine = jnp.cos(angles), jnp.sin(angles)
    cosine = jnp.concatenate([cosine, cosine], axis=1)
    sine = jnp.concatenate([-sine, sine], axis=1)

    k_heads = jnp.transpose(k_pages, (0, 2, 1, 3))
    v_heads = jnp.transpose(v_pages, (0, 2, 1, 3))

    step_requests = req_local // CHUNKS
    step_tokens = step_requests * tree_size
    merge = lambda ours, got: merge_flat(ours, got, heads, size)

    gate_up = up_gate.reshape(width, -1)
    token = None
    sent_mid = None
    attended_in = []
    for chunk in range(CHUNKS):
        rows = slice(chunk * step_tokens, (chunk + 1) * step_tokens)
        stream_vals = streams[rows].astype(jnp.float32)
        mixed_in = blend(stream_vals, hc_in[0])
        normed, token, sent = gathered_norm(mixed_in, width, token)
        if chunk == 0:
            normed, k_heads, v_heads, gate_up = lax.optimization_barrier(
                (normed, k_heads, v_heads, gate_up)
            )
        attended_in.append(normed)

    all_shape = (step_requests, tree_size, heads * size)
    before_queries = None
    attn_parts, mlp_parts = [], []
    for chunk in range(CHUNKS):
        rows = slice(chunk * step_tokens, (chunk + 1) * step_tokens)
        asked = slice(chunk * step_requests, (chunk + 1) * step_requests)
        normed = attended_in[chunk]
        projected = jnp.concatenate(
            [
                jnp.dot(normed, qkv_weight[:, third], preferred_element_type=jnp.float32)
                for third in range(3)
            ],
            axis=1,
        )
        queries, keys, values = rotate_all(
            projected, cosine[rows], sine[rows], heads, size, 2 * tree_size
        )
        queries, keys, values = (item.reshape(all_shape) for item in (queries, keys, values))
        if before_queries is not None:
            queries, before_queries = lax.optimization_barrier((queries, before_queries))
        even, odd = gather_requests(queries)
        plan = page_plan(
            page_owner, page_fill, chunk * step_requests, step_requests, req_local, parts
        )
        sums, logs = page_attention(even, odd, k_heads, v_heads, plan, heads, size)
        keys, sums, logs = lax.optimization_barrier((keys, sums, logs))
        tree_pair = tree_attention(queries, keys, values, reach[asked], heads, size)
        done = scatter_requests(
            sums.reshape((parts,) + all_shape),
            logs.reshape(parts, step_requests, 8, LANES),
            merge,
        )
        part_requests = step_requests // 2
        attended = []
        for part, (ours, got) in enumerate(done):
            own = slice(part * part_requests, (part + 1) * part_requests)
            pairs = [
                tuple(value.reshape((-1,) + value.shape[2:]) for value in pair)
                for pair in (ours, got)
            ] + [(tree_pair[0][own], tree_pair[1][own])]
            attended.append(merge_partials(pairs, heads, size, with_logs=False)[0])
        attended = jnp.concatenate(attended).reshape(step_tokens, heads * size)
        before_queries = attended
        attn_delta = scatter_columns(project(attended, out_weight))
        if sent_mid is not None:
            attn_delta, sent_mid = lax.optimization_barrier((attn_delta, sent_mid))
        attn_parts.append(attn_delta)

        stream_vals = streams[rows].astype(jnp.float32)
        mixed_mid = blend(stream_vals, mid_in) + mid_out * attn_delta
        normed_mid, gathered, sent_mid = gathered_norm(mixed_mid, width)
        shares = mlp(normed_mid, gate_up, down_weight)
        first_shares = shares if chunk == 0 else first_shares
        mlp_parts.append(scatter_columns(shares))

    attn_delta = jnp.concatenate(attn_parts)
    mlp_delta = jnp.concatenate(mlp_parts)
    stream_vals = streams.astype(jnp.float32)
    new_streams = both_out[None, :, None] * attn_delta[:, None] + (
        hc_out[1][None, :, None] * mlp_delta[:, None]
    )
    for index in range(stream_count):
        new_streams = (
            new_streams + both_mix[index][None, :, None] * stream_vals[:, index : index + 1]
        )
    new_streams = new_streams.astype(jnp.bfloat16)

    rows_taken = jnp.arange(req_local, dtype=jnp.int32) * tree_size + accepted_index
    stream_rows = streams[rows_taken].astype(jnp.float32)
    is_taken = jnp.arange(tree_size, dtype=jnp.int32)[None, :] == accepted_index[:, None]
    attn_rows = jnp.concatenate(
        [
            jnp.sum(
                jnp.where(
                    is_taken[chunk * step_requests : (chunk + 1) * step_requests, :, None],
                    part.reshape(step_requests, tree_size, feature_local),
                    0.0,
                ),
                axis=1,
            )
            for chunk, part in enumerate(attn_parts)
        ]
    )
    mid_rows = blend(stream_rows, mid_in) + mid_out * attn_rows
    mid_full = jnp.concatenate(list(shift_gather(mid_rows)), axis=1)
    mid_full, first_shares = lax.optimization_barrier((mid_full, first_shares))
    mlp_rows = shift_scatter(
        mlp(layer_norm(mid_full).astype(jnp.bfloat16), gate_up, down_weight)
    )
    final_local = (
        jnp.sum(both_out) * attn_rows + jnp.sum(hc_out[1]) * mlp_rows
    ) + blend(stream_rows, jnp.sum(both_mix, axis=1))
    final_full = jnp.concatenate(list(shift_gather(final_local)), axis=1)
    final_norm = layer_norm(final_full)
    own_columns = lax.dynamic_slice_in_dim(
        final_norm, lax.axis_index("head") * feature_local, feature_local, 1
    )
    branch = jnp.einsum(
        "jd,kde->jke",
        final_norm.astype(jnp.bfloat16),
        draft_weight,
        preferred_element_type=jnp.float32,
    )
    drafted = (own_columns[:, None, :] + jax.nn.silu(branch)).astype(jnp.bfloat16)
    draft_full = jnp.concatenate(list(shift_gather(drafted)), axis=2)
    draft_all = gather_small(draft_full)
    logits_local = jnp.dot(
        draft_all.reshape(-1, width), lm_head, preferred_element_type=jnp.float32
    )
    logits_local = logits_local.reshape(all_requests, draft_count, -1)
    logits = lax.all_to_all(
        logits_local.astype(jnp.bfloat16), ("req", "head"), split_axis=0, concat_axis=2, tiled=True
    ).astype(logits_local.dtype)
    return (new_streams, logits)


def merge_flat(ours, got, heads, size):
    lead = ours[0].shape[:2]
    pairs = [
        tuple(value.reshape((-1,) + value.shape[2:]) for value in pair) for pair in (ours, got)
    ]
    merged = merge_partials(pairs, heads, size)
    return [value.reshape(lead + value.shape[1:]) for value in merged]


def solution(mesh):
    in_specs = (
        P("req", None, "head"),
        P(),
        P(),
        P(),
        P(None, None, "head"),
        P("head", None),
        P(None, None, "head"),
        P("head", None),
        P(None, None, "head"),
        P(None, ("req", "head")),
        P("req", None, "head", None),
        P("req", None, "head", None),
        P("req"),
        P("req"),
        P("req"),
        P("req", None),
        P("req"),
    )
    out_specs = (P("req", None, "head"), P(("req", "head"), None, None))
    return jax.shard_map(
        on_device, mesh=mesh, in_specs=in_specs, out_specs=out_specs, check_vma=False
    )
```

```python
import functools
import math

import jax
import jax.numpy as jnp
from jax import lax
from jax.experimental import pallas as pl
from jax.experimental.pallas import tpu as pltpu
from jax.sharding import PartitionSpec as P

NEG_FILL = -1e30
EMPTY = -1e29
PRECISE = lax.Precision.HIGHEST
CHUNKS = 2
LANES = 128
PAGES_A_STEP = 2
VMEM_BYTES = 56 * 1024 * 1024


def params(count=1):
    return pltpu.CompilerParams(
        dimension_semantics=("arbitrary",) * count, vmem_limit_bytes=VMEM_BYTES
    )


def ancestors(parents):
    length = parents.shape[1]
    places = jnp.arange(length, dtype=jnp.int32)
    linked = (parents[:, :, None] == places[None, None, :]) | (places[:, None] == places[None, :])[
        None
    ]
    reach = linked.astype(jnp.float32)
    for repeat in range(max(1, (length - 1).bit_length())):
        reach = jnp.minimum(jnp.einsum("jik,jkl->jil", reach, reach, precision=PRECISE), 1.0)
    return reach


def layer_norm(values):
    center = jnp.mean(values, axis=-1, keepdims=True)
    square = jnp.mean(values * values, axis=-1, keepdims=True)
    return (values - center) * lax.rsqrt(square - center * center + 1e-05)


def blend(stream_vals, weights):
    total = weights[0] * stream_vals[:, 0]
    for index in range(1, stream_vals.shape[1]):
        total = total + weights[index] * stream_vals[:, index]
    return total


def shift_gather(small):
    count = lax.axis_size("head")
    rank = lax.axis_index("head")
    parts = [small] + [
        lax.ppermute(small, "head", [(z, (z + step) % count) for z in range(count)])
        for step in range(1, count)
    ]
    stacked = jnp.stack(parts)
    return jnp.stack(
        [
            lax.dynamic_index_in_dim(stacked, (rank - source) % count, 0, keepdims=False)
            for source in range(count)
        ]
    )


def shift_scatter(shares):
    count = lax.axis_size("head")
    rank = lax.axis_index("head")
    width = shares.shape[1] // count
    total = None
    for step in range(count):
        block = lax.dynamic_slice_in_dim(shares, (rank + step) % count * width, width, 1)
        if step:
            block = lax.ppermute(block, "head", [(z, (z + step) % count) for z in range(count)])
        block = block.astype(jnp.float32)
        total = block if total is None else total + block
    return total


def gathered_norm(values, width, after=None):
    local = values.shape[1]
    sums = jnp.sum(values, axis=1)
    squares = jnp.sum(values * values, axis=1)
    center = sums / local
    sent = (values - center[:, None]).astype(jnp.bfloat16)
    stats = shift_gather(jnp.stack([sums, squares]))
    if after is not None:
        sent, after = lax.optimization_barrier((sent, after))
    gathered = lax.all_gather(sent, "head", axis=1, tiled=True)
    mean = jnp.sum(stats[:, 0], axis=0) / width
    variance = jnp.sum(stats[:, 1], axis=0) / width - mean * mean
    scale = lax.rsqrt(variance + 1e-05)
    normed = [
        (
            (
                gathered[:, rank * local : (rank + 1) * local].astype(jnp.float32)
                + (stats[rank, 0] / local - mean)[:, None]
            )
            * scale[:, None]
        ).astype(jnp.bfloat16)
        for rank in range(lax.axis_size("head"))
    ]
    return jnp.concatenate(normed, axis=1), gathered, sent


def scatter_columns(shares):
    return lax.psum_scatter(shares, "head", scatter_dimension=1, tiled=True).astype(jnp.float32)


def swapped(values, bit):
    count = lax.axis_size("req")
    return lax.ppermute(values, "req", [(r, r ^ bit) for r in range(count)])


def bit_orders():
    bits = [1 << index for index in range((lax.axis_size("req") - 1).bit_length())]
    return bits[0], (bits[1:], bits[1:][::-1])


def gather_requests(values):
    half = values.shape[0] // 2
    near, orders = bit_orders()
    parts = []
    for part, order in enumerate(orders):
        blocks = {0: values[part * half : (part + 1) * half]}
        for bit in order:
            for index in list(blocks):
                blocks[index ^ bit] = swapped(blocks[index], bit)
        parts.append(blocks)
    even = jnp.concatenate([blocks[index] for index in sorted(parts[0]) for blocks in parts])
    return even, swapped(even, near)


def gather_small(values):
    count = lax.axis_size("req")
    near, orders = bit_orders()
    stacked = values[None]
    bits = []
    for bit in list(orders[0]) + [near]:
        stacked = jnp.concatenate([stacked, swapped(stacked, bit)])
        bits.append(bit)
    index = lax.axis_index("req") ^ jnp.arange(count, dtype=jnp.int32)
    place = jnp.zeros_like(index)
    for spot, bit in enumerate(bits):
        place = place + jnp.where((index & bit) != 0, 1 << spot, 0)
    return stacked[place]


def scatter_requests(sums, logs, merge):
    near, orders = bit_orders()
    count = lax.axis_size("req")
    far = count // 2
    state = []
    mine = [sums[:far], logs[:far]]
    theirs = [swapped(sums[far:], near), swapped(logs[far:], near)]
    merged = first_merged = merge(mine, theirs)
    half = sums.shape[1] // 2
    done = []
    for part, order in enumerate(orders):
        kept = [value[:, part * half : (part + 1) * half] for value in merged]
        places = list(range(far))
        for place, bit in enumerate(order):
            stay = [at for at, index in enumerate(places) if not index & (bit >> 1)]
            leave = [at for at, index in enumerate(places) if index & (bit >> 1)]
            pick = lambda value, which: jnp.concatenate([value[at : at + 1] for at in which])
            ours = [pick(value, stay) for value in kept]
            got = [swapped(pick(value, leave), bit) for value in kept]
            places = [places[at] for at in stay]
            kept = merge(ours, got) if place < len(order) - 1 else (ours, got)
        done.append(kept)
    return done, first_merged[1]


def rotate_kernel(heads, size, scale, x_ref, cos_ref, sin_ref, q_ref, k_ref, v_ref):
    width = heads * size
    cosine, sine = cos_ref[...], sin_ref[...]
    for head in range(heads):
        at = head * size
        for base, out_ref, factor in ((0, q_ref, scale), (width, k_ref, 1.0)):
            values = x_ref[:, base + at : base + at + size]
            turned = values * cosine + pltpu.roll(values, size // 2, 1) * sine
            out_ref[:, at : at + size] = (turned * factor).astype(out_ref.dtype)
    v_ref[...] = x_ref[:, 2 * width :].astype(v_ref.dtype)


def rotate_all(projected, cosine, sine, heads, size, rows):
    tokens = projected.shape[0]
    out = jax.ShapeDtypeStruct((tokens, heads * size), jnp.bfloat16)
    block = lambda width: pl.BlockSpec((rows, width), lambda i: (i, 0))
    return pl.pallas_call(
        functools.partial(rotate_kernel, heads, size, size ** (-0.5)),
        grid=(tokens // rows,),
        in_specs=[block(3 * heads * size), block(size), block(size)],
        out_specs=[block(heads * size)] * 3,
        out_shape=[out] * 3,
        compiler_params=params(),
        name="rotate",
    )(projected, cosine, sine)


def lay_logs(columns, rows):
    lane = lax.broadcasted_iota(jnp.int32, (LANES, LANES), 1)
    table = jnp.full((LANES, LANES), NEG_FILL, jnp.float32)
    for head, column in enumerate(columns):
        tall = jnp.concatenate(
            [column, jnp.full((LANES - rows, 1), NEG_FILL, jnp.float32)], axis=0
        )
        table = jnp.where(lane == head, tall, table)
    return jnp.transpose(table)[:8]


def tree_kernel(heads, size, q_ref, k_ref, v_ref, reach_ref, out_ref, log_ref):
    seen = reach_ref[0] > 0
    logs = []
    for head in range(heads):
        at = slice(head * size, (head + 1) * size)
        scores = lax.dot_general(
            q_ref[0, :, at],
            k_ref[0, :, at],
            (((1,), (1,)), ((), ())),
            preferred_element_type=jnp.float32,
        )
        scores = jnp.where(seen, scores, NEG_FILL)
        top = jnp.max(scores, axis=1, keepdims=True)
        weights = jnp.where(seen, jnp.exp(scores - top), 0.0)
        total = jnp.sum(weights, axis=1, keepdims=True)
        summed = jnp.dot(
            weights.astype(jnp.bfloat16), v_ref[0, :, at], preferred_element_type=jnp.float32
        )
        out_ref[0, :, at] = summed / total
        logs.append(top + jnp.log(total))
    log_ref[0] = lay_logs(logs, q_ref.shape[1])


def tree_attention(queries, keys, values, reach, heads, size):
    requests, tree, width = queries.shape
    block = pl.BlockSpec((1, tree, width), lambda j: (j, 0, 0))
    return pl.pallas_call(
        functools.partial(tree_kernel, heads, size),
        grid=(requests,),
        in_specs=[block] * 3 + [pl.BlockSpec((1, tree, tree), lambda j: (j, 0, 0))],
        out_specs=[block, pl.BlockSpec((1, 8, LANES), lambda j: (j, 0, 0))],
        out_shape=[
            jax.ShapeDtypeStruct((requests, tree, width), jnp.float32),
            jax.ShapeDtypeStruct((requests, 8, LANES), jnp.float32),
        ],
        compiler_params=params(),
        name="tree_attention",
    )(queries, keys, values, reach)


def page_kernel(
    heads,
    size,
    page_ref,
    place_ref,
    fill_ref,
    first_ref,
    last_ref,
    live_ref,
    even_ref,
    odd_ref,
    *refs,
):
    leaves = refs[: 2 * PAGES_A_STEP]
    out_ref, log_ref, acc_ref, top_ref, total_ref = refs[2 * PAGES_A_STEP :]
    step = pl.program_id(0)
    half, tree = even_ref.shape[:2]
    spans = [slice(head * size, (head + 1) * size) for head in range(heads)]
    entries = leaves[0].shape[2]

    @pl.when(step == 0)
    def _():
        log_ref[...] = jnp.full(log_ref.shape, NEG_FILL, jnp.float32)

    @pl.when(step * PAGES_A_STEP < live_ref[0])
    def _():
        column = lax.broadcasted_iota(jnp.int32, (tree, entries), 1)
        units = [(part, head) for part in range(PAGES_A_STEP) for head in range(heads)]
        asked, valid = [], []
        for part in range(PAGES_A_STEP):
            visit = step * PAGES_A_STEP + part
            place = place_ref[visit]
            asked.append(
                jnp.where(
                    place < half,
                    even_ref[jnp.minimum(place, half - 1)],
                    odd_ref[jnp.maximum(place - half, 0)],
                )
            )
            valid.append(column < fill_ref[visit])
        scores = [
            lax.dot_general(
                asked[part][:, spans[head]],
                leaves[2 * part][0, head],
                (((1,), (1,)), ((), ())),
                preferred_element_type=jnp.float32,
            )
            for part, head in units
        ]
        scores = [
            jnp.where(valid[part], score, NEG_FILL) for (part, head), score in zip(units, scores)
        ]
        tops = [jnp.max(score, axis=1, keepdims=True) for score in scores]
        weights = [
            jnp.where(valid[part], jnp.exp(score - top), 0.0)
            for (part, head), score, top in zip(units, scores, tops)
        ]
        totals = [jnp.sum(weight, axis=1, keepdims=True) for weight in weights]
        sums = [
            jnp.dot(
                weight.astype(jnp.bfloat16),
                leaves[2 * part + 1][0, head],
                preferred_element_type=jnp.float32,
            )
            for (part, head), weight in zip(units, weights)
        ]
        for part in range(PAGES_A_STEP):
            visit = step * PAGES_A_STEP + part
            merge_page(
                visit,
                spans,
                tops[part * heads : (part + 1) * heads],
                totals[part * heads : (part + 1) * heads],
                sums[part * heads : (part + 1) * heads],
                place_ref,
                first_ref,
                last_ref,
                live_ref,
                out_ref,
                log_ref,
                acc_ref,
                top_ref,
                total_ref,
            )


def merge_page(
    visit,
    spans,
    tops,
    totals,
    sums,
    place_ref,
    first_ref,
    last_ref,
    live_ref,
    out_ref,
    log_ref,
    acc_ref,
    top_ref,
    total_ref,
):
    tree = acc_ref.shape[0]
    live = visit < live_ref[0]
    alone = (first_ref[visit] == 1) & (last_ref[visit] == 1)

    def write(tops, totals, sums):
        logs = []
        for span, top, total, value in zip(spans, tops, totals, sums):
            some = total > 0
            safe = jnp.where(some, total, 1.0)
            out_ref[place_ref[visit], :, span] = (value / safe).astype(out_ref.dtype)
            logs.append(jnp.where(some, top + jnp.log(safe), NEG_FILL)[:, :1])
        log_ref[place_ref[visit]] = lay_logs(logs, tree)

    @pl.when(live & alone)
    def _():
        write(tops, totals, sums)

    @pl.when(live & jnp.logical_not(alone))
    def _():
        @pl.when(first_ref[visit] == 1)
        def _():
            acc_ref[...] = jnp.zeros(acc_ref.shape, jnp.float32)
            top_ref[...] = jnp.full(top_ref.shape, NEG_FILL, jnp.float32)
            total_ref[...] = jnp.zeros(total_ref.shape, jnp.float32)

        for head, span in enumerate(spans):
            before = top_ref[head]
            top = jnp.maximum(before, tops[head])
            decay, gain = jnp.exp(before - top), jnp.exp(tops[head] - top)
            top_ref[head] = top
            total_ref[head] = total_ref[head] * decay + totals[head] * gain
            acc_ref[:, span] = acc_ref[:, span] * decay + sums[head] * gain

        @pl.when(last_ref[visit] == 1)
        def _():
            heads = range(len(spans))
            write(
                [top_ref[head] for head in heads],
                [total_ref[head] for head in heads],
                [acc_ref[:, span] for span in spans],
            )


def page_attention(even, odd, k_pages, v_pages, plan, heads, size):
    half, tree, width = even.shape
    requests = 2 * half
    slots, entries = k_pages.shape[0], k_pages.shape[2]
    whole = lambda shape: pl.BlockSpec(shape, lambda p, *rest: (0, 0, 0))

    def leaf(part):
        return pl.BlockSpec(
            (1, heads, entries, size),
            lambda p, page, *rest: (page[p * PAGES_A_STEP + part], 0, 0, 0),
        )

    grid_spec = pltpu.PrefetchScalarGridSpec(
        num_scalar_prefetch=6,
        grid=(slots // PAGES_A_STEP,),
        in_specs=[whole(even.shape), whole(odd.shape)]
        + [leaf(part) for part in range(PAGES_A_STEP) for _ in range(2)],
        out_specs=[whole((requests, tree, width)), whole((requests, 8, LANES))],
        scratch_shapes=[
            pltpu.VMEM((tree, width), jnp.float32),
            pltpu.VMEM((heads, tree, size), jnp.float32),
            pltpu.VMEM((heads, tree, size), jnp.float32),
        ],
    )
    return pl.pallas_call(
        functools.partial(page_kernel, heads, size),
        grid_spec=grid_spec,
        out_shape=[
            jax.ShapeDtypeStruct((requests, tree, width), jnp.bfloat16),
            jax.ShapeDtypeStruct((requests, 8, LANES), jnp.float32),
        ],
        compiler_params=params(),
        name="page_attention",
    )(*plan, even, odd, *([k_pages, v_pages] * PAGES_A_STEP))


def project_kernel(x_ref, w_ref, out_ref):
    out_ref[...] = jnp.dot(x_ref[...], w_ref[...], preferred_element_type=jnp.float32).astype(
        out_ref.dtype
    )


def project(values, weight):
    rows, depth = values.shape
    columns = weight.shape[1]
    tile = min(columns, 512)
    return pl.pallas_call(
        project_kernel,
        grid=(columns // tile,),
        in_specs=[
            pl.BlockSpec((rows, depth), lambda i: (0, 0)),
            pl.BlockSpec((depth, tile), lambda i: (0, i)),
        ],
        out_specs=pl.BlockSpec((rows, tile), lambda i: (0, i)),
        out_shape=jax.ShapeDtypeStruct((rows, columns), jnp.bfloat16),
        compiler_params=params(),
        name="project",
    )(values, weight)


def mlp_kernel(steps, tile, x_ref, gate_ref, up_ref, down_ref, out_ref, hidden_ref):
    step = pl.program_id(0)

    @pl.when(step < steps)
    def _():
        gate = jnp.dot(x_ref[...], gate_ref[...], preferred_element_type=jnp.float32)
        up = jnp.dot(x_ref[...], up_ref[...], preferred_element_type=jnp.float32)
        at = pl.ds(pl.multiple_of(step * tile, tile), tile)
        hidden_ref[:, at] = (jax.nn.silu(gate) * up).astype(hidden_ref.dtype)

    @pl.when(step >= steps)
    def _():
        out_ref[...] = jnp.dot(
            hidden_ref[...], down_ref[...], preferred_element_type=jnp.float32
        ).astype(out_ref.dtype)


def mlp(values, gate_up, down):
    rows, width = values.shape
    hidden, columns = down.shape
    tile = min(hidden, 512)
    steps = hidden // tile
    out_tile = min(columns, 512)
    late = lambda i: jnp.maximum(i - steps, 0)
    early = lambda i: jnp.minimum(i, steps - 1)
    return pl.pallas_call(
        functools.partial(mlp_kernel, steps, tile),
        grid=(steps + columns // out_tile,),
        in_specs=[
            pl.BlockSpec((rows, width), lambda i: (0, 0)),
            pl.BlockSpec((width, tile), lambda i: (0, early(i))),
            pl.BlockSpec((width, tile), lambda i: (0, steps + early(i))),
            pl.BlockSpec((hidden, out_tile), lambda i: (0, late(i))),
        ],
        out_specs=pl.BlockSpec((rows, out_tile), lambda i: (0, late(i))),
        out_shape=jax.ShapeDtypeStruct((rows, columns), jnp.bfloat16),
        scratch_shapes=[pltpu.VMEM((rows, hidden), jnp.bfloat16)],
        compiler_params=params(),
        name="mlp",
    )(values, gate_up, gate_up, down)


def merge_kernel(heads, size, count, *refs):
    sums, logs, out_ref = refs[:count], refs[count : 2 * count], refs[2 * count]
    log_ref = refs[2 * count + 1] if len(refs) > 2 * count + 1 else None
    tree = out_ref.shape[1]
    for request in range(out_ref.shape[0]):
        tables = [ref[request] for ref in logs]
        top = functools.reduce(jnp.maximum, tables)
        total = functools.reduce(lambda a, b: a + b, [jnp.exp(table - top) for table in tables])
        merged = top + jnp.log(total)
        if log_ref is not None:
            log_ref[request] = merged
        shares = [
            jnp.transpose(jnp.where(table > EMPTY, jnp.exp(table - merged), 0.0))
            for table in tables
        ]
        for head in range(heads):
            at = slice(head * size, (head + 1) * size)
            value = jnp.zeros((tree, size), jnp.float32)
            for ref, share in zip(sums, shares):
                factor = share[:tree, head : head + 1]
                term = ref[request, :, at].astype(jnp.float32)
                value = value + jnp.where(factor > 0, term * factor, 0.0)
            out_ref[request, :, at] = value.astype(out_ref.dtype)


def merge_partials(pairs, heads, size, with_logs=True):
    requests, tree, width = pairs[0][0].shape
    group = max(size for size in (1, 2, 4, 8) if requests % size == 0)
    big = pl.BlockSpec((group, tree, width), lambda j: (j, 0, 0))
    small = pl.BlockSpec((group, 8, LANES), lambda j: (j, 0, 0))
    out_specs = [big, small] if with_logs else [big]
    out_shape = [
        jax.ShapeDtypeStruct((requests, tree, width), jnp.bfloat16),
        jax.ShapeDtypeStruct((requests, 8, LANES), jnp.float32),
    ][: len(out_specs)]
    return pl.pallas_call(
        functools.partial(merge_kernel, heads, size, len(pairs)),
        grid=(requests // group,),
        in_specs=[big] * len(pairs) + [small] * len(pairs),
        out_specs=out_specs,
        out_shape=out_shape,
        compiler_params=params(),
        name="merge_partials",
    )(*[pair[0] for pair in pairs], *[pair[1] for pair in pairs])


def page_plan(owner, fill, first_request, requests, all_local, count):
    slots = owner.shape[0]
    me = lax.axis_index("req")
    source = owner // all_local
    local = owner % all_local - first_request
    mine = (owner >= 0) & (local >= 0) & (local < requests)
    index = source ^ me
    index = (index & 1) * (count // 2) + (index >> 1)
    place = jnp.where(mine, index * requests + local, count * requests)
    spot = jnp.arange(slots, dtype=jnp.int32)
    ahead = (place[None, :] < place[:, None]) | (
        (place[None, :] == place[:, None]) & (spot[None, :] < spot[:, None])
    )
    rank = jnp.sum(ahead.astype(jnp.int32), axis=1)
    live = jnp.sum(mine.astype(jnp.int32))
    wanted = jnp.minimum(spot, jnp.maximum(live - 1, 0))
    chosen = rank[None, :] == wanted[:, None]
    take = lambda values: jnp.sum(jnp.where(chosen, values[None, :], 0), axis=1)
    pages, places, fills = take(spot), take(jnp.where(mine, place, 0)), take(fill)
    changed = (places[1:] != places[:-1]).astype(jnp.int32)
    one = jnp.ones((1,), jnp.int32)
    first = jnp.concatenate([one, changed])
    last = jnp.concatenate([changed, one])
    last = jnp.where(spot == live - 1, 1, last)
    return (pages, places, fills, first, last, live[None])


def on_device(
    streams,
    hc_in,
    hc_mix,
    hc_out,
    qkv_weight,
    out_weight,
    up_gate,
    down_weight,
    draft_weight,
    lm_head,
    k_pages,
    v_pages,
    page_owner,
    page_fill,
    cache_len,
    tree_parent,
    accepted_index,
):
    tokens_local = streams.shape[0]
    stream_count = streams.shape[1]
    feature_local = streams.shape[2]
    width = qkv_weight.shape[0]
    req_local = cache_len.shape[0]
    tree_size = tree_parent.shape[1]
    heads = k_pages.shape[2]
    size = k_pages.shape[3]
    draft_count = draft_weight.shape[0]
    parts = lax.axis_size("req")
    all_requests = req_local * parts

    identity = jnp.eye(stream_count, dtype=jnp.float32)
    first_mix, second_mix = identity + hc_mix[0], identity + hc_mix[1]
    mid_in = jnp.sum(first_mix * hc_in[1][None, :], axis=1)
    mid_out = jnp.sum(hc_out[0] * hc_in[1])
    both_mix = jnp.sum(first_mix[:, :, None] * second_mix[None, :, :], axis=1)
    both_out = jnp.sum(hc_out[0][:, None] * second_mix, axis=0)

    reach = ancestors(tree_parent)
    depth = (jnp.sum(reach, axis=2) - 1.0).astype(jnp.int32)
    positions = (cache_len[:, None] + depth).reshape(tokens_local)
    half = size // 2
    freqs = jnp.exp(jnp.arange(half, dtype=jnp.float32) * (-2.0 * math.log(10000.0) / size))
    angles = positions.astype(jnp.float32)[:, None] * freqs[None, :]
    cosine, sine = jnp.cos(angles), jnp.sin(angles)
    cosine = jnp.concatenate([cosine, cosine], axis=1)
    sine = jnp.concatenate([-sine, sine], axis=1)

    k_heads = jnp.transpose(k_pages, (0, 2, 1, 3))
    v_heads = jnp.transpose(v_pages, (0, 2, 1, 3))

    step_requests = req_local // CHUNKS
    step_tokens = step_requests * tree_size
    merge = lambda ours, got: merge_flat(ours, got, heads, size)

    gate_up = up_gate.reshape(width, -1)
    token = None
    first_shares = None
    before_normed = None
    attended_in = []
    for chunk in range(CHUNKS):
        rows = slice(chunk * step_tokens, (chunk + 1) * step_tokens)
        stream_vals = streams[rows].astype(jnp.float32)
        mixed_in = blend(stream_vals, hc_in[0])
        normed, token, sent = gathered_norm(mixed_in, width, token)
        if chunk == 0:
            normed, k_heads, v_heads, gate_up = lax.optimization_barrier(
                (normed, k_heads, v_heads, gate_up)
            )
        attended_in.append(normed)

    all_shape = (step_requests, tree_size, heads * size)
    before_queries = None
    attn_parts, mlp_parts = [], []
    for chunk in range(CHUNKS):
        rows = slice(chunk * step_tokens, (chunk + 1) * step_tokens)
        asked = slice(chunk * step_requests, (chunk + 1) * step_requests)
        normed = attended_in[chunk]
        if before_normed is not None:
            normed, before_normed = lax.optimization_barrier((normed, before_normed))
        projected = jnp.concatenate(
            [
                jnp.dot(normed, qkv_weight[:, third], preferred_element_type=jnp.float32)
                for third in range(3)
            ],
            axis=1,
        )
        queries, keys, values = rotate_all(
            projected, cosine[rows], sine[rows], heads, size, 2 * tree_size
        )
        queries, keys, values = (item.reshape(all_shape) for item in (queries, keys, values))
        if before_queries is not None:
            queries, before_queries = lax.optimization_barrier((queries, before_queries))
        even, odd = gather_requests(queries)
        plan = page_plan(
            page_owner, page_fill, chunk * step_requests, step_requests, req_local, parts
        )
        sums, logs = page_attention(even, odd, k_heads, v_heads, plan, heads, size)
        keys, sums, logs = lax.optimization_barrier((keys, sums, logs))
        tree_pair = tree_attention(queries, keys, values, reach[asked], heads, size)
        done, before_normed = scatter_requests(
            sums.reshape((parts,) + all_shape),
            logs.reshape(parts, step_requests, 8, LANES),
            merge,
        )
        part_requests = step_requests // 2
        attended = []
        for part, (ours, got) in enumerate(done):
            own = slice(part * part_requests, (part + 1) * part_requests)
            pairs = [
                tuple(value.reshape((-1,) + value.shape[2:]) for value in pair)
                for pair in (ours, got)
            ] + [(tree_pair[0][own], tree_pair[1][own])]
            attended.append(merge_partials(pairs, heads, size, with_logs=False)[0])
        attended = jnp.concatenate(attended).reshape(step_tokens, heads * size)
        before_queries = attended
        attn_delta = scatter_columns(project(attended, out_weight))
        if first_shares is not None:
            attn_delta, first_shares = lax.optimization_barrier((attn_delta, first_shares))
        attn_parts.append(attn_delta)

        stream_vals = streams[rows].astype(jnp.float32)
        mixed_mid = blend(stream_vals, mid_in) + mid_out * attn_delta
        normed_mid, gathered, sent_mid = gathered_norm(mixed_mid, width)
        shares = mlp(normed_mid, gate_up, down_weight)
        if first_shares is None:
            first_shares = shares
        else:
            first_shares, sent_mid = lax.optimization_barrier((first_shares, sent_mid))
            mlp_parts.append(scatter_columns(first_shares))
            mlp_parts.append(scatter_columns(shares))

    attn_delta = jnp.concatenate(attn_parts)
    mlp_delta = jnp.concatenate(mlp_parts)
    stream_vals = streams.astype(jnp.float32)
    new_streams = both_out[None, :, None] * attn_delta[:, None] + (
        hc_out[1][None, :, None] * mlp_delta[:, None]
    )
    for index in range(stream_count):
        new_streams = (
            new_streams + both_mix[index][None, :, None] * stream_vals[:, index : index + 1]
        )
    new_streams = new_streams.astype(jnp.bfloat16)

    rows_taken = jnp.arange(req_local, dtype=jnp.int32) * tree_size + accepted_index
    stream_rows = streams[rows_taken].astype(jnp.float32)
    is_taken = jnp.arange(tree_size, dtype=jnp.int32)[None, :] == accepted_index[:, None]
    attn_rows = jnp.concatenate(
        [
            jnp.sum(
                jnp.where(
                    is_taken[chunk * step_requests : (chunk + 1) * step_requests, :, None],
                    part.reshape(step_requests, tree_size, feature_local),
                    0.0,
                ),
                axis=1,
            )
            for chunk, part in enumerate(attn_parts)
        ]
    )
    mid_rows = blend(stream_rows, mid_in) + mid_out * attn_rows
    mid_full = jnp.concatenate(list(shift_gather(mid_rows)), axis=1)
    mid_full, first_shares = lax.optimization_barrier((mid_full, first_shares))
    mlp_rows = shift_scatter(
        mlp(layer_norm(mid_full).astype(jnp.bfloat16), gate_up, down_weight)
    )
    final_local = (
        jnp.sum(both_out) * attn_rows + jnp.sum(hc_out[1]) * mlp_rows
    ) + blend(stream_rows, jnp.sum(both_mix, axis=1))
    final_full = jnp.concatenate(list(shift_gather(final_local)), axis=1)
    final_norm = layer_norm(final_full)
    own_columns = lax.dynamic_slice_in_dim(
        final_norm, lax.axis_index("head") * feature_local, feature_local, 1
    )
    branch = jnp.einsum(
        "jd,kde->jke",
        final_norm.astype(jnp.bfloat16),
        draft_weight,
        preferred_element_type=jnp.float32,
    )
    drafted = (own_columns[:, None, :] + jax.nn.silu(branch)).astype(jnp.bfloat16)
    draft_full = jnp.concatenate(list(shift_gather(drafted)), axis=2)
    draft_all = gather_small(draft_full)
    logits_local = jnp.dot(
        draft_all.reshape(-1, width), lm_head, preferred_element_type=jnp.float32
    )
    logits_local = logits_local.reshape(all_requests, draft_count, -1)
    logits = lax.all_to_all(
        logits_local.astype(jnp.bfloat16), ("req", "head"), split_axis=0, concat_axis=2, tiled=True
    ).astype(logits_local.dtype)
    return (new_streams, logits)


def merge_flat(ours, got, heads, size):
    lead = ours[0].shape[:2]
    pairs = [
        tuple(value.reshape((-1,) + value.shape[2:]) for value in pair) for pair in (ours, got)
    ]
    merged = merge_partials(pairs, heads, size)
    return [value.reshape(lead + value.shape[1:]) for value in merged]


def solution(mesh):
    in_specs = (
        P("req", None, "head"),
        P(),
        P(),
        P(),
        P(None, None, "head"),
        P("head", None),
        P(None, None, "head"),
        P("head", None),
        P(None, None, "head"),
        P(None, ("req", "head")),
        P("req", None, "head", None),
        P("req", None, "head", None),
        P("req"),
        P("req"),
        P("req"),
        P("req", None),
        P("req"),
    )
    out_specs = (P("req", None, "head"), P(("req", "head"), None, None))
    return jax.shard_map(
        on_device, mesh=mesh, in_specs=in_specs, out_specs=out_specs, check_vma=False
    )
```

```python
import functools
import math

import jax
import jax.numpy as jnp
from jax import lax
from jax.experimental import pallas as pl
from jax.experimental.pallas import tpu as pltpu
from jax.sharding import PartitionSpec as P

NEG_FILL = -1e30
EMPTY = -1e29
PRECISE = lax.Precision.HIGHEST
CHUNKS = 2
LANES = 128
PAGES_A_STEP = 2
MIB = 1024 * 1024


def params(mebibytes):
    return pltpu.CompilerParams(
        dimension_semantics=("arbitrary",), vmem_limit_bytes=mebibytes * MIB
    )


def ancestors(parents):
    length = parents.shape[1]
    places = jnp.arange(length, dtype=jnp.int32)
    linked = (parents[:, :, None] == places[None, None, :]) | (places[:, None] == places[None, :])[
        None
    ]
    reach = linked.astype(jnp.float32)
    for repeat in range(max(1, (length - 1).bit_length())):
        reach = jnp.minimum(jnp.einsum("jik,jkl->jil", reach, reach, precision=PRECISE), 1.0)
    return reach


def layer_norm(values):
    center = jnp.mean(values, axis=-1, keepdims=True)
    square = jnp.mean(values * values, axis=-1, keepdims=True)
    return (values - center) * lax.rsqrt(square - center * center + 1e-05)


def blend(stream_vals, weights):
    total = weights[0] * stream_vals[:, 0]
    for index in range(1, stream_vals.shape[1]):
        total = total + weights[index] * stream_vals[:, index]
    return total


def shift_gather(small):
    count = lax.axis_size("head")
    rank = lax.axis_index("head")
    parts = [small] + [
        lax.ppermute(small, "head", [(z, (z + step) % count) for z in range(count)])
        for step in range(1, count)
    ]
    stacked = jnp.stack(parts)
    return jnp.stack(
        [
            lax.dynamic_index_in_dim(stacked, (rank - source) % count, 0, keepdims=False)
            for source in range(count)
        ]
    )


def shift_scatter(shares):
    count = lax.axis_size("head")
    rank = lax.axis_index("head")
    width = shares.shape[1] // count
    total = None
    for step in range(count):
        block = lax.dynamic_slice_in_dim(shares, (rank + step) % count * width, width, 1)
        if step:
            block = lax.ppermute(block, "head", [(z, (z + step) % count) for z in range(count)])
        block = block.astype(jnp.float32)
        total = block if total is None else total + block
    return total


def gathered_norm(values, width, after=None):
    local = values.shape[1]
    sums = jnp.sum(values, axis=1)
    squares = jnp.sum(values * values, axis=1)
    center = sums / local
    sent = (values - center[:, None]).astype(jnp.bfloat16)
    stats = shift_gather(jnp.stack([sums, squares]))
    if after is not None:
        sent, after = lax.optimization_barrier((sent, after))
    gathered = lax.all_gather(sent, "head", axis=1, tiled=True)
    mean = jnp.sum(stats[:, 0], axis=0) / width
    variance = jnp.sum(stats[:, 1], axis=0) / width - mean * mean
    scale = lax.rsqrt(variance + 1e-05)
    normed = [
        (
            (
                gathered[:, rank * local : (rank + 1) * local].astype(jnp.float32)
                + (stats[rank, 0] / local - mean)[:, None]
            )
            * scale[:, None]
        ).astype(jnp.bfloat16)
        for rank in range(lax.axis_size("head"))
    ]
    return jnp.concatenate(normed, axis=1), gathered, sent


def scatter_columns(shares):
    return lax.psum_scatter(shares, "head", scatter_dimension=1, tiled=True).astype(jnp.float32)


def swapped(values, bit):
    count = lax.axis_size("req")
    return lax.ppermute(values, "req", [(r, r ^ bit) for r in range(count)])


def bit_orders():
    bits = [1 << index for index in range((lax.axis_size("req") - 1).bit_length())]
    return bits[0], (bits[1:], bits[1:][::-1])


def gather_requests(values):
    half = values.shape[0] // 2
    near, orders = bit_orders()
    parts = []
    for part, order in enumerate(orders):
        blocks = {0: values[part * half : (part + 1) * half]}
        for bit in order:
            for index in list(blocks):
                blocks[index ^ bit] = swapped(blocks[index], bit)
        parts.append(blocks)
    even = jnp.concatenate([blocks[index] for index in sorted(parts[0]) for blocks in parts])
    return even, swapped(even, near)


def gather_small(values):
    count = lax.axis_size("req")
    near, orders = bit_orders()
    stacked = values[None]
    bits = []
    for bit in list(orders[0]) + [near]:
        stacked = jnp.concatenate([stacked, swapped(stacked, bit)])
        bits.append(bit)
    index = lax.axis_index("req") ^ jnp.arange(count, dtype=jnp.int32)
    place = jnp.zeros_like(index)
    for spot, bit in enumerate(bits):
        place = place + jnp.where((index & bit) != 0, 1 << spot, 0)
    return stacked[place]


def scatter_requests(sums, logs, merge):
    near, orders = bit_orders()
    count = lax.axis_size("req")
    far = count // 2
    state = []
    mine = [sums[:far], logs[:far]]
    theirs = [swapped(sums[far:], near), swapped(logs[far:], near)]
    merged = first_merged = merge(mine, theirs)
    half = sums.shape[1] // 2
    done = []
    for part, order in enumerate(orders):
        kept = [value[:, part * half : (part + 1) * half] for value in merged]
        places = list(range(far))
        for place, bit in enumerate(order):
            stay = [at for at, index in enumerate(places) if not index & (bit >> 1)]
            leave = [at for at, index in enumerate(places) if index & (bit >> 1)]
            pick = lambda value, which: jnp.concatenate([value[at : at + 1] for at in which])
            ours = [pick(value, stay) for value in kept]
            got = [swapped(pick(value, leave), bit) for value in kept]
            places = [places[at] for at in stay]
            kept = merge(ours, got) if place < len(order) - 1 else (ours, got)
        done.append(kept)
    return done, first_merged[1]


def rotate_kernel(heads, size, scale, x_ref, y_ref, z_ref, cos_ref, sin_ref, q_ref, k_ref, v_ref):
    cosine, sine = cos_ref[...], sin_ref[...]
    for head in range(heads):
        at = slice(head * size, (head + 1) * size)
        for in_ref, out_ref, factor in ((x_ref, q_ref, scale), (y_ref, k_ref, 1.0)):
            values = in_ref[:, at]
            turned = values * cosine + pltpu.roll(values, size // 2, 1) * sine
            out_ref[:, at] = (turned * factor).astype(out_ref.dtype)
    v_ref[...] = z_ref[...].astype(v_ref.dtype)


def rotate_all(thirds, cosine, sine, heads, size, rows):
    tokens, width = thirds[0].shape
    out = jax.ShapeDtypeStruct((tokens, width), jnp.bfloat16)
    block = lambda lanes: pl.BlockSpec((rows, lanes), lambda i: (i, 0))
    return pl.pallas_call(
        functools.partial(rotate_kernel, heads, size, size ** (-0.5)),
        grid=(tokens // rows,),
        in_specs=[block(width)] * 3 + [block(size)] * 2,
        out_specs=[block(width)] * 3,
        out_shape=[out] * 3,
        compiler_params=params(8),
        name="rotate",
    )(*thirds, cosine, sine)


def lay_logs(columns, rows):
    lane = lax.broadcasted_iota(jnp.int32, (LANES, LANES), 1)
    table = jnp.full((LANES, LANES), NEG_FILL, jnp.float32)
    for head, column in enumerate(columns):
        tall = jnp.concatenate(
            [column, jnp.full((LANES - rows, 1), NEG_FILL, jnp.float32)], axis=0
        )
        table = jnp.where(lane == head, tall, table)
    return jnp.transpose(table)[:8]


def tree_kernel(heads, size, q_ref, k_ref, v_ref, reach_ref, out_ref, log_ref):
    seen = reach_ref[0] > 0
    logs = []
    for head in range(heads):
        at = slice(head * size, (head + 1) * size)
        scores = lax.dot_general(
            q_ref[0, :, at],
            k_ref[0, :, at],
            (((1,), (1,)), ((), ())),
            preferred_element_type=jnp.float32,
        )
        scores = jnp.where(seen, scores, NEG_FILL)
        top = jnp.max(scores, axis=1, keepdims=True)
        weights = jnp.where(seen, jnp.exp(scores - top), 0.0)
        total = jnp.sum(weights, axis=1, keepdims=True)
        summed = jnp.dot(
            weights.astype(jnp.bfloat16), v_ref[0, :, at], preferred_element_type=jnp.float32
        )
        out_ref[0, :, at] = summed / total
        logs.append(top + jnp.log(total))
    log_ref[0] = lay_logs(logs, q_ref.shape[1])


def tree_attention(queries, keys, values, reach, heads, size):
    requests, tree, width = queries.shape
    block = pl.BlockSpec((1, tree, width), lambda j: (j, 0, 0))
    return pl.pallas_call(
        functools.partial(tree_kernel, heads, size),
        grid=(requests,),
        in_specs=[block] * 3 + [pl.BlockSpec((1, tree, tree), lambda j: (j, 0, 0))],
        out_specs=[block, pl.BlockSpec((1, 8, LANES), lambda j: (j, 0, 0))],
        out_shape=[
            jax.ShapeDtypeStruct((requests, tree, width), jnp.float32),
            jax.ShapeDtypeStruct((requests, 8, LANES), jnp.float32),
        ],
        compiler_params=params(8),
        name="tree_attention",
    )(queries, keys, values, reach)


def page_kernel(
    heads,
    size,
    page_ref,
    place_ref,
    fill_ref,
    first_ref,
    last_ref,
    live_ref,
    even_ref,
    odd_ref,
    *refs,
):
    leaves = refs[: 2 * PAGES_A_STEP]
    out_ref, log_ref, acc_ref, top_ref, total_ref = refs[2 * PAGES_A_STEP :]
    step = pl.program_id(0)
    half, tree = even_ref.shape[:2]
    spans = [slice(head * size, (head + 1) * size) for head in range(heads)]
    entries = leaves[0].shape[2]

    @pl.when(step == 0)
    def _():
        log_ref[...] = jnp.full(log_ref.shape, NEG_FILL, jnp.float32)

    @pl.when(step * PAGES_A_STEP < live_ref[0])
    def _():
        column = lax.broadcasted_iota(jnp.int32, (tree, entries), 1)
        units = [(part, head) for part in range(PAGES_A_STEP) for head in range(heads)]
        asked, valid = [], []
        for part in range(PAGES_A_STEP):
            visit = step * PAGES_A_STEP + part
            place = place_ref[visit]
            asked.append(
                jnp.where(
                    place < half,
                    even_ref[jnp.minimum(place, half - 1)],
                    odd_ref[jnp.maximum(place - half, 0)],
                )
            )
            valid.append(column < fill_ref[visit])
        scores = [
            lax.dot_general(
                asked[part][:, spans[head]],
                leaves[2 * part][0, head],
                (((1,), (1,)), ((), ())),
                preferred_element_type=jnp.float32,
            )
            for part, head in units
        ]
        scores = [
            jnp.where(valid[part], score, NEG_FILL) for (part, head), score in zip(units, scores)
        ]
        tops = [jnp.max(score, axis=1, keepdims=True) for score in scores]
        weights = [
            jnp.where(valid[part], jnp.exp(score - top), 0.0)
            for (part, head), score, top in zip(units, scores, tops)
        ]
        totals = [jnp.sum(weight, axis=1, keepdims=True) for weight in weights]
        sums = [
            jnp.dot(
                weight.astype(jnp.bfloat16),
                leaves[2 * part + 1][0, head],
                preferred_element_type=jnp.float32,
            )
            for (part, head), weight in zip(units, weights)
        ]
        for part in range(PAGES_A_STEP):
            visit = step * PAGES_A_STEP + part
            merge_page(
                visit,
                spans,
                tops[part * heads : (part + 1) * heads],
                totals[part * heads : (part + 1) * heads],
                sums[part * heads : (part + 1) * heads],
                place_ref,
                first_ref,
                last_ref,
                live_ref,
                out_ref,
                log_ref,
                acc_ref,
                top_ref,
                total_ref,
            )


def merge_page(
    visit,
    spans,
    tops,
    totals,
    sums,
    place_ref,
    first_ref,
    last_ref,
    live_ref,
    out_ref,
    log_ref,
    acc_ref,
    top_ref,
    total_ref,
):
    tree = acc_ref.shape[0]
    live = visit < live_ref[0]
    alone = (first_ref[visit] == 1) & (last_ref[visit] == 1)

    def write(tops, totals, sums):
        logs = []
        for span, top, total, value in zip(spans, tops, totals, sums):
            some = total > 0
            safe = jnp.where(some, total, 1.0)
            out_ref[place_ref[visit], :, span] = (value / safe).astype(out_ref.dtype)
            logs.append(jnp.where(some, top + jnp.log(safe), NEG_FILL)[:, :1])
        log_ref[place_ref[visit]] = lay_logs(logs, tree)

    @pl.when(live & alone)
    def _():
        write(tops, totals, sums)

    @pl.when(live & jnp.logical_not(alone))
    def _():
        @pl.when(first_ref[visit] == 1)
        def _():
            acc_ref[...] = jnp.zeros(acc_ref.shape, jnp.float32)
            top_ref[...] = jnp.full(top_ref.shape, NEG_FILL, jnp.float32)
            total_ref[...] = jnp.zeros(total_ref.shape, jnp.float32)

        for head, span in enumerate(spans):
            before = top_ref[head]
            top = jnp.maximum(before, tops[head])
            decay, gain = jnp.exp(before - top), jnp.exp(tops[head] - top)
            top_ref[head] = top
            total_ref[head] = total_ref[head] * decay + totals[head] * gain
            acc_ref[:, span] = acc_ref[:, span] * decay + sums[head] * gain

        @pl.when(last_ref[visit] == 1)
        def _():
            heads = range(len(spans))
            write(
                [top_ref[head] for head in heads],
                [total_ref[head] for head in heads],
                [acc_ref[:, span] for span in spans],
            )


def page_attention(even, odd, k_pages, v_pages, plan, heads, size):
    half, tree, width = even.shape
    requests = 2 * half
    slots, entries = k_pages.shape[0], k_pages.shape[2]
    whole = lambda shape: pl.BlockSpec(shape, lambda p, *rest: (0, 0, 0))

    def leaf(part):
        return pl.BlockSpec(
            (1, heads, entries, size),
            lambda p, page, *rest: (page[p * PAGES_A_STEP + part], 0, 0, 0),
        )

    grid_spec = pltpu.PrefetchScalarGridSpec(
        num_scalar_prefetch=6,
        grid=(slots // PAGES_A_STEP,),
        in_specs=[whole(even.shape), whole(odd.shape)]
        + [leaf(part) for part in range(PAGES_A_STEP) for _ in range(2)],
        out_specs=[whole((requests, tree, width)), whole((requests, 8, LANES))],
        scratch_shapes=[
            pltpu.VMEM((tree, width), jnp.float32),
            pltpu.VMEM((heads, tree, size), jnp.float32),
            pltpu.VMEM((heads, tree, size), jnp.float32),
        ],
    )
    return pl.pallas_call(
        functools.partial(page_kernel, heads, size),
        grid_spec=grid_spec,
        out_shape=[
            jax.ShapeDtypeStruct((requests, tree, width), jnp.bfloat16),
            jax.ShapeDtypeStruct((requests, 8, LANES), jnp.float32),
        ],
        compiler_params=params(20),
        name="page_attention",
    )(*plan, even, odd, *([k_pages, v_pages] * PAGES_A_STEP))


def project_kernel(x_ref, w_ref, out_ref):
    out_ref[...] = jnp.dot(x_ref[...], w_ref[...], preferred_element_type=jnp.float32).astype(
        out_ref.dtype
    )


def project(values, weight):
    rows, depth = values.shape
    columns = weight.shape[1]
    tile = min(columns, 512)
    return pl.pallas_call(
        project_kernel,
        grid=(columns // tile,),
        in_specs=[
            pl.BlockSpec((rows, depth), lambda i: (0, 0)),
            pl.BlockSpec((depth, tile), lambda i: (0, i)),
        ],
        out_specs=pl.BlockSpec((rows, tile), lambda i: (0, i)),
        out_shape=jax.ShapeDtypeStruct((rows, columns), jnp.bfloat16),
        compiler_params=params(8),
        name="project",
    )(values, weight)


def mlp_kernel(steps, tile, x_ref, gate_ref, up_ref, down_ref, out_ref, hidden_ref):
    step = pl.program_id(0)

    @pl.when(step < steps)
    def _():
        gate = jnp.dot(x_ref[...], gate_ref[...], preferred_element_type=jnp.float32)
        up = jnp.dot(x_ref[...], up_ref[...], preferred_element_type=jnp.float32)
        at = pl.ds(pl.multiple_of(step * tile, tile), tile)
        hidden_ref[:, at] = (jax.nn.silu(gate) * up).astype(hidden_ref.dtype)

    @pl.when(step >= steps)
    def _():
        out_ref[...] = jnp.dot(
            hidden_ref[...], down_ref[...], preferred_element_type=jnp.float32
        ).astype(out_ref.dtype)


def mlp(values, gate_up, down):
    rows, width = values.shape
    hidden, columns = down.shape
    tile = min(hidden, 256)
    steps = hidden // tile
    out_tile = min(columns, 256)
    late = lambda i: jnp.maximum(i - steps, 0)
    early = lambda i: jnp.minimum(i, steps - 1)
    return pl.pallas_call(
        functools.partial(mlp_kernel, steps, tile),
        grid=(steps + columns // out_tile,),
        in_specs=[
            pl.BlockSpec((rows, width), lambda i: (0, 0)),
            pl.BlockSpec((width, tile), lambda i: (0, early(i))),
            pl.BlockSpec((width, tile), lambda i: (0, steps + early(i))),
            pl.BlockSpec((hidden, out_tile), lambda i: (0, late(i))),
        ],
        out_specs=pl.BlockSpec((rows, out_tile), lambda i: (0, late(i))),
        out_shape=jax.ShapeDtypeStruct((rows, columns), jnp.bfloat16),
        scratch_shapes=[pltpu.VMEM((rows, hidden), jnp.bfloat16)],
        compiler_params=params(16),
        name="mlp",
    )(values, gate_up, gate_up, down)


def merge_kernel(heads, size, count, *refs):
    sums, logs, out_ref = refs[:count], refs[count : 2 * count], refs[2 * count]
    log_ref = refs[2 * count + 1] if len(refs) > 2 * count + 1 else None
    tree = out_ref.shape[1]
    for request in range(out_ref.shape[0]):
        tables = [ref[request] for ref in logs]
        top = functools.reduce(jnp.maximum, tables)
        total = functools.reduce(lambda a, b: a + b, [jnp.exp(table - top) for table in tables])
        merged = top + jnp.log(total)
        if log_ref is not None:
            log_ref[request] = merged
        shares = [
            jnp.transpose(jnp.where(table > EMPTY, jnp.exp(table - merged), 0.0))
            for table in tables
        ]
        for head in range(heads):
            at = slice(head * size, (head + 1) * size)
            value = jnp.zeros((tree, size), jnp.float32)
            for ref, share in zip(sums, shares):
                factor = share[:tree, head : head + 1]
                term = ref[request, :, at].astype(jnp.float32)
                value = value + jnp.where(factor > 0, term * factor, 0.0)
            out_ref[request, :, at] = value.astype(out_ref.dtype)


def merge_partials(pairs, heads, size, with_logs=True):
    requests, tree, width = pairs[0][0].shape
    group = max(size for size in (1, 2, 4, 8) if requests % size == 0)
    big = pl.BlockSpec((group, tree, width), lambda j: (j, 0, 0))
    small = pl.BlockSpec((group, 8, LANES), lambda j: (j, 0, 0))
    out_specs = [big, small] if with_logs else [big]
    out_shape = [
        jax.ShapeDtypeStruct((requests, tree, width), jnp.bfloat16),
        jax.ShapeDtypeStruct((requests, 8, LANES), jnp.float32),
    ][: len(out_specs)]
    return pl.pallas_call(
        functools.partial(merge_kernel, heads, size, len(pairs)),
        grid=(requests // group,),
        in_specs=[big] * len(pairs) + [small] * len(pairs),
        out_specs=out_specs,
        out_shape=out_shape,
        compiler_params=params(10),
        name="merge_partials",
    )(*[pair[0] for pair in pairs], *[pair[1] for pair in pairs])


def page_plan(owner, fill, first_request, requests, all_local, count):
    slots = owner.shape[0]
    me = lax.axis_index("req")
    source = owner // all_local
    local = owner % all_local - first_request
    mine = (owner >= 0) & (local >= 0) & (local < requests)
    index = source ^ me
    index = (index & 1) * (count // 2) + (index >> 1)
    place = jnp.where(mine, index * requests + local, count * requests)
    spot = jnp.arange(slots, dtype=jnp.int32)
    ahead = (place[None, :] < place[:, None]) | (
        (place[None, :] == place[:, None]) & (spot[None, :] < spot[:, None])
    )
    rank = jnp.sum(ahead.astype(jnp.int32), axis=1)
    live = jnp.sum(mine.astype(jnp.int32))
    wanted = jnp.minimum(spot, jnp.maximum(live - 1, 0))
    chosen = rank[None, :] == wanted[:, None]
    take = lambda values: jnp.sum(jnp.where(chosen, values[None, :], 0), axis=1)
    pages, places, fills = take(spot), take(jnp.where(mine, place, 0)), take(fill)
    changed = (places[1:] != places[:-1]).astype(jnp.int32)
    one = jnp.ones((1,), jnp.int32)
    first = jnp.concatenate([one, changed])
    last = jnp.concatenate([changed, one])
    last = jnp.where(spot == live - 1, 1, last)
    return (pages, places, fills, first, last, live[None])


def on_device(
    streams,
    hc_in,
    hc_mix,
    hc_out,
    qkv_weight,
    out_weight,
    up_gate,
    down_weight,
    draft_weight,
    lm_head,
    k_pages,
    v_pages,
    page_owner,
    page_fill,
    cache_len,
    tree_parent,
    accepted_index,
):
    tokens_local = streams.shape[0]
    stream_count = streams.shape[1]
    feature_local = streams.shape[2]
    width = qkv_weight.shape[0]
    req_local = cache_len.shape[0]
    tree_size = tree_parent.shape[1]
    heads = k_pages.shape[2]
    size = k_pages.shape[3]
    draft_count = draft_weight.shape[0]
    parts = lax.axis_size("req")
    all_requests = req_local * parts

    identity = jnp.eye(stream_count, dtype=jnp.float32)
    first_mix, second_mix = identity + hc_mix[0], identity + hc_mix[1]
    mid_in = jnp.sum(first_mix * hc_in[1][None, :], axis=1)
    mid_out = jnp.sum(hc_out[0] * hc_in[1])
    both_mix = jnp.sum(first_mix[:, :, None] * second_mix[None, :, :], axis=1)
    both_out = jnp.sum(hc_out[0][:, None] * second_mix, axis=0)

    reach = ancestors(tree_parent)
    depth = (jnp.sum(reach, axis=2) - 1.0).astype(jnp.int32)
    positions = (cache_len[:, None] + depth).reshape(tokens_local)
    half = size // 2
    freqs = jnp.exp(jnp.arange(half, dtype=jnp.float32) * (-2.0 * math.log(10000.0) / size))
    angles = positions.astype(jnp.float32)[:, None] * freqs[None, :]
    cosine, sine = jnp.cos(angles), jnp.sin(angles)
    cosine = jnp.concatenate([cosine, cosine], axis=1)
    sine = jnp.concatenate([-sine, sine], axis=1)

    k_heads = jnp.transpose(k_pages, (0, 2, 1, 3))
    v_heads = jnp.transpose(v_pages, (0, 2, 1, 3))

    step_requests = req_local // CHUNKS
    step_tokens = step_requests * tree_size
    merge = lambda ours, got: merge_flat(ours, got, heads, size)

    gate_up = up_gate.reshape(width, -1)
    token = None
    first_shares = None
    before_normed = None
    attended_in = []
    for chunk in range(CHUNKS):
        rows = slice(chunk * step_tokens, (chunk + 1) * step_tokens)
        stream_vals = streams[rows].astype(jnp.float32)
        mixed_in = blend(stream_vals, hc_in[0])
        normed, token, sent = gathered_norm(mixed_in, width, token)
        if chunk == 0:
            normed, k_heads, v_heads, gate_up = lax.optimization_barrier(
                (normed, k_heads, v_heads, gate_up)
            )
        attended_in.append(normed)

    all_shape = (step_requests, tree_size, heads * size)
    before_queries = None
    attn_parts, mlp_parts = [], []
    for chunk in range(CHUNKS):
        rows = slice(chunk * step_tokens, (chunk + 1) * step_tokens)
        asked = slice(chunk * step_requests, (chunk + 1) * step_requests)
        normed = attended_in[chunk]
        if before_normed is not None:
            normed, before_normed = lax.optimization_barrier((normed, before_normed))
        thirds = [
            jnp.dot(normed, qkv_weight[:, third], preferred_element_type=jnp.float32)
            for third in range(3)
        ]
        queries, keys, values = rotate_all(
            thirds, cosine[rows], sine[rows], heads, size, 2 * tree_size
        )
        queries, keys, values = (item.reshape(all_shape) for item in (queries, keys, values))
        if before_queries is not None:
            queries, before_queries = lax.optimization_barrier((queries, before_queries))
        even, odd = gather_requests(queries)
        plan = page_plan(
            page_owner, page_fill, chunk * step_requests, step_requests, req_local, parts
        )
        sums, logs = page_attention(even, odd, k_heads, v_heads, plan, heads, size)
        keys, sums, logs = lax.optimization_barrier((keys, sums, logs))
        tree_pair = tree_attention(queries, keys, values, reach[asked], heads, size)
        done, before_normed = scatter_requests(
            sums.reshape((parts,) + all_shape),
            logs.reshape(parts, step_requests, 8, LANES),
            merge,
        )
        part_requests = step_requests // 2
        attended = []
        for part, (ours, got) in enumerate(done):
            own = slice(part * part_requests, (part + 1) * part_requests)
            pairs = [
                tuple(value.reshape((-1,) + value.shape[2:]) for value in pair)
                for pair in (ours, got)
            ] + [(tree_pair[0][own], tree_pair[1][own])]
            attended.append(merge_partials(pairs, heads, size, with_logs=False)[0])
        attended = jnp.concatenate(attended).reshape(step_tokens, heads * size)
        before_queries = attended
        attn_delta = scatter_columns(project(attended, out_weight))
        if first_shares is not None:
            attn_delta, first_shares = lax.optimization_barrier((attn_delta, first_shares))
        attn_parts.append(attn_delta)

        stream_vals = streams[rows].astype(jnp.float32)
        mixed_mid = blend(stream_vals, mid_in) + mid_out * attn_delta
        normed_mid, gathered, sent_mid = gathered_norm(mixed_mid, width)
        shares = mlp(normed_mid, gate_up, down_weight)
        if first_shares is None:
            first_shares = shares
        else:
            first_shares, sent_mid = lax.optimization_barrier((first_shares, sent_mid))
            mlp_parts.append(scatter_columns(first_shares))
            last_shares = shares
            mlp_parts.append(scatter_columns(shares))

    rows_taken = jnp.arange(req_local, dtype=jnp.int32) * tree_size + accepted_index
    stream_rows = streams[rows_taken].astype(jnp.float32)
    is_taken = jnp.arange(tree_size, dtype=jnp.int32)[None, :] == accepted_index[:, None]
    attn_rows = jnp.concatenate(
        [
            jnp.sum(
                jnp.where(
                    is_taken[chunk * step_requests : (chunk + 1) * step_requests, :, None],
                    part.reshape(step_requests, tree_size, feature_local),
                    0.0,
                ),
                axis=1,
            )
            for chunk, part in enumerate(attn_parts)
        ]
    )
    mid_rows = blend(stream_rows, mid_in) + mid_out * attn_rows
    mid_full = jnp.concatenate(list(shift_gather(mid_rows)), axis=1)
    mid_full, first_shares = lax.optimization_barrier((mid_full, first_shares))
    mlp_rows = shift_scatter(
        mlp(layer_norm(mid_full).astype(jnp.bfloat16), gate_up, down_weight)
    )
    final_local = (
        jnp.sum(both_out) * attn_rows + jnp.sum(hc_out[1]) * mlp_rows
    ) + blend(stream_rows, jnp.sum(both_mix, axis=1))
    final_full = jnp.concatenate(list(shift_gather(final_local)), axis=1)
    final_full, last_shares = lax.optimization_barrier((final_full, last_shares))
    final_norm = layer_norm(final_full)
    attn_delta = jnp.concatenate(attn_parts)
    mlp_delta = jnp.concatenate(mlp_parts)
    stream_vals = streams.astype(jnp.float32)
    new_streams = both_out[None, :, None] * attn_delta[:, None] + (
        hc_out[1][None, :, None] * mlp_delta[:, None]
    )
    for index in range(stream_count):
        new_streams = (
            new_streams + both_mix[index][None, :, None] * stream_vals[:, index : index + 1]
        )
    new_streams = new_streams.astype(jnp.bfloat16)

    own_columns = lax.dynamic_slice_in_dim(
        final_norm, lax.axis_index("head") * feature_local, feature_local, 1
    )
    branch = jnp.einsum(
        "jd,kde->jke",
        final_norm.astype(jnp.bfloat16),
        draft_weight,
        preferred_element_type=jnp.float32,
    )
    drafted = (own_columns[:, None, :] + jax.nn.silu(branch)).astype(jnp.bfloat16)
    draft_full = jnp.concatenate(list(shift_gather(drafted)), axis=2)
    draft_all = gather_small(draft_full)
    logits_local = jnp.dot(
        draft_all.reshape(-1, width), lm_head, preferred_element_type=jnp.float32
    )
    logits_local = logits_local.reshape(all_requests, draft_count, -1)
    logits = lax.all_to_all(
        logits_local.astype(jnp.bfloat16), ("req", "head"), split_axis=0, concat_axis=2, tiled=True
    ).astype(logits_local.dtype)
    return (new_streams, logits)


def merge_flat(ours, got, heads, size):
    lead = ours[0].shape[:2]
    pairs = [
        tuple(value.reshape((-1,) + value.shape[2:]) for value in pair) for pair in (ours, got)
    ]
    merged = merge_partials(pairs, heads, size)
    return [value.reshape(lead + value.shape[1:]) for value in merged]


def solution(mesh):
    in_specs = (
        P("req", None, "head"),
        P(),
        P(),
        P(),
        P(None, None, "head"),
        P("head", None),
        P(None, None, "head"),
        P("head", None),
        P(None, None, "head"),
        P(None, ("req", "head")),
        P("req", None, "head", None),
        P("req", None, "head", None),
        P("req"),
        P("req"),
        P("req"),
        P("req", None),
        P("req"),
    )
    out_specs = (P("req", None, "head"), P(("req", "head"), None, None))
    return jax.shard_map(
        on_device, mesh=mesh, in_specs=in_specs, out_specs=out_specs, check_vma=False
    )
```

```python
import functools
import math

import jax
import jax.numpy as jnp
from jax import lax
from jax.experimental import pallas as pl
from jax.experimental.pallas import tpu as pltpu
from jax.sharding import PartitionSpec as P

NEG_FILL = -1e30
EMPTY = -1e29
PRECISE = lax.Precision.HIGHEST
CHUNKS = 2
LANES = 128
PAGES_A_STEP = 2
MIB = 1024 * 1024


def params(mebibytes):
    return pltpu.CompilerParams(
        dimension_semantics=("arbitrary",), vmem_limit_bytes=mebibytes * MIB
    )


def ancestors(parents):
    length = parents.shape[1]
    places = jnp.arange(length, dtype=jnp.int32)
    linked = (parents[:, :, None] == places[None, None, :]) | (places[:, None] == places[None, :])[
        None
    ]
    reach = linked.astype(jnp.float32)
    for repeat in range(max(1, (length - 1).bit_length())):
        reach = jnp.minimum(jnp.einsum("jik,jkl->jil", reach, reach, precision=PRECISE), 1.0)
    return reach


def layer_norm(values):
    center = jnp.mean(values, axis=-1, keepdims=True)
    square = jnp.mean(values * values, axis=-1, keepdims=True)
    return (values - center) * lax.rsqrt(square - center * center + 1e-05)


def blend(stream_vals, weights):
    total = weights[0] * stream_vals[:, 0]
    for index in range(1, stream_vals.shape[1]):
        total = total + weights[index] * stream_vals[:, index]
    return total


def shift_gather(small):
    count = lax.axis_size("head")
    rank = lax.axis_index("head")
    parts = [small] + [
        lax.ppermute(small, "head", [(z, (z + step) % count) for z in range(count)])
        for step in range(1, count)
    ]
    stacked = jnp.stack(parts)
    return jnp.stack(
        [
            lax.dynamic_index_in_dim(stacked, (rank - source) % count, 0, keepdims=False)
            for source in range(count)
        ]
    )


def shift_scatter(shares):
    count = lax.axis_size("head")
    rank = lax.axis_index("head")
    width = shares.shape[1] // count
    total = None
    for step in range(count):
        block = lax.dynamic_slice_in_dim(shares, (rank + step) % count * width, width, 1)
        if step:
            block = lax.ppermute(block, "head", [(z, (z + step) % count) for z in range(count)])
        block = block.astype(jnp.float32)
        total = block if total is None else total + block
    return total


def gathered_norm(values, width, after=None):
    local = values.shape[1]
    sums = jnp.sum(values, axis=1)
    squares = jnp.sum(values * values, axis=1)
    center = sums / local
    sent = (values - center[:, None]).astype(jnp.bfloat16)
    stats = shift_gather(jnp.stack([sums, squares]))
    if after is not None:
        sent, after = lax.optimization_barrier((sent, after))
    gathered = lax.all_gather(sent, "head", axis=1, tiled=True)
    mean = jnp.sum(stats[:, 0], axis=0) / width
    variance = jnp.sum(stats[:, 1], axis=0) / width - mean * mean
    scale = lax.rsqrt(variance + 1e-05)

    def finish(gathered):
        normed = [
            (
                (
                    gathered[:, rank * local : (rank + 1) * local].astype(jnp.float32)
                    + (stats[rank, 0] / local - mean)[:, None]
                )
                * scale[:, None]
            ).astype(jnp.bfloat16)
            for rank in range(lax.axis_size("head"))
        ]
        return jnp.concatenate(normed, axis=1)

    return gathered, finish, sent


def scatter_columns(shares):
    return lax.psum_scatter(shares, "head", scatter_dimension=1, tiled=True).astype(jnp.float32)


def swapped(values, bit):
    count = lax.axis_size("req")
    return lax.ppermute(values, "req", [(r, r ^ bit) for r in range(count)])


def bit_orders():
    bits = [1 << index for index in range((lax.axis_size("req") - 1).bit_length())]
    return bits[0], (bits[1:], bits[1:][::-1])


def gather_requests(values):
    half = values.shape[0] // 2
    near, orders = bit_orders()
    parts = []
    for part, order in enumerate(orders):
        blocks = {0: values[part * half : (part + 1) * half]}
        for bit in order:
            for index in list(blocks):
                blocks[index ^ bit] = swapped(blocks[index], bit)
        parts.append(blocks)
    even = jnp.concatenate([blocks[index] for index in sorted(parts[0]) for blocks in parts])
    return even, swapped(even, near)


def gather_small(values):
    count = lax.axis_size("req")
    near, orders = bit_orders()
    stacked = values[None]
    bits = []
    for bit in list(orders[0]) + [near]:
        stacked = jnp.concatenate([stacked, swapped(stacked, bit)])
        bits.append(bit)
    index = lax.axis_index("req") ^ jnp.arange(count, dtype=jnp.int32)
    place = jnp.zeros_like(index)
    for spot, bit in enumerate(bits):
        place = place + jnp.where((index & bit) != 0, 1 << spot, 0)
    return stacked[place]


def scatter_requests(sums, logs, merge):
    near, orders = bit_orders()
    count = lax.axis_size("req")
    far = count // 2
    state = []
    mine = [sums[:far], logs[:far]]
    theirs = [swapped(sums[far:], near), swapped(logs[far:], near)]
    merged = first_merged = merge(mine, theirs)
    half = sums.shape[1] // 2
    done = []
    for part, order in enumerate(orders):
        kept = [value[:, part * half : (part + 1) * half] for value in merged]
        places = list(range(far))
        for place, bit in enumerate(order):
            stay = [at for at, index in enumerate(places) if not index & (bit >> 1)]
            leave = [at for at, index in enumerate(places) if index & (bit >> 1)]
            pick = lambda value, which: jnp.concatenate([value[at : at + 1] for at in which])
            ours = [pick(value, stay) for value in kept]
            got = [swapped(pick(value, leave), bit) for value in kept]
            places = [places[at] for at in stay]
            kept = merge(ours, got) if place < len(order) - 1 else (ours, got)
        done.append(kept)
    return done, first_merged[1]


def rotate_kernel(heads, size, scale, x_ref, y_ref, z_ref, cos_ref, sin_ref, q_ref, k_ref, v_ref):
    cosine, sine = cos_ref[...], sin_ref[...]
    for head in range(heads):
        at = slice(head * size, (head + 1) * size)
        for in_ref, out_ref, factor in ((x_ref, q_ref, scale), (y_ref, k_ref, 1.0)):
            values = in_ref[:, at]
            turned = values * cosine + pltpu.roll(values, size // 2, 1) * sine
            out_ref[:, at] = (turned * factor).astype(out_ref.dtype)
    v_ref[...] = z_ref[...].astype(v_ref.dtype)


def rotate_all(thirds, cosine, sine, heads, size, rows):
    tokens, width = thirds[0].shape
    out = jax.ShapeDtypeStruct((tokens, width), jnp.bfloat16)
    block = lambda lanes: pl.BlockSpec((rows, lanes), lambda i: (i, 0))
    return pl.pallas_call(
        functools.partial(rotate_kernel, heads, size, size ** (-0.5)),
        grid=(tokens // rows,),
        in_specs=[block(width)] * 3 + [block(size)] * 2,
        out_specs=[block(width)] * 3,
        out_shape=[out] * 3,
        compiler_params=params(8),
        name="rotate",
    )(*thirds, cosine, sine)


def lay_logs(columns, rows):
    lane = lax.broadcasted_iota(jnp.int32, (LANES, LANES), 1)
    table = jnp.full((LANES, LANES), NEG_FILL, jnp.float32)
    for head, column in enumerate(columns):
        tall = jnp.concatenate(
            [column, jnp.full((LANES - rows, 1), NEG_FILL, jnp.float32)], axis=0
        )
        table = jnp.where(lane == head, tall, table)
    return jnp.transpose(table)[:8]


def tree_kernel(heads, size, q_ref, k_ref, v_ref, reach_ref, out_ref, log_ref):
    seen = reach_ref[0] > 0
    logs = []
    for head in range(heads):
        at = slice(head * size, (head + 1) * size)
        scores = lax.dot_general(
            q_ref[0, :, at],
            k_ref[0, :, at],
            (((1,), (1,)), ((), ())),
            preferred_element_type=jnp.float32,
        )
        scores = jnp.where(seen, scores, NEG_FILL)
        top = jnp.max(scores, axis=1, keepdims=True)
        weights = jnp.where(seen, jnp.exp(scores - top), 0.0)
        total = jnp.sum(weights, axis=1, keepdims=True)
        summed = jnp.dot(
            weights.astype(jnp.bfloat16), v_ref[0, :, at], preferred_element_type=jnp.float32
        )
        out_ref[0, :, at] = summed / total
        logs.append(top + jnp.log(total))
    log_ref[0] = lay_logs(logs, q_ref.shape[1])


def tree_attention(queries, keys, values, reach, heads, size):
    requests, tree, width = queries.shape
    block = pl.BlockSpec((1, tree, width), lambda j: (j, 0, 0))
    return pl.pallas_call(
        functools.partial(tree_kernel, heads, size),
        grid=(requests,),
        in_specs=[block] * 3 + [pl.BlockSpec((1, tree, tree), lambda j: (j, 0, 0))],
        out_specs=[block, pl.BlockSpec((1, 8, LANES), lambda j: (j, 0, 0))],
        out_shape=[
            jax.ShapeDtypeStruct((requests, tree, width), jnp.float32),
            jax.ShapeDtypeStruct((requests, 8, LANES), jnp.float32),
        ],
        compiler_params=params(8),
        name="tree_attention",
    )(queries, keys, values, reach)


def page_kernel(
    heads,
    size,
    page_ref,
    place_ref,
    fill_ref,
    first_ref,
    last_ref,
    live_ref,
    even_ref,
    odd_ref,
    *refs,
):
    leaves = refs[: 2 * PAGES_A_STEP]
    out_ref, log_ref, acc_ref, top_ref, total_ref = refs[2 * PAGES_A_STEP :]
    step = pl.program_id(0)
    half, tree = even_ref.shape[:2]
    spans = [slice(head * size, (head + 1) * size) for head in range(heads)]
    entries = leaves[0].shape[2]

    @pl.when(step == 0)
    def _():
        log_ref[...] = jnp.full(log_ref.shape, NEG_FILL, jnp.float32)

    @pl.when(step * PAGES_A_STEP < live_ref[0])
    def _():
        column = lax.broadcasted_iota(jnp.int32, (tree, entries), 1)
        units = [(part, head) for part in range(PAGES_A_STEP) for head in range(heads)]
        asked, valid = [], []
        for part in range(PAGES_A_STEP):
            visit = step * PAGES_A_STEP + part
            place = place_ref[visit]
            asked.append(
                jnp.where(
                    place < half,
                    even_ref[jnp.minimum(place, half - 1)],
                    odd_ref[jnp.maximum(place - half, 0)],
                )
            )
            valid.append(column < fill_ref[visit])
        scores = [
            lax.dot_general(
                asked[part][:, spans[head]],
                leaves[2 * part][0, head],
                (((1,), (1,)), ((), ())),
                preferred_element_type=jnp.float32,
            )
            for part, head in units
        ]
        scores = [
            jnp.where(valid[part], score, NEG_FILL) for (part, head), score in zip(units, scores)
        ]
        tops = [jnp.max(score, axis=1, keepdims=True) for score in scores]
        weights = [
            jnp.where(valid[part], jnp.exp(score - top), 0.0)
            for (part, head), score, top in zip(units, scores, tops)
        ]
        totals = [jnp.sum(weight, axis=1, keepdims=True) for weight in weights]
        sums = [
            jnp.dot(
                weight.astype(jnp.bfloat16),
                leaves[2 * part + 1][0, head],
                preferred_element_type=jnp.float32,
            )
            for (part, head), weight in zip(units, weights)
        ]
        for part in range(PAGES_A_STEP):
            visit = step * PAGES_A_STEP + part
            merge_page(
                visit,
                spans,
                tops[part * heads : (part + 1) * heads],
                totals[part * heads : (part + 1) * heads],
                sums[part * heads : (part + 1) * heads],
                place_ref,
                first_ref,
                last_ref,
                live_ref,
                out_ref,
                log_ref,
                acc_ref,
                top_ref,
                total_ref,
            )


def merge_page(
    visit,
    spans,
    tops,
    totals,
    sums,
    place_ref,
    first_ref,
    last_ref,
    live_ref,
    out_ref,
    log_ref,
    acc_ref,
    top_ref,
    total_ref,
):
    tree = acc_ref.shape[0]
    live = visit < live_ref[0]
    alone = (first_ref[visit] == 1) & (last_ref[visit] == 1)

    def write(tops, totals, sums):
        logs = []
        for span, top, total, value in zip(spans, tops, totals, sums):
            some = total > 0
            safe = jnp.where(some, total, 1.0)
            out_ref[place_ref[visit], :, span] = (value / safe).astype(out_ref.dtype)
            logs.append(jnp.where(some, top + jnp.log(safe), NEG_FILL)[:, :1])
        log_ref[place_ref[visit]] = lay_logs(logs, tree)

    @pl.when(live & alone)
    def _():
        write(tops, totals, sums)

    @pl.when(live & jnp.logical_not(alone))
    def _():
        @pl.when(first_ref[visit] == 1)
        def _():
            acc_ref[...] = jnp.zeros(acc_ref.shape, jnp.float32)
            top_ref[...] = jnp.full(top_ref.shape, NEG_FILL, jnp.float32)
            total_ref[...] = jnp.zeros(total_ref.shape, jnp.float32)

        for head, span in enumerate(spans):
            before = top_ref[head]
            top = jnp.maximum(before, tops[head])
            decay, gain = jnp.exp(before - top), jnp.exp(tops[head] - top)
            top_ref[head] = top
            total_ref[head] = total_ref[head] * decay + totals[head] * gain
            acc_ref[:, span] = acc_ref[:, span] * decay + sums[head] * gain

        @pl.when(last_ref[visit] == 1)
        def _():
            heads = range(len(spans))
            write(
                [top_ref[head] for head in heads],
                [total_ref[head] for head in heads],
                [acc_ref[:, span] for span in spans],
            )


def page_attention(even, odd, k_pages, v_pages, plan, heads, size):
    half, tree, width = even.shape
    requests = 2 * half
    slots, entries = k_pages.shape[0], k_pages.shape[2]
    whole = lambda shape: pl.BlockSpec(shape, lambda p, *rest: (0, 0, 0))

    def leaf(part):
        return pl.BlockSpec(
            (1, heads, entries, size),
            lambda p, page, *rest: (page[p * PAGES_A_STEP + part], 0, 0, 0),
        )

    grid_spec = pltpu.PrefetchScalarGridSpec(
        num_scalar_prefetch=6,
        grid=(slots // PAGES_A_STEP,),
        in_specs=[whole(even.shape), whole(odd.shape)]
        + [leaf(part) for part in range(PAGES_A_STEP) for _ in range(2)],
        out_specs=[whole((requests, tree, width)), whole((requests, 8, LANES))],
        scratch_shapes=[
            pltpu.VMEM((tree, width), jnp.float32),
            pltpu.VMEM((heads, tree, size), jnp.float32),
            pltpu.VMEM((heads, tree, size), jnp.float32),
        ],
    )
    return pl.pallas_call(
        functools.partial(page_kernel, heads, size),
        grid_spec=grid_spec,
        out_shape=[
            jax.ShapeDtypeStruct((requests, tree, width), jnp.bfloat16),
            jax.ShapeDtypeStruct((requests, 8, LANES), jnp.float32),
        ],
        compiler_params=params(20),
        name="page_attention",
    )(*plan, even, odd, *([k_pages, v_pages] * PAGES_A_STEP))


def project_kernel(x_ref, w_ref, out_ref):
    out_ref[...] = jnp.dot(x_ref[...], w_ref[...], preferred_element_type=jnp.float32).astype(
        out_ref.dtype
    )


def project(values, weight):
    rows, depth = values.shape
    columns = weight.shape[1]
    tile = min(columns, 512)
    return pl.pallas_call(
        project_kernel,
        grid=(columns // tile,),
        in_specs=[
            pl.BlockSpec((rows, depth), lambda i: (0, 0)),
            pl.BlockSpec((depth, tile), lambda i: (0, i)),
        ],
        out_specs=pl.BlockSpec((rows, tile), lambda i: (0, i)),
        out_shape=jax.ShapeDtypeStruct((rows, columns), jnp.bfloat16),
        compiler_params=params(8),
        name="project",
    )(values, weight)


def mlp_kernel(steps, tile, x_ref, gate_ref, up_ref, down_ref, out_ref, hidden_ref):
    step = pl.program_id(0)

    @pl.when(step < steps)
    def _():
        gate = jnp.dot(x_ref[...], gate_ref[...], preferred_element_type=jnp.float32)
        up = jnp.dot(x_ref[...], up_ref[...], preferred_element_type=jnp.float32)
        at = pl.ds(pl.multiple_of(step * tile, tile), tile)
        hidden_ref[:, at] = (jax.nn.silu(gate) * up).astype(hidden_ref.dtype)

    @pl.when(step >= steps)
    def _():
        out_ref[...] = jnp.dot(
            hidden_ref[...], down_ref[...], preferred_element_type=jnp.float32
        ).astype(out_ref.dtype)


def mlp(values, gate_up, down):
    rows, width = values.shape
    hidden, columns = down.shape
    tile = min(hidden, 256)
    steps = hidden // tile
    out_tile = min(columns, 256)
    late = lambda i: jnp.maximum(i - steps, 0)
    early = lambda i: jnp.minimum(i, steps - 1)
    return pl.pallas_call(
        functools.partial(mlp_kernel, steps, tile),
        grid=(steps + columns // out_tile,),
        in_specs=[
            pl.BlockSpec((rows, width), lambda i: (0, 0)),
            pl.BlockSpec((width, tile), lambda i: (0, early(i))),
            pl.BlockSpec((width, tile), lambda i: (0, steps + early(i))),
            pl.BlockSpec((hidden, out_tile), lambda i: (0, late(i))),
        ],
        out_specs=pl.BlockSpec((rows, out_tile), lambda i: (0, late(i))),
        out_shape=jax.ShapeDtypeStruct((rows, columns), jnp.bfloat16),
        scratch_shapes=[pltpu.VMEM((rows, hidden), jnp.bfloat16)],
        compiler_params=params(56),
        name="mlp",
    )(values, gate_up, gate_up, down)


def merge_kernel(heads, size, count, *refs):
    sums, logs, out_ref = refs[:count], refs[count : 2 * count], refs[2 * count]
    log_ref = refs[2 * count + 1] if len(refs) > 2 * count + 1 else None
    tree = out_ref.shape[1]
    for request in range(out_ref.shape[0]):
        tables = [ref[request] for ref in logs]
        top = functools.reduce(jnp.maximum, tables)
        total = functools.reduce(lambda a, b: a + b, [jnp.exp(table - top) for table in tables])
        merged = top + jnp.log(total)
        if log_ref is not None:
            log_ref[request] = merged
        shares = [
            jnp.transpose(jnp.where(table > EMPTY, jnp.exp(table - merged), 0.0))
            for table in tables
        ]
        for head in range(heads):
            at = slice(head * size, (head + 1) * size)
            value = jnp.zeros((tree, size), jnp.float32)
            for ref, share in zip(sums, shares):
                factor = share[:tree, head : head + 1]
                term = ref[request, :, at].astype(jnp.float32)
                value = value + jnp.where(factor > 0, term * factor, 0.0)
            out_ref[request, :, at] = value.astype(out_ref.dtype)


def merge_partials(pairs, heads, size, with_logs=True):
    requests, tree, width = pairs[0][0].shape
    group = max(size for size in (1, 2, 4, 8) if requests % size == 0)
    big = pl.BlockSpec((group, tree, width), lambda j: (j, 0, 0))
    small = pl.BlockSpec((group, 8, LANES), lambda j: (j, 0, 0))
    out_specs = [big, small] if with_logs else [big]
    out_shape = [
        jax.ShapeDtypeStruct((requests, tree, width), jnp.bfloat16),
        jax.ShapeDtypeStruct((requests, 8, LANES), jnp.float32),
    ][: len(out_specs)]
    return pl.pallas_call(
        functools.partial(merge_kernel, heads, size, len(pairs)),
        grid=(requests // group,),
        in_specs=[big] * len(pairs) + [small] * len(pairs),
        out_specs=out_specs,
        out_shape=out_shape,
        compiler_params=params(10),
        name="merge_partials",
    )(*[pair[0] for pair in pairs], *[pair[1] for pair in pairs])


def page_plan(owner, fill, first_request, requests, all_local, count):
    slots = owner.shape[0]
    me = lax.axis_index("req")
    source = owner // all_local
    local = owner % all_local - first_request
    mine = (owner >= 0) & (local >= 0) & (local < requests)
    index = source ^ me
    index = (index & 1) * (count // 2) + (index >> 1)
    place = jnp.where(mine, index * requests + local, count * requests)
    spot = jnp.arange(slots, dtype=jnp.int32)
    ahead = (place[None, :] < place[:, None]) | (
        (place[None, :] == place[:, None]) & (spot[None, :] < spot[:, None])
    )
    rank = jnp.sum(ahead.astype(jnp.int32), axis=1)
    live = jnp.sum(mine.astype(jnp.int32))
    wanted = jnp.minimum(spot, jnp.maximum(live - 1, 0))
    chosen = rank[None, :] == wanted[:, None]
    take = lambda values: jnp.sum(jnp.where(chosen, values[None, :], 0), axis=1)
    pages, places, fills = take(spot), take(jnp.where(mine, place, 0)), take(fill)
    changed = (places[1:] != places[:-1]).astype(jnp.int32)
    one = jnp.ones((1,), jnp.int32)
    first = jnp.concatenate([one, changed])
    last = jnp.concatenate([changed, one])
    last = jnp.where(spot == live - 1, 1, last)
    return (pages, places, fills, first, last, live[None])


def on_device(
    streams,
    hc_in,
    hc_mix,
    hc_out,
    qkv_weight,
    out_weight,
    up_gate,
    down_weight,
    draft_weight,
    lm_head,
    k_pages,
    v_pages,
    page_owner,
    page_fill,
    cache_len,
    tree_parent,
    accepted_index,
):
    tokens_local = streams.shape[0]
    stream_count = streams.shape[1]
    feature_local = streams.shape[2]
    width = qkv_weight.shape[0]
    req_local = cache_len.shape[0]
    tree_size = tree_parent.shape[1]
    heads = k_pages.shape[2]
    size = k_pages.shape[3]
    draft_count = draft_weight.shape[0]
    parts = lax.axis_size("req")
    all_requests = req_local * parts

    identity = jnp.eye(stream_count, dtype=jnp.float32)
    first_mix, second_mix = identity + hc_mix[0], identity + hc_mix[1]
    mid_in = jnp.sum(first_mix * hc_in[1][None, :], axis=1)
    mid_out = jnp.sum(hc_out[0] * hc_in[1])
    both_mix = jnp.sum(first_mix[:, :, None] * second_mix[None, :, :], axis=1)
    both_out = jnp.sum(hc_out[0][:, None] * second_mix, axis=0)

    reach = ancestors(tree_parent)
    depth = (jnp.sum(reach, axis=2) - 1.0).astype(jnp.int32)
    positions = (cache_len[:, None] + depth).reshape(tokens_local)
    half = size // 2
    freqs = jnp.exp(jnp.arange(half, dtype=jnp.float32) * (-2.0 * math.log(10000.0) / size))
    angles = positions.astype(jnp.float32)[:, None] * freqs[None, :]
    cosine, sine = jnp.cos(angles), jnp.sin(angles)
    cosine = jnp.concatenate([cosine, cosine], axis=1)
    sine = jnp.concatenate([-sine, sine], axis=1)

    k_heads = jnp.transpose(k_pages, (0, 2, 1, 3))
    v_heads = jnp.transpose(v_pages, (0, 2, 1, 3))

    step_requests = req_local // CHUNKS
    step_tokens = step_requests * tree_size
    merge = lambda ours, got: merge_flat(ours, got, heads, size)

    gate_up = up_gate.reshape(width, -1)
    token = None
    first_shares = None
    before_normed = None
    attended_in = []
    for chunk in range(CHUNKS):
        rows = slice(chunk * step_tokens, (chunk + 1) * step_tokens)
        stream_vals = streams[rows].astype(jnp.float32)
        mixed_in = blend(stream_vals, hc_in[0])
        token, finish, sent = gathered_norm(mixed_in, width, token)
        attended_in.append((token, finish))

    all_shape = (step_requests, tree_size, heads * size)
    before_queries = None
    attn_parts, mlp_parts = [], []
    for chunk in range(CHUNKS):
        rows = slice(chunk * step_tokens, (chunk + 1) * step_tokens)
        asked = slice(chunk * step_requests, (chunk + 1) * step_requests)
        gathered, finish = attended_in[chunk]
        if before_normed is None:
            normed, k_heads, v_heads, gate_up = lax.optimization_barrier(
                (finish(gathered), k_heads, v_heads, gate_up)
            )
        else:
            gathered, before_normed = lax.optimization_barrier((gathered, before_normed))
            normed = finish(gathered)
        thirds = [
            jnp.dot(normed, qkv_weight[:, third], preferred_element_type=jnp.float32)
            for third in range(3)
        ]
        queries, keys, values = rotate_all(
            thirds, cosine[rows], sine[rows], heads, size, 2 * tree_size
        )
        queries, keys, values = (item.reshape(all_shape) for item in (queries, keys, values))
        if before_queries is not None:
            queries, before_queries = lax.optimization_barrier((queries, before_queries))
        even, odd = gather_requests(queries)
        plan = page_plan(
            page_owner, page_fill, chunk * step_requests, step_requests, req_local, parts
        )
        sums, logs = page_attention(even, odd, k_heads, v_heads, plan, heads, size)
        keys, sums, logs = lax.optimization_barrier((keys, sums, logs))
        tree_pair = tree_attention(queries, keys, values, reach[asked], heads, size)
        done, before_normed = scatter_requests(
            sums.reshape((parts,) + all_shape),
            logs.reshape(parts, step_requests, 8, LANES),
            merge,
        )
        part_requests = step_requests // 2
        attended = []
        for part, (ours, got) in enumerate(done):
            own = slice(part * part_requests, (part + 1) * part_requests)
            pairs = [
                tuple(value.reshape((-1,) + value.shape[2:]) for value in pair)
                for pair in (ours, got)
            ] + [(tree_pair[0][own], tree_pair[1][own])]
            attended.append(merge_partials(pairs, heads, size, with_logs=False)[0])
        attended = jnp.concatenate(attended).reshape(step_tokens, heads * size)
        before_queries = attended
        attn_delta = scatter_columns(project(attended, out_weight))
        if first_shares is not None:
            attn_delta, first_shares = lax.optimization_barrier((attn_delta, first_shares))
        attn_parts.append(attn_delta)

        stream_vals = streams[rows].astype(jnp.float32)
        mixed_mid = blend(stream_vals, mid_in) + mid_out * attn_delta
        gathered, finish, sent_mid = gathered_norm(mixed_mid, width)
        normed_mid = finish(gathered)
        shares = mlp(normed_mid, gate_up, down_weight)
        if first_shares is None:
            first_shares = shares
        else:
            first_shares, sent_mid = lax.optimization_barrier((first_shares, sent_mid))
            mlp_parts.append(scatter_columns(first_shares))
            last_shares = shares
            mlp_parts.append(scatter_columns(shares))

    rows_taken = jnp.arange(req_local, dtype=jnp.int32) * tree_size + accepted_index
    stream_rows = streams[rows_taken].astype(jnp.float32)
    is_taken = jnp.arange(tree_size, dtype=jnp.int32)[None, :] == accepted_index[:, None]
    attn_rows = jnp.concatenate(
        [
            jnp.sum(
                jnp.where(
                    is_taken[chunk * step_requests : (chunk + 1) * step_requests, :, None],
                    part.reshape(step_requests, tree_size, feature_local),
                    0.0,
                ),
                axis=1,
            )
            for chunk, part in enumerate(attn_parts)
        ]
    )
    mid_rows = blend(stream_rows, mid_in) + mid_out * attn_rows
    mid_full = jnp.concatenate(list(shift_gather(mid_rows)), axis=1)
    mid_full, first_shares = lax.optimization_barrier((mid_full, first_shares))
    mlp_rows = shift_scatter(
        mlp(layer_norm(mid_full).astype(jnp.bfloat16), gate_up, down_weight)
    )
    final_local = (
        jnp.sum(both_out) * attn_rows + jnp.sum(hc_out[1]) * mlp_rows
    ) + blend(stream_rows, jnp.sum(both_mix, axis=1))
    final_local, last_shares = lax.optimization_barrier((final_local, last_shares))
    final_full = jnp.concatenate(list(shift_gather(final_local)), axis=1)
    final_norm = layer_norm(final_full)
    own_columns = lax.dynamic_slice_in_dim(
        final_norm, lax.axis_index("head") * feature_local, feature_local, 1
    )
    branch = jnp.einsum(
        "jd,kde->jke",
        final_norm.astype(jnp.bfloat16),
        draft_weight,
        preferred_element_type=jnp.float32,
    )
    drafted = (own_columns[:, None, :] + jax.nn.silu(branch)).astype(jnp.bfloat16)
    draft_full = jnp.concatenate(list(shift_gather(drafted)), axis=2)
    draft_all = gather_small(draft_full)
    logits_local = jnp.dot(
        draft_all.reshape(-1, width), lm_head, preferred_element_type=jnp.float32
    )
    logits_local = logits_local.reshape(all_requests, draft_count, -1)
    logits_local, mlp_parts[-1] = lax.optimization_barrier((logits_local, mlp_parts[-1]))
    logits = lax.all_to_all(
        logits_local.astype(jnp.bfloat16), ("req", "head"), split_axis=0, concat_axis=2, tiled=True
    ).astype(logits_local.dtype)
    attn_delta = jnp.concatenate(attn_parts)
    mlp_delta = jnp.concatenate(mlp_parts)
    stream_vals = streams.astype(jnp.float32)
    new_streams = both_out[None, :, None] * attn_delta[:, None] + (
        hc_out[1][None, :, None] * mlp_delta[:, None]
    )
    for index in range(stream_count):
        new_streams = (
            new_streams + both_mix[index][None, :, None] * stream_vals[:, index : index + 1]
        )
    new_streams = new_streams.astype(jnp.bfloat16)

    return (new_streams, logits)


def merge_flat(ours, got, heads, size):
    lead = ours[0].shape[:2]
    pairs = [
        tuple(value.reshape((-1,) + value.shape[2:]) for value in pair) for pair in (ours, got)
    ]
    merged = merge_partials(pairs, heads, size)
    return [value.reshape(lead + value.shape[1:]) for value in merged]


def solution(mesh):
    in_specs = (
        P("req", None, "head"),
        P(),
        P(),
        P(),
        P(None, None, "head"),
        P("head", None),
        P(None, None, "head"),
        P("head", None),
        P(None, None, "head"),
        P(None, ("req", "head")),
        P("req", None, "head", None),
        P("req", None, "head", None),
        P("req"),
        P("req"),
        P("req"),
        P("req", None),
        P("req"),
    )
    out_specs = (P("req", None, "head"), P(("req", "head"), None, None))
    return jax.shard_map(
        on_device, mesh=mesh, in_specs=in_specs, out_specs=out_specs, check_vma=False
    )
```

```python
import functools
import math

import jax
import jax.numpy as jnp
from jax import lax
from jax.experimental import pallas as pl
from jax.experimental.pallas import tpu as pltpu
from jax.sharding import PartitionSpec as P

NEG_FILL = -1e30
EMPTY = -1e29
PRECISE = lax.Precision.HIGHEST
CHUNKS = 2
LANES = 128
PAGES_A_STEP = 2
MIB = 1024 * 1024


def params(mebibytes):
    return pltpu.CompilerParams(
        dimension_semantics=("arbitrary",), vmem_limit_bytes=mebibytes * MIB
    )


def ancestors(parents):
    length = parents.shape[1]
    places = jnp.arange(length, dtype=jnp.int32)
    linked = (parents[:, :, None] == places[None, None, :]) | (places[:, None] == places[None, :])[
        None
    ]
    reach = linked.astype(jnp.float32)
    for repeat in range(max(1, (length - 1).bit_length())):
        reach = jnp.minimum(jnp.einsum("jik,jkl->jil", reach, reach, precision=PRECISE), 1.0)
    return reach


def layer_norm(values):
    center = jnp.mean(values, axis=-1, keepdims=True)
    square = jnp.mean(values * values, axis=-1, keepdims=True)
    return (values - center) * lax.rsqrt(square - center * center + 1e-05)


def blend(stream_vals, weights):
    total = weights[0] * stream_vals[:, 0]
    for index in range(1, stream_vals.shape[1]):
        total = total + weights[index] * stream_vals[:, index]
    return total


def shift_gather(small):
    count = lax.axis_size("head")
    rank = lax.axis_index("head")
    parts = [small] + [
        lax.ppermute(small, "head", [(z, (z + step) % count) for z in range(count)])
        for step in range(1, count)
    ]
    stacked = jnp.stack(parts)
    return jnp.stack(
        [
            lax.dynamic_index_in_dim(stacked, (rank - source) % count, 0, keepdims=False)
            for source in range(count)
        ]
    )


def shift_scatter(shares):
    count = lax.axis_size("head")
    rank = lax.axis_index("head")
    width = shares.shape[1] // count
    total = None
    for step in range(count):
        block = lax.dynamic_slice_in_dim(shares, (rank + step) % count * width, width, 1)
        if step:
            block = lax.ppermute(block, "head", [(z, (z + step) % count) for z in range(count)])
        block = block.astype(jnp.float32)
        total = block if total is None else total + block
    return total


def gathered_norm(values, width, after=None):
    local = values.shape[1]
    sums = jnp.sum(values, axis=1)
    squares = jnp.sum(values * values, axis=1)
    center = sums / local
    sent = (values - center[:, None]).astype(jnp.bfloat16)
    stats = shift_gather(jnp.stack([sums, squares]))
    if after is not None:
        sent, after = lax.optimization_barrier((sent, after))
    gathered = lax.all_gather(sent, "head", axis=1, tiled=True)
    mean = jnp.sum(stats[:, 0], axis=0) / width
    variance = jnp.sum(stats[:, 1], axis=0) / width - mean * mean
    scale = lax.rsqrt(variance + 1e-05)

    def finish(gathered):
        normed = [
            (
                (
                    gathered[:, rank * local : (rank + 1) * local].astype(jnp.float32)
                    + (stats[rank, 0] / local - mean)[:, None]
                )
                * scale[:, None]
            ).astype(jnp.bfloat16)
            for rank in range(lax.axis_size("head"))
        ]
        return jnp.concatenate(normed, axis=1)

    return gathered, finish, sent


def scatter_columns(shares):
    return lax.psum_scatter(shares, "head", scatter_dimension=1, tiled=True).astype(jnp.float32)


def swapped(values, bit):
    count = lax.axis_size("req")
    return lax.ppermute(values, "req", [(r, r ^ bit) for r in range(count)])


def bit_orders():
    bits = [1 << index for index in range((lax.axis_size("req") - 1).bit_length())]
    return bits[0], (bits[1:], bits[1:][::-1])


def gather_requests(values):
    half = values.shape[0] // 2
    near, orders = bit_orders()
    parts = []
    for part, order in enumerate(orders):
        blocks = {0: values[part * half : (part + 1) * half]}
        for bit in order:
            for index in list(blocks):
                blocks[index ^ bit] = swapped(blocks[index], bit)
        parts.append(blocks)
    even = jnp.concatenate([blocks[index] for index in sorted(parts[0]) for blocks in parts])
    return even, swapped(even, near)


def gather_small(values):
    count = lax.axis_size("req")
    near, orders = bit_orders()
    stacked = values[None]
    bits = []
    for bit in list(orders[0]) + [near]:
        stacked = jnp.concatenate([stacked, swapped(stacked, bit)])
        bits.append(bit)
    index = lax.axis_index("req") ^ jnp.arange(count, dtype=jnp.int32)
    place = jnp.zeros_like(index)
    for spot, bit in enumerate(bits):
        place = place + jnp.where((index & bit) != 0, 1 << spot, 0)
    return stacked[place]


def scatter_requests(sums, logs, merge):
    near, orders = bit_orders()
    count = lax.axis_size("req")
    far = count // 2
    state = []
    mine = [sums[:far], logs[:far]]
    theirs = [swapped(sums[far:], near), swapped(logs[far:], near)]
    merged = merge(mine, theirs)
    half = sums.shape[1] // 2
    done = []
    for part, order in enumerate(orders):
        kept = [value[:, part * half : (part + 1) * half] for value in merged]
        places = list(range(far))
        for place, bit in enumerate(order):
            stay = [at for at, index in enumerate(places) if not index & (bit >> 1)]
            leave = [at for at, index in enumerate(places) if index & (bit >> 1)]
            pick = lambda value, which: jnp.concatenate([value[at : at + 1] for at in which])
            ours = [pick(value, stay) for value in kept]
            got = [swapped(pick(value, leave), bit) for value in kept]
            places = [places[at] for at in stay]
            kept = merge(ours, got) if place < len(order) - 1 else (ours, got)
        done.append(kept)
    return done


def rotate_kernel(heads, size, scale, x_ref, y_ref, z_ref, cos_ref, sin_ref, q_ref, k_ref, v_ref):
    cosine, sine = cos_ref[...], sin_ref[...]
    for head in range(heads):
        at = slice(head * size, (head + 1) * size)
        for in_ref, out_ref, factor in ((x_ref, q_ref, scale), (y_ref, k_ref, 1.0)):
            values = in_ref[:, at]
            turned = values * cosine + pltpu.roll(values, size // 2, 1) * sine
            out_ref[:, at] = (turned * factor).astype(out_ref.dtype)
    v_ref[...] = z_ref[...].astype(v_ref.dtype)


def rotate_all(thirds, cosine, sine, heads, size, rows):
    tokens, width = thirds[0].shape
    out = jax.ShapeDtypeStruct((tokens, width), jnp.bfloat16)
    block = lambda lanes: pl.BlockSpec((rows, lanes), lambda i: (i, 0))
    return pl.pallas_call(
        functools.partial(rotate_kernel, heads, size, size ** (-0.5)),
        grid=(tokens // rows,),
        in_specs=[block(width)] * 3 + [block(size)] * 2,
        out_specs=[block(width)] * 3,
        out_shape=[out] * 3,
        compiler_params=params(8),
        name="rotate",
    )(*thirds, cosine, sine)


def lay_logs(columns, rows):
    lane = lax.broadcasted_iota(jnp.int32, (LANES, LANES), 1)
    table = jnp.full((LANES, LANES), NEG_FILL, jnp.float32)
    for head, column in enumerate(columns):
        tall = jnp.concatenate(
            [column, jnp.full((LANES - rows, 1), NEG_FILL, jnp.float32)], axis=0
        )
        table = jnp.where(lane == head, tall, table)
    return jnp.transpose(table)[:8]


def tree_kernel(heads, size, q_ref, k_ref, v_ref, reach_ref, out_ref, log_ref):
    seen = reach_ref[0] > 0
    logs = []
    for head in range(heads):
        at = slice(head * size, (head + 1) * size)
        scores = lax.dot_general(
            q_ref[0, :, at],
            k_ref[0, :, at],
            (((1,), (1,)), ((), ())),
            preferred_element_type=jnp.float32,
        )
        scores = jnp.where(seen, scores, NEG_FILL)
        top = jnp.max(scores, axis=1, keepdims=True)
        weights = jnp.where(seen, jnp.exp(scores - top), 0.0)
        total = jnp.sum(weights, axis=1, keepdims=True)
        summed = jnp.dot(
            weights.astype(jnp.bfloat16), v_ref[0, :, at], preferred_element_type=jnp.float32
        )
        out_ref[0, :, at] = summed / total
        logs.append(top + jnp.log(total))
    log_ref[0] = lay_logs(logs, q_ref.shape[1])


def tree_attention(queries, keys, values, reach, heads, size):
    requests, tree, width = queries.shape
    block = pl.BlockSpec((1, tree, width), lambda j: (j, 0, 0))
    return pl.pallas_call(
        functools.partial(tree_kernel, heads, size),
        grid=(requests,),
        in_specs=[block] * 3 + [pl.BlockSpec((1, tree, tree), lambda j: (j, 0, 0))],
        out_specs=[block, pl.BlockSpec((1, 8, LANES), lambda j: (j, 0, 0))],
        out_shape=[
            jax.ShapeDtypeStruct((requests, tree, width), jnp.float32),
            jax.ShapeDtypeStruct((requests, 8, LANES), jnp.float32),
        ],
        compiler_params=params(8),
        name="tree_attention",
    )(queries, keys, values, reach)


def page_kernel(
    heads,
    size,
    page_ref,
    place_ref,
    fill_ref,
    first_ref,
    last_ref,
    live_ref,
    even_ref,
    odd_ref,
    *refs,
):
    leaves = refs[: 2 * PAGES_A_STEP]
    out_ref, log_ref, acc_ref, top_ref, total_ref = refs[2 * PAGES_A_STEP :]
    step = pl.program_id(0)
    half, tree = even_ref.shape[:2]
    spans = [slice(head * size, (head + 1) * size) for head in range(heads)]
    entries = leaves[0].shape[2]

    @pl.when(step == 0)
    def _():
        log_ref[...] = jnp.full(log_ref.shape, NEG_FILL, jnp.float32)

    @pl.when(step * PAGES_A_STEP < live_ref[0])
    def _():
        column = lax.broadcasted_iota(jnp.int32, (tree, entries), 1)
        units = [(part, head) for part in range(PAGES_A_STEP) for head in range(heads)]
        asked, valid = [], []
        for part in range(PAGES_A_STEP):
            visit = step * PAGES_A_STEP + part
            place = place_ref[visit]
            asked.append(
                jnp.where(
                    place < half,
                    even_ref[jnp.minimum(place, half - 1)],
                    odd_ref[jnp.maximum(place - half, 0)],
                )
            )
            valid.append(column < fill_ref[visit])
        scores = [
            lax.dot_general(
                asked[part][:, spans[head]],
                leaves[2 * part][0, head],
                (((1,), (1,)), ((), ())),
                preferred_element_type=jnp.float32,
            )
            for part, head in units
        ]
        scores = [
            jnp.where(valid[part], score, NEG_FILL) for (part, head), score in zip(units, scores)
        ]
        tops = [jnp.max(score, axis=1, keepdims=True) for score in scores]
        weights = [
            jnp.where(valid[part], jnp.exp(score - top), 0.0)
            for (part, head), score, top in zip(units, scores, tops)
        ]
        totals = [jnp.sum(weight, axis=1, keepdims=True) for weight in weights]
        sums = [
            jnp.dot(
                weight.astype(jnp.bfloat16),
                leaves[2 * part + 1][0, head],
                preferred_element_type=jnp.float32,
            )
            for (part, head), weight in zip(units, weights)
        ]
        for part in range(PAGES_A_STEP):
            visit = step * PAGES_A_STEP + part
            merge_page(
                visit,
                spans,
                tops[part * heads : (part + 1) * heads],
                totals[part * heads : (part + 1) * heads],
                sums[part * heads : (part + 1) * heads],
                place_ref,
                first_ref,
                last_ref,
                live_ref,
                out_ref,
                log_ref,
                acc_ref,
                top_ref,
                total_ref,
            )


def merge_page(
    visit,
    spans,
    tops,
    totals,
    sums,
    place_ref,
    first_ref,
    last_ref,
    live_ref,
    out_ref,
    log_ref,
    acc_ref,
    top_ref,
    total_ref,
):
    tree = acc_ref.shape[0]
    live = visit < live_ref[0]
    alone = (first_ref[visit] == 1) & (last_ref[visit] == 1)

    def write(tops, totals, sums):
        logs = []
        for span, top, total, value in zip(spans, tops, totals, sums):
            some = total > 0
            safe = jnp.where(some, total, 1.0)
            out_ref[place_ref[visit], :, span] = (value / safe).astype(out_ref.dtype)
            logs.append(jnp.where(some, top + jnp.log(safe), NEG_FILL)[:, :1])
        log_ref[place_ref[visit]] = lay_logs(logs, tree)

    @pl.when(live & alone)
    def _():
        write(tops, totals, sums)

    @pl.when(live & jnp.logical_not(alone))
    def _():
        @pl.when(first_ref[visit] == 1)
        def _():
            acc_ref[...] = jnp.zeros(acc_ref.shape, jnp.float32)
            top_ref[...] = jnp.full(top_ref.shape, NEG_FILL, jnp.float32)
            total_ref[...] = jnp.zeros(total_ref.shape, jnp.float32)

        for head, span in enumerate(spans):
            before = top_ref[head]
            top = jnp.maximum(before, tops[head])
            decay, gain = jnp.exp(before - top), jnp.exp(tops[head] - top)
            top_ref[head] = top
            total_ref[head] = total_ref[head] * decay + totals[head] * gain
            acc_ref[:, span] = acc_ref[:, span] * decay + sums[head] * gain

        @pl.when(last_ref[visit] == 1)
        def _():
            heads = range(len(spans))
            write(
                [top_ref[head] for head in heads],
                [total_ref[head] for head in heads],
                [acc_ref[:, span] for span in spans],
            )


def page_attention(even, odd, k_pages, v_pages, plan, heads, size):
    half, tree, width = even.shape
    requests = 2 * half
    slots, entries = k_pages.shape[0], k_pages.shape[2]
    whole = lambda shape: pl.BlockSpec(shape, lambda p, *rest: (0, 0, 0))

    def leaf(part):
        return pl.BlockSpec(
            (1, heads, entries, size),
            lambda p, page, *rest: (page[p * PAGES_A_STEP + part], 0, 0, 0),
        )

    grid_spec = pltpu.PrefetchScalarGridSpec(
        num_scalar_prefetch=6,
        grid=(slots // PAGES_A_STEP,),
        in_specs=[whole(even.shape), whole(odd.shape)]
        + [leaf(part) for part in range(PAGES_A_STEP) for _ in range(2)],
        out_specs=[whole((requests, tree, width)), whole((requests, 8, LANES))],
        scratch_shapes=[
            pltpu.VMEM((tree, width), jnp.float32),
            pltpu.VMEM((heads, tree, size), jnp.float32),
            pltpu.VMEM((heads, tree, size), jnp.float32),
        ],
    )
    return pl.pallas_call(
        functools.partial(page_kernel, heads, size),
        grid_spec=grid_spec,
        out_shape=[
            jax.ShapeDtypeStruct((requests, tree, width), jnp.bfloat16),
            jax.ShapeDtypeStruct((requests, 8, LANES), jnp.float32),
        ],
        compiler_params=params(20),
        name="page_attention",
    )(*plan, even, odd, *([k_pages, v_pages] * PAGES_A_STEP))


def project_kernel(x_ref, w_ref, out_ref):
    out_ref[...] = jnp.dot(x_ref[...], w_ref[...], preferred_element_type=jnp.float32).astype(
        out_ref.dtype
    )


def project(values, weight):
    rows, depth = values.shape
    columns = weight.shape[1]
    tile = min(columns, 512)
    return pl.pallas_call(
        project_kernel,
        grid=(columns // tile,),
        in_specs=[
            pl.BlockSpec((rows, depth), lambda i: (0, 0)),
            pl.BlockSpec((depth, tile), lambda i: (0, i)),
        ],
        out_specs=pl.BlockSpec((rows, tile), lambda i: (0, i)),
        out_shape=jax.ShapeDtypeStruct((rows, columns), jnp.bfloat16),
        compiler_params=params(8),
        name="project",
    )(values, weight)


def mlp_kernel(steps, tile, x_ref, gate_ref, up_ref, down_ref, out_ref, hidden_ref):
    step = pl.program_id(0)

    @pl.when(step < steps)
    def _():
        gate = jnp.dot(x_ref[...], gate_ref[...], preferred_element_type=jnp.float32)
        up = jnp.dot(x_ref[...], up_ref[...], preferred_element_type=jnp.float32)
        at = pl.ds(pl.multiple_of(step * tile, tile), tile)
        hidden_ref[:, at] = (jax.nn.silu(gate) * up).astype(hidden_ref.dtype)

    @pl.when(step >= steps)
    def _():
        out_ref[...] = jnp.dot(
            hidden_ref[...], down_ref[...], preferred_element_type=jnp.float32
        ).astype(out_ref.dtype)


def mlp(values, gate_up, down):
    rows, width = values.shape
    hidden, columns = down.shape
    tile = min(hidden, 256)
    steps = hidden // tile
    out_tile = min(columns, 256)
    late = lambda i: jnp.maximum(i - steps, 0)
    early = lambda i: jnp.minimum(i, steps - 1)
    return pl.pallas_call(
        functools.partial(mlp_kernel, steps, tile),
        grid=(steps + columns // out_tile,),
        in_specs=[
            pl.BlockSpec((rows, width), lambda i: (0, 0)),
            pl.BlockSpec((width, tile), lambda i: (0, early(i))),
            pl.BlockSpec((width, tile), lambda i: (0, steps + early(i))),
            pl.BlockSpec((hidden, out_tile), lambda i: (0, late(i))),
        ],
        out_specs=pl.BlockSpec((rows, out_tile), lambda i: (0, late(i))),
        out_shape=jax.ShapeDtypeStruct((rows, columns), jnp.bfloat16),
        scratch_shapes=[pltpu.VMEM((rows, hidden), jnp.bfloat16)],
        compiler_params=params(40),
        name="mlp",
    )(values, gate_up, gate_up, down)


def merge_kernel(heads, size, count, *refs):
    sums, logs, out_ref = refs[:count], refs[count : 2 * count], refs[2 * count]
    log_ref = refs[2 * count + 1] if len(refs) > 2 * count + 1 else None
    tree = out_ref.shape[1]
    for request in range(out_ref.shape[0]):
        tables = [ref[request] for ref in logs]
        top = functools.reduce(jnp.maximum, tables)
        total = functools.reduce(lambda a, b: a + b, [jnp.exp(table - top) for table in tables])
        merged = top + jnp.log(total)
        if log_ref is not None:
            log_ref[request] = merged
        shares = [
            jnp.transpose(jnp.where(table > EMPTY, jnp.exp(table - merged), 0.0))
            for table in tables
        ]
        for head in range(heads):
            at = slice(head * size, (head + 1) * size)
            value = jnp.zeros((tree, size), jnp.float32)
            for ref, share in zip(sums, shares):
                factor = share[:tree, head : head + 1]
                term = ref[request, :, at].astype(jnp.float32)
                value = value + jnp.where(factor > 0, term * factor, 0.0)
            out_ref[request, :, at] = value.astype(out_ref.dtype)


def merge_partials(pairs, heads, size, with_logs=True):
    requests, tree, width = pairs[0][0].shape
    group = max(size for size in (1, 2, 4, 8) if requests % size == 0)
    big = pl.BlockSpec((group, tree, width), lambda j: (j, 0, 0))
    small = pl.BlockSpec((group, 8, LANES), lambda j: (j, 0, 0))
    out_specs = [big, small] if with_logs else [big]
    out_shape = [
        jax.ShapeDtypeStruct((requests, tree, width), jnp.bfloat16),
        jax.ShapeDtypeStruct((requests, 8, LANES), jnp.float32),
    ][: len(out_specs)]
    return pl.pallas_call(
        functools.partial(merge_kernel, heads, size, len(pairs)),
        grid=(requests // group,),
        in_specs=[big] * len(pairs) + [small] * len(pairs),
        out_specs=out_specs,
        out_shape=out_shape,
        compiler_params=params(10),
        name="merge_partials",
    )(*[pair[0] for pair in pairs], *[pair[1] for pair in pairs])


def page_plan(owner, fill, first_request, requests, all_local, count):
    slots = owner.shape[0]
    me = lax.axis_index("req")
    source = owner // all_local
    local = owner % all_local - first_request
    mine = (owner >= 0) & (local >= 0) & (local < requests)
    index = source ^ me
    index = (index & 1) * (count // 2) + (index >> 1)
    place = jnp.where(mine, index * requests + local, count * requests)
    spot = jnp.arange(slots, dtype=jnp.int32)
    ahead = (place[None, :] < place[:, None]) | (
        (place[None, :] == place[:, None]) & (spot[None, :] < spot[:, None])
    )
    rank = jnp.sum(ahead.astype(jnp.int32), axis=1)
    live = jnp.sum(mine.astype(jnp.int32))
    wanted = jnp.minimum(spot, jnp.maximum(live - 1, 0))
    chosen = rank[None, :] == wanted[:, None]
    take = lambda values: jnp.sum(jnp.where(chosen, values[None, :], 0), axis=1)
    pages, places, fills = take(spot), take(jnp.where(mine, place, 0)), take(fill)
    changed = (places[1:] != places[:-1]).astype(jnp.int32)
    one = jnp.ones((1,), jnp.int32)
    first = jnp.concatenate([one, changed])
    last = jnp.concatenate([changed, one])
    last = jnp.where(spot == live - 1, 1, last)
    return (pages, places, fills, first, last, live[None])


def on_device(
    streams,
    hc_in,
    hc_mix,
    hc_out,
    qkv_weight,
    out_weight,
    up_gate,
    down_weight,
    draft_weight,
    lm_head,
    k_pages,
    v_pages,
    page_owner,
    page_fill,
    cache_len,
    tree_parent,
    accepted_index,
):
    tokens_local = streams.shape[0]
    stream_count = streams.shape[1]
    feature_local = streams.shape[2]
    width = qkv_weight.shape[0]
    req_local = cache_len.shape[0]
    tree_size = tree_parent.shape[1]
    heads = k_pages.shape[2]
    size = k_pages.shape[3]
    draft_count = draft_weight.shape[0]
    parts = lax.axis_size("req")
    all_requests = req_local * parts

    identity = jnp.eye(stream_count, dtype=jnp.float32)
    first_mix, second_mix = identity + hc_mix[0], identity + hc_mix[1]
    mid_in = jnp.sum(first_mix * hc_in[1][None, :], axis=1)
    mid_out = jnp.sum(hc_out[0] * hc_in[1])
    both_mix = jnp.sum(first_mix[:, :, None] * second_mix[None, :, :], axis=1)
    both_out = jnp.sum(hc_out[0][:, None] * second_mix, axis=0)

    reach = ancestors(tree_parent)
    depth = (jnp.sum(reach, axis=2) - 1.0).astype(jnp.int32)
    positions = (cache_len[:, None] + depth).reshape(tokens_local)
    half = size // 2
    freqs = jnp.exp(jnp.arange(half, dtype=jnp.float32) * (-2.0 * math.log(10000.0) / size))
    angles = positions.astype(jnp.float32)[:, None] * freqs[None, :]
    cosine, sine = jnp.cos(angles), jnp.sin(angles)
    cosine = jnp.concatenate([cosine, cosine], axis=1)
    sine = jnp.concatenate([-sine, sine], axis=1)

    k_heads = jnp.transpose(k_pages, (0, 2, 1, 3))
    v_heads = jnp.transpose(v_pages, (0, 2, 1, 3))

    step_requests = req_local // CHUNKS
    step_tokens = step_requests * tree_size
    merge = lambda ours, got: merge_flat(ours, got, heads, size)

    gate_up = up_gate.reshape(width, -1)
    token = None
    first_shares = None
    attended_in = []
    for chunk in range(CHUNKS):
        rows = slice(chunk * step_tokens, (chunk + 1) * step_tokens)
        stream_vals = streams[rows].astype(jnp.float32)
        mixed_in = blend(stream_vals, hc_in[0])
        token, finish, sent = gathered_norm(mixed_in, width, token)
        attended_in.append((token, finish))

    all_shape = (step_requests, tree_size, heads * size)
    attn_parts, mlp_parts = [], []
    for chunk in range(CHUNKS):
        rows = slice(chunk * step_tokens, (chunk + 1) * step_tokens)
        asked = slice(chunk * step_requests, (chunk + 1) * step_requests)
        gathered, finish = attended_in[chunk]
        if chunk == 0:
            normed, k_heads, v_heads, gate_up = lax.optimization_barrier(
                (finish(gathered), k_heads, v_heads, gate_up)
            )
        else:
            normed = finish(gathered)
        thirds = [
            jnp.dot(normed, qkv_weight[:, third], preferred_element_type=jnp.float32)
            for third in range(3)
        ]
        queries, keys, values = rotate_all(
            thirds, cosine[rows], sine[rows], heads, size, 2 * tree_size
        )
        queries, keys, values = (item.reshape(all_shape) for item in (queries, keys, values))
        even, odd = gather_requests(queries)
        plan = page_plan(
            page_owner, page_fill, chunk * step_requests, step_requests, req_local, parts
        )
        sums, logs = page_attention(even, odd, k_heads, v_heads, plan, heads, size)
        keys, sums, logs = lax.optimization_barrier((keys, sums, logs))
        tree_pair = tree_attention(queries, keys, values, reach[asked], heads, size)
        done = scatter_requests(
            sums.reshape((parts,) + all_shape),
            logs.reshape(parts, step_requests, 8, LANES),
            merge,
        )
        part_requests = step_requests // 2
        attended = []
        for part, (ours, got) in enumerate(done):
            own = slice(part * part_requests, (part + 1) * part_requests)
            pairs = [
                tuple(value.reshape((-1,) + value.shape[2:]) for value in pair)
                for pair in (ours, got)
            ] + [(tree_pair[0][own], tree_pair[1][own])]
            attended.append(merge_partials(pairs, heads, size, with_logs=False)[0])
        attended = jnp.concatenate(attended).reshape(step_tokens, heads * size)
        if chunk + 1 < CHUNKS:
            later, later_finish = attended_in[chunk + 1]
            attended, later = lax.optimization_barrier((attended, later))
            attended_in[chunk + 1] = (later, later_finish)
        attn_delta = scatter_columns(project(attended, out_weight))
        if first_shares is not None:
            attn_delta, first_shares = lax.optimization_barrier((attn_delta, first_shares))
        attn_parts.append(attn_delta)

        stream_vals = streams[rows].astype(jnp.float32)
        mixed_mid = blend(stream_vals, mid_in) + mid_out * attn_delta
        gathered, finish, sent_mid = gathered_norm(mixed_mid, width)
        if chunk == CHUNKS - 1:
            rows_taken = jnp.arange(req_local, dtype=jnp.int32) * tree_size + accepted_index
            stream_rows = streams[rows_taken].astype(jnp.float32)
            is_taken = jnp.arange(tree_size, dtype=jnp.int32)[None, :] == accepted_index[:, None]
            attn_rows = jnp.concatenate(
                [
                    jnp.sum(
                        jnp.where(
                            is_taken[piece * step_requests : (piece + 1) * step_requests, :, None],
                            part.reshape(step_requests, tree_size, feature_local),
                            0.0,
                        ),
                        axis=1,
                    )
                    for piece, part in enumerate(attn_parts)
                ]
            )
            mid_rows = blend(stream_rows, mid_in) + mid_out * attn_rows
            mid_full = jnp.concatenate(list(shift_gather(mid_rows)), axis=1)
            row_shares = mlp(layer_norm(mid_full).astype(jnp.bfloat16), gate_up, down_weight)
            gathered, row_shares = lax.optimization_barrier((gathered, row_shares))
        normed_mid = finish(gathered)
        shares = mlp(normed_mid, gate_up, down_weight)
        if first_shares is None:
            first_shares = shares
        else:
            first_shares, sent_mid = lax.optimization_barrier((first_shares, sent_mid))
            mlp_parts.append(scatter_columns(first_shares))
            last_shares = shares
            mlp_parts.append(scatter_columns(shares))

    mlp_rows = shift_scatter(row_shares)
    final_local = (
        jnp.sum(both_out) * attn_rows + jnp.sum(hc_out[1]) * mlp_rows
    ) + blend(stream_rows, jnp.sum(both_mix, axis=1))
    final_local, last_shares = lax.optimization_barrier((final_local, last_shares))
    final_full = jnp.concatenate(list(shift_gather(final_local)), axis=1)
    final_norm = layer_norm(final_full)
    own_columns = lax.dynamic_slice_in_dim(
        final_norm, lax.axis_index("head") * feature_local, feature_local, 1
    )
    branch = jnp.einsum(
        "jd,kde->jke",
        final_norm.astype(jnp.bfloat16),
        draft_weight,
        preferred_element_type=jnp.float32,
    )
    drafted = (own_columns[:, None, :] + jax.nn.silu(branch)).astype(jnp.bfloat16)
    draft_full = jnp.concatenate(list(shift_gather(drafted)), axis=2)
    draft_all = gather_small(draft_full)
    logits_local = jnp.dot(
        draft_all.reshape(-1, width), lm_head, preferred_element_type=jnp.float32
    )
    logits_local = logits_local.reshape(all_requests, draft_count, -1)
    logits_local, mlp_parts[-1] = lax.optimization_barrier((logits_local, mlp_parts[-1]))
    logits = lax.all_to_all(
        logits_local.astype(jnp.bfloat16), ("req", "head"), split_axis=0, concat_axis=2, tiled=True
    ).astype(logits_local.dtype)
    attn_delta = jnp.concatenate(attn_parts)
    mlp_delta = jnp.concatenate(mlp_parts)
    stream_vals = streams.astype(jnp.float32)
    new_streams = both_out[None, :, None] * attn_delta[:, None] + (
        hc_out[1][None, :, None] * mlp_delta[:, None]
    )
    for index in range(stream_count):
        new_streams = (
            new_streams + both_mix[index][None, :, None] * stream_vals[:, index : index + 1]
        )
    new_streams = new_streams.astype(jnp.bfloat16)

    return (new_streams, logits)


def merge_flat(ours, got, heads, size):
    lead = ours[0].shape[:2]
    pairs = [
        tuple(value.reshape((-1,) + value.shape[2:]) for value in pair) for pair in (ours, got)
    ]
    merged = merge_partials(pairs, heads, size)
    return [value.reshape(lead + value.shape[1:]) for value in merged]


def solution(mesh):
    in_specs = (
        P("req", None, "head"),
        P(),
        P(),
        P(),
        P(None, None, "head"),
        P("head", None),
        P(None, None, "head"),
        P("head", None),
        P(None, None, "head"),
        P(None, ("req", "head")),
        P("req", None, "head", None),
        P("req", None, "head", None),
        P("req"),
        P("req"),
        P("req"),
        P("req", None),
        P("req"),
    )
    out_specs = (P("req", None, "head"), P(("req", "head"), None, None))
    return jax.shard_map(
        on_device, mesh=mesh, in_specs=in_specs, out_specs=out_specs, check_vma=False
    )
```
